128 devices in a mesh: ctx: 32 (over z, x_hi, y), chan: 4 (over x_lo, core).
Axes of the slice: x: 4 (x_hi: 2, x_lo: 2; x = x_hi * 2 + x_lo), y: 4, z: 4, core: 2. Of those that a mesh axis runs over, the one named last changes fastest.
Arguments:
- token_ids: int32 [24576], P('ctx'), may hold values from 0 to 511
- embed_table: bfloat16 [512, 4096], P(None, 'chan'), may hold values from -6 to 6
- norm_gain: float32 [4096], replicated, may hold values from 0.1 to 1.9
- in_weight: bfloat16 [4096, 3, 2048], P('ctx', None, 'chan'), may hold values from -0.09375 to 0.09375
- short_filter: float32 [3, 3, 2048], P(None, None, 'chan'), may hold values from -3 to 3
- residue: float32 [16, 2048], P(None, 'chan'), may hold values from -1.5 to 1.5
- decay_rate: float32 [16, 2048], P(None, 'chan'), may hold values from 2.0345053e-05 to 0.033
- skip_bias: float32 [2048], P('chan'), may hold values from -4 to 4
Outputs:
- gated_output: bfloat16 [24576, 2048], P('ctx', 'chan')
The draws below stay inside these ranges and needn't reach their ends.
All inputs are finite; a program needn't handle non-finite values.
Results may differ from the reference program's by a relative error of at most 0.014.
Values may be sent and summed in bfloat16 or wider, within the bound.
A program may use at most 128 MiB of HBM per device.

```python
import math
import jax
import jax.numpy as jnp
from jax import lax

D = 4096
VOCAB = 512
CH = 2048
MODES = 16
SHORT = 3
LENGTH = 24576


def place_ends(drawn, rng, smallest, largest):
    dims = drawn.shape
    place = [jax.random.randint(jax.random.fold_in(rng, axis), (), 0, dims[axis]) for axis in range(len(dims))]
    drawn = drawn.at[tuple(place)].set(smallest)
    longest = dims.index(max(dims))
    place[longest] = (place[longest] + 1) % dims[longest]
    return drawn.at[tuple(place)].set(largest)


def level_of(rng, extent, shards, low, high):
    factor_of = 1.0
    for position, blocks in shards:
        steps = jax.random.uniform(jax.random.fold_in(jax.random.fold_in(rng, 6), position), (blocks,), jnp.float32, low / len(shards), high / len(shards))
        factor_of = factor_of * jnp.repeat(jnp.exp(steps), extent[position] // blocks).reshape((-1,) + (1,) * (len(extent) - 1 - position))
    return factor_of


def normal_values(rng, shape, scale, limit, split=(), held_as=jnp.bfloat16):
    gain = level_of(rng, shape, split, -0.22, 0.18) if split else 1.0
    entries = jax.random.normal(rng, shape, jnp.float32) * scale * gain
    return jnp.minimum(jnp.maximum(entries, -limit), limit).astype(held_as)


def setup_inputs(seed: int = 0) -> dict:
    key_list = jax.random.split(jax.random.key(seed), 9)
    return {
        "token_ids": place_ends(jax.random.randint(key_list[0], (LENGTH,), 0, VOCAB), jax.random.fold_in(key_list[0], 1), 0, VOCAB - 1).astype(jnp.int32),
        "embed_table": normal_values(key_list[1], (VOCAB, D), 1.0, 6.0, ((1, 4),)),
        "norm_gain": jnp.clip(1.0 + 0.18 * jax.random.normal(key_list[2], (D,), jnp.float32), 0.1, 1.9),
        "in_weight": normal_values(key_list[3], (D, 3, CH), D ** -0.5, 0.09375, ((0, 32), (2, 4))),
        "short_filter": normal_values(key_list[4], (SHORT, 3, CH), 0.6, 3.0, ((2, 4),), jnp.float32),
        "residue": normal_values(key_list[5], (MODES, CH), 0.25, 1.5, ((1, 4),), jnp.float32),
        "decay_rate": jnp.clip(jnp.exp(math.log(0.033) - 7.391425 * jax.random.uniform(key_list[6], (MODES, CH), jnp.float32) ** level_of(key_list[6], (MODES, CH), ((1, 4),), -0.2, 0.2)), 2.0345052689663135e-05, 0.033),
        "skip_bias": normal_values(key_list[7], (CH,), 1.0, 4.0, ((0, 4),), jnp.float32),
    }


norm_epsilon = 1e-06

def block_convolve(operands):
    carried_block, residue_block, decay_block = operands
    positions = jnp.arange(LENGTH, dtype=jnp.float32)[:, None]
    filter_block = jnp.zeros_like(carried_block)
    for mode_index in range(MODES):
        weight_mode = residue_block[mode_index] * jnp.sqrt(decay_block[mode_index])
        filter_block = filter_block + weight_mode * jnp.exp(-decay_block[mode_index] * positions)
    points = 2 * LENGTH
    spectrum = jnp.fft.rfft(carried_block, n=points, axis=0) * jnp.fft.rfft(filter_block, n=points, axis=0)
    return jnp.fft.irfft(spectrum, n=points, axis=0)[:LENGTH].astype(jnp.float32)

def reference(token_ids, embed_table, norm_gain, in_weight, short_filter, residue, decay_rate, skip_bias):
    embedded = jnp.take(embed_table, token_ids, axis=0)
    wide = embedded.astype(jnp.float32)
    mean_square = lax.optimization_barrier(jnp.mean(wide * wide, axis=-1, keepdims=True))
    normed = (wide * lax.rsqrt(mean_square + norm_epsilon) * norm_gain).astype(jnp.bfloat16)
    projected = jnp.dot(normed, in_weight.reshape(D, 3 * CH), preferred_element_type=jnp.float32)
    projected = projected.astype(jnp.bfloat16).reshape(LENGTH, 3, CH).astype(jnp.float32)
    padded = jnp.pad(projected, ((SHORT - 1, 0), (0, 0), (0, 0)))
    branches = jnp.zeros_like(projected)
    for offset in range(SHORT):
        begin = SHORT - 1 - offset
        branches = branches + short_filter[offset] * padded[begin:begin + LENGTH]
    query = branches[:, 0]
    carried = (branches[:, 1] * branches[:, 2]).astype(jnp.bfloat16)
    width_block = min(128, CH)
    blocks = CH // width_block
    carried_blocks = carried.astype(jnp.float32).reshape(LENGTH, blocks, width_block).transpose(1, 0, 2)
    residue_blocks = residue.reshape(MODES, blocks, width_block).transpose(1, 0, 2)
    decay_blocks = decay_rate.reshape(MODES, blocks, width_block).transpose(1, 0, 2)
    long_conv = lax.map(block_convolve, (carried_blocks, residue_blocks, decay_blocks))
    long_conv = long_conv.transpose(1, 0, 2).reshape(LENGTH, CH)
    gated_output = query * (long_conv + skip_bias * carried.astype(jnp.float32))
    return gated_output.astype(jnp.bfloat16)
```

```python
import functools

import jax
import jax.numpy as jnp
from jax import lax
from jax.experimental import pallas as pl
from jax.experimental.pallas import tpu as pltpu
from jax.sharding import PartitionSpec as P

MESH = pl.DeviceIdType.MESH
EPS = 1e-06
VMEM_LIMIT = 48 * 1024 * 1024

CTX, CHAN, PLANE = 32, 4, 8
OWN = 16
SEG = 256
SEGS = 96
PER = 3
MODES = 16
NT = (((1,), (1,)), ((), ()))
HIGHEST = lax.Precision.HIGHEST


def dot(a, b):
    return jnp.dot(a, b, preferred_element_type=jnp.float32)


def high_low(x):
    high = x.astype(jnp.bfloat16)
    return high, (x - high.astype(jnp.float32)).astype(jnp.bfloat16)


def send(src, dst, send_sem, recv_sem, i, c):
    return pltpu.make_async_remote_copy(
        src_ref=src, dst_ref=dst, send_sem=send_sem, recv_sem=recv_sem, device_id=(i, c), device_id_type=MESH
    )


def table_kernel(
    tok_ref, embed_ref, gain_ref, weight_ref, table_ref, tokens_ref,
    got_weight, got_square, part, part_send, part_got, scaled,
    w_send, w_recv, t_send, t_recv, s_send, s_recv, p_send, p_recv,
):
    i, c = lax.axis_index("ctx"), lax.axis_index("chan")
    plane, place = i // PLANE, i % PLANE

    barrier = pltpu.get_barrier_semaphore()

    @pl.loop(0, CTX)
    def _(j):
        row, col = c * PLANE + j % PLANE, j // PLANE

        @pl.when(jnp.logical_or(row != i, col != c))
        def _():
            pl.semaphore_signal(barrier, inc=1, device_id=(row, col), device_id_type=MESH)

    @pl.loop(1, CTX)
    def _(j):
        pl.semaphore_signal(barrier, inc=1, device_id=((i + j) % CTX, c), device_id_type=MESH)

    for d in range(1, CHAN):
        pl.semaphore_signal(barrier, inc=1, device_id=(i, (c + d) % CHAN), device_id_type=MESH)
    own = jnp.where(plane == c, 1, 0)
    pl.semaphore_wait(barrier, CTX - own + (CTX - 1) + (CHAN - 1))

    def weight_copy(j):
        to = (i + j) % CTX
        return send(
            weight_ref.at[:, pl.ds(to * OWN, OWN), :],
            got_weight.at[c, :, :, pl.ds(place * 128, 128)],
            w_send.at[j],
            w_recv.at[c * PLANE + place],
            to,
            plane,
        )

    def token_copy(j):
        return send(tok_ref, tokens_ref.at[i], t_send.at[j], t_recv.at[i], (i + j) % CTX, c)

    @pl.loop(1, CTX)
    def _(j):
        weight_copy(j).start()

    self_copy = pltpu.make_async_copy(
        weight_ref.at[:, pl.ds(i * OWN, OWN), :],
        got_weight.at[c, :, :, pl.ds(place * 128, 128)],
        w_recv.at[c * PLANE + place],
    )

    @pl.when(plane == c)
    def _():
        self_copy.start()

    @pl.when(plane != c)
    def _():
        weight_copy(0).start()

    own_tokens = pltpu.make_async_copy(tok_ref, tokens_ref.at[i], t_recv.at[i])
    own_tokens.start()

    @pl.loop(1, CTX)
    def _(j):
        token_copy(j).start()

    wide = embed_ref[...].astype(jnp.float32)
    square_high, square_low = high_low(wide * wide)
    ones = jnp.ones((8, square_high.shape[1]), jnp.bfloat16)
    squares = lax.dot_general(ones, square_high, NT, preferred_element_type=jnp.float32)
    squares = squares + lax.dot_general(ones, square_low, NT, preferred_element_type=jnp.float32)
    got_square[c] = squares
    scaled[...] = (wide * gain_ref[c]).astype(jnp.bfloat16)

    def square_copy(d):
        return send(got_square.at[c], got_square.at[c], s_send.at[d], s_recv.at[c], i, (c + d) % CHAN)

    for d in range(1, CHAN):
        square_copy(d).start()

    @pl.loop(0, CTX)
    def _(s):
        pltpu.make_async_copy(
            weight_ref.at[:, pl.ds(0, OWN), :],
            got_weight.at[s // PLANE, :, :, pl.ds((s % PLANE) * 128, 128)],
            w_recv.at[s],
        ).wait()

    def part_copy(d):
        to = (c + d) % CHAN
        return send(part_send.at[to], part_got.at[c], p_send.at[d], p_recv.at[c], i, to)

    for q in range(CHAN):
        weights = got_weight[q].reshape(3 * OWN, got_weight.shape[3])
        product = lax.dot_general(weights, scaled[...], NT, preferred_element_type=jnp.float32)
        part[q] = product
        part_send[q] = product.astype(jnp.bfloat16)
    for d in range(1, CHAN):
        part_copy(d).start()
    total = part[c]
    mean = got_square[c]
    for d in range(1, CHAN):
        source = (c + d) % CHAN
        send(got_square.at[c], got_square.at[source], s_send.at[d], s_recv.at[source], i, source).wait_recv()
        mean = mean + got_square[source]
    scale = lax.rsqrt(mean[0:1] * (1.0 / (CHAN * embed_ref.shape[1])) + EPS)
    for d in range(1, CHAN):
        source = (c + d) % CHAN
        send(part_send.at[0], part_got.at[source], p_send.at[d], p_recv.at[source], i, source).wait_recv()
        total = total + part_got[source].astype(jnp.float32)
    table_ref[...] = (total * scale).astype(jnp.bfloat16)

    @pl.loop(0, CTX)
    def _(s):
        pltpu.make_async_copy(tok_ref, tokens_ref.at[s], t_recv.at[s]).wait()

    @pl.loop(1, CTX)
    def _(j):
        weight_copy(j).wait_send()
        token_copy(j).wait_send()

    @pl.when(plane != c)
    def _():
        weight_copy(0).wait_send()

    for d in range(1, CHAN):
        square_copy(d).wait_send()
        part_copy(d).wait_send()


def table_and_tokens(token_ids, embed_table, norm_gain, in_weight):
    rows = token_ids.shape[0]
    vocab, feats = embed_table.shape
    weight = jnp.transpose(in_weight, (1, 2, 0))
    dma = pltpu.SemaphoreType.DMA
    return pl.pallas_call(
        table_kernel,
        name="table",
        out_shape=(
            jax.ShapeDtypeStruct((3 * OWN, vocab), jnp.bfloat16),
            jax.ShapeDtypeStruct((CTX, 1, rows), jnp.int32),
        ),
        in_specs=[pl.BlockSpec(memory_space=pltpu.VMEM)] * 4,
        out_specs=(pl.BlockSpec(memory_space=pltpu.VMEM),) * 2,
        scratch_shapes=[
            pltpu.VMEM((CHAN, 3, OWN, feats), jnp.bfloat16),
            pltpu.VMEM((CHAN, 8, vocab), jnp.float32),
            pltpu.VMEM((CHAN, 3 * OWN, vocab), jnp.float32),
            pltpu.VMEM((CHAN, 3 * OWN, vocab), jnp.bfloat16),
            pltpu.VMEM((CHAN, 3 * OWN, vocab), jnp.bfloat16),
            pltpu.VMEM((vocab, feats), jnp.bfloat16),
            dma((CTX,)), dma((CTX,)), dma((CTX,)), dma((CTX,)),
            dma((CHAN,)), dma((CHAN,)), dma((CHAN,)), dma((CHAN,)),
        ],
        compiler_params=pltpu.CompilerParams(
            collective_id=0, has_side_effects=True, vmem_limit_bytes=VMEM_LIMIT
        ),
    )(token_ids.reshape(1, rows), embed_table, norm_gain.reshape(CHAN, 1, feats), weight)


def conv_kernel(
    table_ref, tokens_ref, taps_ref, residue_ref, decay_ref, skip_ref, out_ref,
    toeplitz, carried_ref, query_ref, result,
):
    first = lax.axis_index("ctx") * OWN
    chans = decay_ref.shape[1]
    f32, bf16 = jnp.float32, jnp.bfloat16

    chosen = lax.broadcasted_iota(jnp.int32, (OWN, chans), 1) == first + lax.broadcasted_iota(
        jnp.int32, (OWN, chans), 0
    )

    def column(row):
        return jnp.sum(jnp.where(chosen, row, 0.0), axis=1, keepdims=True)

    decay_all = decay_ref[...]
    weight_all = residue_ref[...] * jnp.sqrt(decay_all)
    lane = lax.broadcasted_iota(jnp.int32, (OWN, SEG), 1)
    steps = lane.astype(f32)
    taps_long = jnp.zeros((OWN, SEG), f32)
    for m in range(MODES):
        taps_long = taps_long + column(weight_all[m : m + 1]) * jnp.exp(-column(decay_all[m : m + 1]) * steps)
    square_row = lax.broadcasted_iota(jnp.int32, (SEG, SEG), 0)
    square_lane = lax.broadcasted_iota(jnp.int32, (SEG, SEG), 1)
    causal = square_lane >= square_row
    for ch in range(OWN):
        spread = jnp.broadcast_to(taps_long[ch : ch + 1], (SEG, SEG))
        rolled = pltpu.roll(spread, 0, axis=1, stride=1, stride_axis=0)
        toeplitz[ch] = jnp.where(causal, rolled, 0.0).astype(bf16)

    pairs = OWN * MODES
    row_of = lax.broadcasted_iota(jnp.int32, (chans, pairs), 0)
    pick = (row_of == first + lax.broadcasted_iota(jnp.int32, (chans, pairs), 1) // MODES).astype(f32)
    own_mode = (
        lax.broadcasted_iota(jnp.int32, (MODES, pairs), 0)
        == lax.broadcasted_iota(jnp.int32, (MODES, pairs), 1) % MODES
    )

    def pair_row(array):
        wide = jnp.dot(array, pick, precision=HIGHEST, preferred_element_type=f32)
        return jnp.sum(jnp.where(own_mode, wide, 0.0), axis=0, keepdims=True)

    decay_row = pair_row(decay_all)
    decay_col = jnp.transpose(jnp.broadcast_to(decay_row, (128, pairs)))[:, 0:1]
    weight_col = jnp.transpose(jnp.broadcast_to(pair_row(weight_all), (128, pairs)))[:, 0:1]
    to_end = (SEG - 1 - square_row).astype(f32)
    gather_high, gather_low = high_low(jnp.exp(-decay_row * to_end))
    spread_high, spread_low = high_low(weight_col * jnp.exp(-decay_col * (square_lane + 1).astype(f32)))

    table = jnp.concatenate([table_ref[:, :SEG], table_ref[:, SEG:]], axis=0)
    taps = []
    for j in range(3):
        taps.append(
            jnp.concatenate([column(taps_ref[j, b : b + 1, :]) for b in range(3)], axis=0)
        )
    vocab_row = lax.broadcasted_iota(jnp.int32, (SEG, SEG), 0)

    def segment(g, part, before):
        ids = tokens_ref[g, :, part * SEG : (part + 1) * SEG]
        onehot = jnp.where(vocab_row == (ids & (SEG - 1)), 1.0, 0.0).astype(bf16)
        both = dot(table, onehot)
        projected = jnp.where(ids >= SEG, both[3 * OWN :], both[: 3 * OWN])
        longer = jnp.concatenate([before, projected], axis=1)
        branches = (
            taps[0] * projected
            + taps[1] * pltpu.roll(longer, 1, axis=1)[:, 128:]
            + taps[2] * pltpu.roll(longer, 2, axis=1)[:, 128:]
        )
        carried = (branches[OWN : 2 * OWN] * branches[2 * OWN :]).astype(bf16).astype(f32)
        at = pl.ds(g * PER + part, OWN, stride=SEGS)
        for half in range(2):
            carried_ref[half, at, :] = carried[:, half * 128 : (half + 1) * 128]
            query_ref[half, at, :] = branches[:OWN, half * 128 : (half + 1) * 128]
        return projected[:, SEG - 128 :]

    def block(g, before):
        for part in range(PER):
            before = segment(g, part, before)
        return before

    lax.fori_loop(0, SEGS // PER, block, jnp.zeros((3 * OWN, 128), f32), unroll=2)

    def both_halves(ref, ch):
        return jnp.concatenate([ref[half, ch * SEGS : (ch + 1) * SEGS, :] for half in range(2)], axis=1)

    channel_of = lax.broadcasted_iota(jnp.int32, (SEGS, pairs), 1) // MODES
    added = jnp.zeros((SEGS, pairs), f32)
    for ch in range(OWN):
        signal = both_halves(carried_ref, ch).astype(bf16)
        added = added + jnp.where(channel_of == ch, dot(signal, gather_high) + dot(signal, gather_low), 0.0)

    def later(x, by):
        return jnp.concatenate([jnp.zeros((by, pairs), f32), x[: SEGS - by]], axis=0)

    state = later(added, 1)
    by = 1
    while by < SEGS:
        state = state + jnp.exp(-decay_row * float(SEG * by)) * later(state, by)
        by *= 2
    state_high, state_low = high_low(state)

    zero = jnp.zeros((), bf16)
    skip_column = column(skip_ref[...])
    for ch in range(OWN):
        carried = both_halves(carried_ref, ch)
        high = jnp.where(channel_of == ch, state_high, zero)
        low = jnp.where(channel_of == ch, state_low, zero)
        conv = dot(carried.astype(bf16), toeplitz[ch])
        conv = conv + dot(high, spread_high) + dot(low, spread_high) + dot(high, spread_low)
        gated = both_halves(query_ref, ch) * (conv + skip_column[ch : ch + 1] * carried)
        for half in range(2):
            result[half, pl.ds(ch, SEGS, stride=OWN), :] = gated[:, half * 128 : (half + 1) * 128]
    out_ref[...] = jnp.concatenate([result[half] for half in range(2)], axis=1).astype(bf16)


def convolved(table, tokens, short_filter, residue, decay_rate, skip_bias):
    f32 = jnp.float32
    return pl.pallas_call(
        conv_kernel,
        name="conv",
        out_shape=jax.ShapeDtypeStruct((SEGS * OWN, SEG), jnp.bfloat16),
        in_specs=[pl.BlockSpec(memory_space=pltpu.VMEM)] * 6,
        out_specs=pl.BlockSpec(memory_space=pltpu.VMEM),
        scratch_shapes=[
            pltpu.VMEM((OWN, SEG, SEG), jnp.bfloat16),
            pltpu.VMEM((2, OWN * SEGS, 128), f32),
            pltpu.VMEM((2, OWN * SEGS, 128), f32),
            pltpu.VMEM((2, SEGS * OWN, 128), f32),
        ],
        compiler_params=pltpu.CompilerParams(vmem_limit_bytes=VMEM_LIMIT),
    )(table, tokens, short_filter, residue, decay_rate, skip_bias.reshape(1, -1))


def exchange_kernel(out_ref, got_ref, send_sem, recv_sem):
    i, c = lax.axis_index("ctx"), lax.axis_index("chan")
    barrier = pltpu.get_barrier_semaphore()

    @pl.loop(1, CTX)
    def _(j):
        pl.semaphore_signal(barrier, inc=1, device_id=((i + j) % CTX, c), device_id_type=MESH)

    pl.semaphore_wait(barrier, CTX - 1)

    def copy(j):
        to = (i + j) % CTX
        return send(
            out_ref.at[to], got_ref.at[:, pl.ds(i * OWN, OWN), :], send_sem.at[j], recv_sem.at[i], to, c
        )

    @pl.loop(1, CTX)
    def _(j):
        copy(j).start()

    own = pltpu.make_async_copy(out_ref.at[i], got_ref.at[:, pl.ds(i * OWN, OWN), :], recv_sem.at[i])
    own.start()

    @pl.loop(0, CTX)
    def _(s):
        pltpu.make_async_copy(out_ref.at[0], got_ref.at[:, pl.ds(s * OWN, OWN), :], recv_sem.at[s]).wait()

    @pl.loop(1, CTX)
    def _(j):
        copy(j).wait_send()


def exchanged(out):
    dma = pltpu.SemaphoreType.DMA
    return pl.pallas_call(
        exchange_kernel,
        name="exchange",
        out_shape=jax.ShapeDtypeStruct((PER, CTX * OWN, SEG), jnp.bfloat16),
        in_specs=[pl.BlockSpec(memory_space=pltpu.VMEM)],
        out_specs=pl.BlockSpec(memory_space=pltpu.VMEM),
        scratch_shapes=[dma((CTX,)), dma((CTX,))],
        compiler_params=pltpu.CompilerParams(
            collective_id=1, has_side_effects=True, vmem_limit_bytes=VMEM_LIMIT
        ),
    )(out.reshape(CTX, PER, OWN, SEG))


def turn_kernel(got_ref, out_ref):
    unit = (
        lax.broadcasted_iota(jnp.int32, (SEG, SEG), 0) == lax.broadcasted_iota(jnp.int32, (SEG, SEG), 1)
    ).astype(jnp.bfloat16)
    for g in range(PER):
        turned = lax.dot_general(unit, got_ref[g], NT, preferred_element_type=jnp.float32)
        out_ref[g * SEG : (g + 1) * SEG, :] = turned.astype(jnp.bfloat16)


def turned(got):
    return pl.pallas_call(
        turn_kernel,
        name="turn",
        out_shape=jax.ShapeDtypeStruct((PER * SEG, got.shape[1]), jnp.bfloat16),
        in_specs=[pl.BlockSpec(memory_space=pltpu.VMEM)],
        out_specs=pl.BlockSpec(memory_space=pltpu.VMEM),
        compiler_params=pltpu.CompilerParams(vmem_limit_bytes=VMEM_LIMIT),
    )(got)


def per_device(
    token_ids, embed_table, norm_gain, in_weight, short_filter, residue, decay_rate, skip_bias
):
    table, tokens = table_and_tokens(token_ids, embed_table, norm_gain, in_weight)
    out = convolved(table, tokens, short_filter, residue, decay_rate, skip_bias)
    return turned(exchanged(out))


def solution(mesh):
    return jax.shard_map(
        per_device,
        mesh=mesh,
        in_specs=(
            P("ctx"),
            P(None, "chan"),
            P(),
            P("ctx", None, "chan"),
            P(None, None, "chan"),
            P(None, "chan"),
            P(None, "chan"),
            P("chan"),
        ),
        out_specs=P("ctx", "chan"),
        check_vma=False,
    )
```

```python
import functools

import jax
import jax.numpy as jnp
from jax import lax
from jax.experimental import pallas as pl
from jax.experimental.pallas import tpu as pltpu
from jax.sharding import PartitionSpec as P

MESH = pl.DeviceIdType.MESH
EPS = 1e-06
VMEM_LIMIT = 48 * 1024 * 1024

CTX, CHAN, PLANE = 32, 4, 8
OWN = 16
SEG = 256
SEGS = 96
PER = 3
PART = 24
HALF = 128
MODES = 16
PAIRS = OWN * MODES
NT = (((1,), (1,)), ((), ()))
HIGHEST = lax.Precision.HIGHEST


def dot(a, b):
    return jnp.dot(a, b, preferred_element_type=jnp.float32)


def high_low(x):
    high = x.astype(jnp.bfloat16)
    return high, (x - high.astype(jnp.float32)).astype(jnp.bfloat16)


def send(src, dst, send_sem, recv_sem, i, c):
    return pltpu.make_async_remote_copy(
        src_ref=src, dst_ref=dst, send_sem=send_sem, recv_sem=recv_sem, device_id=(i, c), device_id_type=MESH
    )


def load_own(row_refs, lanes_from, shift):
    rows = [ref[:, pl.ds(lanes_from, HALF)] for ref in row_refs]
    return [pltpu.roll(array, shift, axis=1) for array in rows]


def filter_tables(decay, weight, toeplitz, gather, spread):
    f32, bf16 = jnp.float32, jnp.bfloat16
    decay_turned = jnp.transpose(decay)[:OWN]
    weight_turned = jnp.transpose(weight)[:OWN]
    lane = lax.broadcasted_iota(jnp.int32, (OWN, HALF), 1).astype(f32)
    near = jnp.zeros((OWN, HALF), f32)
    far = jnp.zeros((OWN, HALF), f32)
    for m in range(MODES):
        rate = jnp.broadcast_to(decay_turned[:, m : m + 1], (OWN, HALF))
        height = jnp.broadcast_to(weight_turned[:, m : m + 1], (OWN, HALF))
        near = near + height * jnp.exp(-rate * lane)
        far = far + height * jnp.exp(-rate * (lane + float(HALF)))
    causal = lax.broadcasted_iota(jnp.int32, (HALF, HALF), 1) >= lax.broadcasted_iota(jnp.int32, (HALF, HALF), 0)
    for ch in range(OWN):
        near_rolled = pltpu.roll(
            jnp.broadcast_to(near[ch : ch + 1], (HALF, HALF)), 0, axis=1, stride=1, stride_axis=0
        )
        far_rolled = pltpu.roll(
            jnp.broadcast_to(far[ch : ch + 1], (HALF, HALF)), 0, axis=1, stride=1, stride_axis=0
        )
        diagonal = jnp.where(causal, near_rolled, 0.0).astype(bf16)
        toeplitz[ch, :HALF, :HALF] = diagonal
        toeplitz[ch, HALF:, HALF:] = diagonal
        toeplitz[ch, :HALF, HALF:] = jnp.where(causal, far_rolled, near_rolled).astype(bf16)
        toeplitz[ch, HALF:, :HALF] = jnp.zeros((HALF, HALF), bf16)

    pick = (
        lax.broadcasted_iota(jnp.int32, (HALF, PAIRS), 0)
        == lax.broadcasted_iota(jnp.int32, (HALF, PAIRS), 1) // MODES
    ).astype(f32)
    own_mode = (
        lax.broadcasted_iota(jnp.int32, (MODES, PAIRS), 0)
        == lax.broadcasted_iota(jnp.int32, (MODES, PAIRS), 1) % MODES
    )

    def pair_row(array):
        wide = jnp.dot(array, pick, precision=HIGHEST, preferred_element_type=f32)
        return jnp.sum(jnp.where(own_mode, wide, 0.0), axis=0, keepdims=True)

    decay_row = pair_row(decay)
    decay_column = jnp.transpose(jnp.broadcast_to(decay_row, (HALF, PAIRS)))
    weight_column = jnp.transpose(jnp.broadcast_to(pair_row(weight), (HALF, PAIRS)))
    to_end = (SEG - 1 - lax.broadcasted_iota(jnp.int32, (SEG, PAIRS), 0)).astype(f32)
    gather[:SEG], gather[SEG:] = high_low(jnp.exp(-decay_row * to_end))
    for half in range(2):
        lanes = slice(half * HALF, (half + 1) * HALF)
        after = lax.broadcasted_iota(jnp.int32, (PAIRS, HALF), 1).astype(f32) + float(half * HALF + 1)
        high, low = high_low(weight_column * jnp.exp(-decay_column * after))
        spread[:PAIRS, lanes] = high
        spread[PAIRS : 2 * PAIRS, lanes] = high
        spread[2 * PAIRS :, lanes] = low
    return decay_row


def short_filter_and_gate(table_ref, tokens_ref, taps_ref, carried_ref, query_ref):
    f32, bf16 = jnp.float32, jnp.bfloat16
    table = jnp.concatenate([table_ref[:, :SEG], table_ref[:, SEG:]], axis=0)
    entry = lax.broadcasted_iota(jnp.int32, (SEG, SEG), 0).astype(f32).astype(bf16)
    lane = lax.broadcasted_iota(jnp.int32, (3 * OWN, HALF), 1)
    one, zero = jnp.ones((), bf16), jnp.zeros((), bf16)

    def block(g, before):
        for part in range(PER):
            ids = tokens_ref[g, :, part * SEG : (part + 1) * SEG]
            chosen = (ids & (SEG - 1)).astype(f32).astype(bf16)
            both = dot(table, jnp.where(entry == chosen, one, zero))
            projected = jnp.where(ids >= SEG, both[3 * OWN :], both[: 3 * OWN])
            at = pl.ds(g * PER + part, OWN, stride=SEGS)
            for half in range(2):
                here = projected[:, half * HALF : (half + 1) * HALF]
                turned = (pltpu.roll(here, 1, axis=1), pltpu.roll(here, 2, axis=1))
                branches = (
                    taps_ref[0] * here
                    + taps_ref[1] * jnp.where(lane < 1, before[0], turned[0])
                    + taps_ref[2] * jnp.where(lane < 2, before[1], turned[1])
                )
                before = turned
                carried = branches[OWN : 2 * OWN] * branches[2 * OWN :]
                carried_ref[half, at, :] = carried.astype(bf16).astype(f32)
                query_ref[half, at, :] = branches[:OWN]
        return before

    nothing = jnp.zeros((3 * OWN, HALF), f32)
    lax.fori_loop(0, SEGS // PER, block, (nothing, nothing), unroll=UNROLL)


UNROLL = 8


def both_halves(ref, rows):
    return jnp.concatenate([ref[half, rows, :] for half in range(2)], axis=1)


def segment_states(carried_ref, gather, decay_row, state_ref):
    f32, bf16 = jnp.float32, jnp.bfloat16
    channel_of = lax.broadcasted_iota(jnp.int32, (SEGS, PAIRS), 1) // MODES
    added = jnp.zeros((SEGS, PAIRS), f32)
    group = 4
    for first in range(0, OWN, group):
        signal = both_halves(carried_ref, slice(first * SEGS, (first + group) * SEGS)).astype(bf16)
        enters = dot(jnp.concatenate([signal, signal], axis=1), gather[...])
        for ch in range(group):
            added = added + jnp.where(channel_of == first + ch, enters[ch * SEGS : (ch + 1) * SEGS], 0.0)

    def later(x, by):
        return jnp.concatenate([jnp.zeros((by, PAIRS), f32), x[: SEGS - by]], axis=0)

    state = later(added, 1)
    by = 1
    while by < SEGS:
        state = state + jnp.exp(-decay_row * float(SEG * by)) * later(state, by)
        by *= 2
    state_ref[...] = state


def outputs_of_part(q, carried_ref, query_ref, state_ref, toeplitz, spread, skip_ref, result, ready):
    f32, bf16 = jnp.float32, jnp.bfloat16
    first = pl.multiple_of(q * PART, PART)
    high, low = high_low(state_ref[pl.ds(first, PART), :])
    channel_of = lax.broadcasted_iota(jnp.int32, (PART, PAIRS), 1) // MODES
    modes = jnp.concatenate([high, low, high], axis=1)
    channels = jnp.concatenate([channel_of] * 3, axis=1)
    zero = jnp.zeros((), bf16)
    for ch in range(OWN):
        rows = pl.ds(pl.multiple_of(ch * SEGS + first, 8), PART)
        carried = both_halves(carried_ref, rows)
        conv = dot(carried.astype(bf16), toeplitz[ch])
        conv = conv + dot(jnp.where(channels == ch, modes, zero), spread[...])
        gated = both_halves(query_ref, rows) * (conv + skip_ref[ch : ch + 1] * carried)
        for half in range(2):
            result[half, pl.ds(ch, PART, stride=OWN), :] = gated[:, half * HALF : (half + 1) * HALF]
    block = both_halves(result, slice(None)).astype(bf16)
    ready[pl.ds(q * PLANE, PLANE)] = block.reshape(PLANE, PER, OWN, SEG)


def main_kernel(
    tok_hbm, embed_hbm, gain_hbm, weight_hbm, taps_hbm, residue_hbm, decay_hbm, skip_hbm, got_ref,
    tok, embed, gain, weight, taps_all, residue, decay, skip_all,
    turned_weight, got_weight, got_square, scaled, part, part_send, part_got, tokens, table,
    toeplitz, gather, spread, taps, skip, carried, query, state, result, ready,
    in_sem, w_send, w_recv, t_send, t_recv, s_send, s_recv, p_send, p_recv, o_send, o_recv,
):
    f32, bf16 = jnp.float32, jnp.bfloat16
    i, c = lax.axis_index("ctx"), lax.axis_index("chan")
    plane, place = i // PLANE, i % PLANE

    loads = [
        pltpu.make_async_copy(src, dst, in_sem.at[n])
        for n, (src, dst) in enumerate(
            (
                (weight_hbm, weight), (tok_hbm, tok), (embed_hbm, embed), (gain_hbm, gain),
                (taps_hbm, taps_all), (residue_hbm, residue), (decay_hbm, decay), (skip_hbm, skip_all),
            )
        )
    ]
    for load in loads:
        load.start()

    barrier = pltpu.get_barrier_semaphore()

    @pl.loop(0, CTX)
    def _(j):
        row, col = c * PLANE + j % PLANE, j // PLANE

        @pl.when(jnp.logical_or(row != i, col != c))
        def _():
            pl.semaphore_signal(barrier, inc=1, device_id=(row, col), device_id_type=MESH)

    @pl.loop(1, CTX)
    def _(j):
        pl.semaphore_signal(barrier, inc=1, device_id=((i + j) % CTX, c), device_id_type=MESH)

    for d in range(1, CHAN):
        pl.semaphore_signal(barrier, inc=1, device_id=(i, (c + d) % CHAN), device_id_type=MESH)

    loads[0].wait()
    for b in range(3):
        turned_weight[b] = jnp.transpose(weight[b])
    loads[1].wait()
    tokens[i] = tok[...].reshape(1, tok.shape[0])

    pl.semaphore_wait(barrier, CTX - jnp.where(plane == c, 1, 0) + (CTX - 1) + (CHAN - 1))

    def weight_copy(j):
        to = (i + j) % CTX
        return send(
            turned_weight.at[:, pl.ds(to * OWN, OWN), :],
            got_weight.at[c, :, :, pl.ds(place * HALF, HALF)],
            w_send.at[j],
            w_recv.at[c * PLANE + place],
            to,
            plane,
        )

    def token_copy(j):
        return send(tokens.at[i], tokens.at[i], t_send.at[j], t_recv.at[i], (i + j) % CTX, c)

    @pl.loop(1, CTX)
    def _(j):
        weight_copy(j).start()

    self_copy = pltpu.make_async_copy(
        turned_weight.at[:, pl.ds(i * OWN, OWN), :],
        got_weight.at[c, :, :, pl.ds(place * HALF, HALF)],
        w_recv.at[c * PLANE + place],
    )

    @pl.when(plane == c)
    def _():
        self_copy.start()

    @pl.when(plane != c)
    def _():
        weight_copy(0).start()

    @pl.loop(1, CTX)
    def _(j):
        token_copy(j).start()

    loads[2].wait()
    loads[3].wait()
    wide = embed[...].astype(f32)
    feats = embed.shape[1]
    square_high, square_low = high_low(wide * wide)
    ones = jnp.ones((8, feats), bf16)
    squares = lax.dot_general(ones, square_high, NT, preferred_element_type=f32)
    got_square[c] = squares + lax.dot_general(ones, square_low, NT, preferred_element_type=f32)

    def square_copy(d):
        return send(got_square.at[c], got_square.at[c], s_send.at[d], s_recv.at[c], i, (c + d) % CHAN)

    for d in range(1, CHAN):
        square_copy(d).start()
    scaled[...] = (wide * gain[pl.ds(c * feats, feats)].reshape(1, feats)).astype(bf16)

    for load in loads[4:]:
        load.wait()
    lanes_from = pl.multiple_of((i // PLANE) * HALF, HALF)
    shift = lax.rem(HALF - place * OWN, HALF)
    decay_own, residue_own = load_own([decay, residue], lanes_from, shift)
    weight_own = residue_own * jnp.sqrt(decay_own)
    decay_row = filter_tables(decay_own, weight_own, toeplitz, gather, spread)
    for j in range(3):
        (rows,) = load_own([taps_all.at[j]], lanes_from, shift)
        padded = jnp.concatenate([rows, jnp.zeros((5, HALF), f32)], axis=0)
        columns = jnp.transpose(padded)[:OWN]
        for b in range(3):
            taps[j, b * OWN : (b + 1) * OWN, :] = jnp.broadcast_to(columns[:, b : b + 1], (OWN, HALF))
    skip_row = pltpu.roll(
        jnp.broadcast_to(skip_all[pl.ds(lanes_from, HALF)].reshape(1, HALF), (8, HALF)), shift, axis=1
    )
    skip_column = jnp.transpose(skip_row)[:OWN, 0:1]
    skip[...] = jnp.broadcast_to(skip_column, (OWN, SEG))

    @pl.loop(0, CTX)
    def _(s):
        pltpu.make_async_copy(
            turned_weight.at[:, pl.ds(0, OWN), :],
            got_weight.at[s // PLANE, :, :, pl.ds((s % PLANE) * HALF, HALF)],
            w_recv.at[s],
        ).wait()

    def part_copy(d):
        to = (c + d) % CHAN
        return send(part_send.at[to], part_got.at[c], p_send.at[d], p_recv.at[c], i, to)

    product = lax.dot_general(
        got_weight[...].reshape(CHAN * 3 * OWN, feats), scaled[...], NT, preferred_element_type=f32
    )
    part[...] = product.reshape(part.shape)
    part_send[...] = product.astype(bf16).reshape(part.shape)
    for d in range(1, CHAN):
        part_copy(d).start()
    mean = got_square[c]
    for d in range(1, CHAN):
        source = (c + d) % CHAN
        send(got_square.at[c], got_square.at[source], s_send.at[d], s_recv.at[source], i, source).wait_recv()
        mean = mean + got_square[source]
    scale = lax.rsqrt(mean[0:1] * (1.0 / (CHAN * feats)) + EPS)

    @pl.loop(1, CTX)
    def _(j):
        s = (i + j) % CTX
        pltpu.make_async_copy(tokens.at[i], tokens.at[s], t_recv.at[s]).wait()

    total = part[c]
    for d in range(1, CHAN):
        source = (c + d) % CHAN
        send(part_send.at[0], part_got.at[source], p_send.at[d], p_recv.at[source], i, source).wait_recv()
        total = total + part_got[source].astype(f32)
    table[...] = (total * scale).astype(bf16)

    short_filter_and_gate(table, tokens, taps, carried, query)
    segment_states(carried, gather, decay_row, state)

    def out_copy(to, slot):
        return send(
            ready.at[to], got_ref.at[:, pl.ds(i * OWN, OWN), :], o_send.at[slot], o_recv.at[i], to, c
        )

    own_out = pltpu.make_async_copy(ready.at[i], got_ref.at[:, pl.ds(i * OWN, OWN), :], o_recv.at[i])

    @pl.loop(0, CTX // PLANE)
    def _(step):
        q = (plane + 1 + step) % (CTX // PLANE)
        outputs_of_part(q, carried, query, state, toeplitz, spread, skip, result, ready)

        @pl.loop(0, PLANE)
        def _(n):
            to = q * PLANE + (place + n) % PLANE

            @pl.when(to != i)
            def _():
                out_copy(to, to).start()

            @pl.when(to == i)
            def _():
                own_out.start()

    @pl.loop(0, CTX)
    def _(s):
        pltpu.make_async_copy(ready.at[0], got_ref.at[:, pl.ds(s * OWN, OWN), :], o_recv.at[s]).wait()

    @pl.loop(1, CTX)
    def _(j):
        weight_copy(j).wait_send()
        token_copy(j).wait_send()
        out_copy((i + j) % CTX, (i + j) % CTX).wait_send()

    @pl.when(plane != c)
    def _():
        weight_copy(0).wait_send()

    for d in range(1, CHAN):
        square_copy(d).wait_send()
        part_copy(d).wait_send()


def gathered(
    token_ids, embed_table, norm_gain, in_weight, short_filter, residue, decay_rate, skip_bias
):
    f32, bf16 = jnp.float32, jnp.bfloat16
    rows = token_ids.shape[0]
    vocab, feats = embed_table.shape
    chans = decay_rate.shape[1]
    weight = jnp.transpose(in_weight, (1, 0, 2))
    operands = (token_ids, embed_table, norm_gain, weight, short_filter, residue, decay_rate, skip_bias)
    dma, vmem = pltpu.SemaphoreType.DMA, pltpu.VMEM
    return pl.pallas_call(
        main_kernel,
        name="hyena",
        out_shape=jax.ShapeDtypeStruct((PER, CTX * OWN, SEG), bf16),
        in_specs=[pl.BlockSpec(memory_space=pltpu.HBM)] * len(operands),
        out_specs=pl.BlockSpec(memory_space=pltpu.VMEM),
        scratch_shapes=[
            vmem(token_ids.shape, jnp.int32),
            vmem(embed_table.shape, bf16),
            vmem(norm_gain.shape, f32),
            vmem(weight.shape, bf16),
            vmem(short_filter.shape, f32),
            vmem(residue.shape, f32),
            vmem(decay_rate.shape, f32),
            vmem(skip_bias.shape, f32),
            vmem((3, chans, in_weight.shape[0]), bf16),
            vmem((CHAN, 3, OWN, feats), bf16),
            vmem((CHAN, 8, vocab), f32),
            vmem((vocab, feats), bf16),
            vmem((CHAN, 3 * OWN, vocab), f32),
            vmem((CHAN, 3 * OWN, vocab), bf16),
            vmem((CHAN, 3 * OWN, vocab), bf16),
            vmem((CTX, 1, rows), jnp.int32),
            vmem((3 * OWN, vocab), bf16),
            vmem((OWN, SEG, SEG), bf16),
            vmem((2 * SEG, PAIRS), bf16),
            vmem((3 * PAIRS, SEG), bf16),
            vmem((3, 3 * OWN, HALF), f32),
            vmem((OWN, SEG), f32),
            vmem((2, OWN * SEGS, HALF), f32),
            vmem((2, OWN * SEGS, HALF), f32),
            vmem((SEGS, PAIRS), f32),
            vmem((2, PART * OWN, HALF), f32),
            vmem((CTX, PER, OWN, SEG), bf16),
            dma((8,)),
            dma((CTX,)), dma((CTX,)), dma((CTX,)), dma((CTX,)),
            dma((CHAN,)), dma((CHAN,)), dma((CHAN,)), dma((CHAN,)),
            dma((CTX,)), dma((CTX,)),
        ],
        compiler_params=pltpu.CompilerParams(
            collective_id=0, has_side_effects=True, vmem_limit_bytes=VMEM_LIMIT
        ),
    )(*operands)


def turn_kernel(got_ref, out_ref):
    unit = (
        lax.broadcasted_iota(jnp.int32, (SEG, SEG), 0) == lax.broadcasted_iota(jnp.int32, (SEG, SEG), 1)
    ).astype(jnp.bfloat16)
    for g in range(PER):
        turned = lax.dot_general(unit, got_ref[g], NT, preferred_element_type=jnp.float32)
        out_ref[g * SEG : (g + 1) * SEG, :] = turned.astype(jnp.bfloat16)


def turned(got):
    return pl.pallas_call(
        turn_kernel,
        name="turn",
        out_shape=jax.ShapeDtypeStruct((PER * SEG, got.shape[1]), jnp.bfloat16),
        in_specs=[pl.BlockSpec(memory_space=pltpu.VMEM)],
        out_specs=pl.BlockSpec(memory_space=pltpu.VMEM),
        compiler_params=pltpu.CompilerParams(vmem_limit_bytes=VMEM_LIMIT),
    )(got)


def per_device(*arrays):
    return turned(gathered(*arrays))


def solution(mesh):
    return jax.shard_map(
        per_device,
        mesh=mesh,
        in_specs=(
            P("ctx"),
            P(None, "chan"),
            P(),
            P("ctx", None, "chan"),
            P(None, None, "chan"),
            P(None, "chan"),
            P(None, "chan"),
            P("chan"),
        ),
        out_specs=P("ctx", "chan"),
        check_vma=False,
    )
```

```python
import functools

import jax
import jax.numpy as jnp
from jax import lax
from jax.experimental import pallas as pl
from jax.experimental.pallas import tpu as pltpu
from jax.sharding import PartitionSpec as P

MESH = pl.DeviceIdType.MESH
EPS = 1e-06
VMEM_LIMIT = 60 * 1024 * 1024

CTX, CHAN, PLANE = 32, 4, 8
OWN = 16
SEG = 256
SEGS = 96
PER = 3
PART = 24
HALF = 128
MODES = 16
PAIRS = OWN * MODES
FEW = 8
FEWS = FEW * MODES
WEIGHT_ROWS = ((0, 32), (32, 16))
TABLE_ROWS = ((0, 8, 16), (32, 24, 40))
NT = (((1,), (1,)), ((), ()))
HIGHEST = lax.Precision.HIGHEST


def dot(a, b):
    return jnp.dot(a, b, preferred_element_type=jnp.float32)


def high_low(x):
    high = x.astype(jnp.bfloat16)
    return high, (x - high.astype(jnp.float32)).astype(jnp.bfloat16)


def send(src, dst, send_sem, recv_sem, i, c):
    return pltpu.make_async_remote_copy(
        src_ref=src, dst_ref=dst, send_sem=send_sem, recv_sem=recv_sem, device_id=(i, c), device_id_type=MESH
    )


def load_own(row_refs, lanes_from, shift):
    rows = [ref[:, pl.ds(lanes_from, HALF)] for ref in row_refs]
    return [pltpu.roll(array, shift, axis=1) for array in rows]


def filter_tables(decay, weight, gather, reach):
    f32, bf16 = jnp.float32, jnp.bfloat16
    decay_turned = jnp.transpose(decay)[:OWN]
    weight_turned = jnp.transpose(weight)[:OWN]
    lane = lax.broadcasted_iota(jnp.int32, (OWN, HALF), 1).astype(f32)
    near = jnp.zeros((OWN, HALF), f32)
    far = jnp.zeros((OWN, HALF), f32)
    for m in range(MODES):
        rate = jnp.broadcast_to(decay_turned[:, m : m + 1], (OWN, HALF))
        height = jnp.broadcast_to(weight_turned[:, m : m + 1], (OWN, HALF))
        near = near + height * jnp.exp(-rate * lane)
        far = far + height * jnp.exp(-rate * (lane + float(HALF)))
    causal = lax.broadcasted_iota(jnp.int32, (HALF, HALF), 1) >= lax.broadcasted_iota(jnp.int32, (HALF, HALF), 0)
    for ch in range(OWN):
        near_rolled = pltpu.roll(
            jnp.broadcast_to(near[ch : ch + 1], (HALF, HALF)), 0, axis=1, stride=1, stride_axis=0
        )
        far_rolled = pltpu.roll(
            jnp.broadcast_to(far[ch : ch + 1], (HALF, HALF)), 0, axis=1, stride=1, stride_axis=0
        )
        diagonal = jnp.where(causal, near_rolled, 0.0).astype(bf16)
        part, top = ch // FEW, ch % FEW * SEG
        middle, end = top + HALF, top + SEG
        reach[part, top:middle, :HALF] = diagonal
        reach[part, middle:end, HALF:] = diagonal
        reach[part, top:middle, HALF:] = jnp.where(causal, far_rolled, near_rolled).astype(bf16)
        reach[part, middle:end, :HALF] = jnp.zeros((HALF, HALF), bf16)

    pick = (
        lax.broadcasted_iota(jnp.int32, (HALF, PAIRS), 0)
        == lax.broadcasted_iota(jnp.int32, (HALF, PAIRS), 1) // MODES
    ).astype(f32)
    own_mode = (
        lax.broadcasted_iota(jnp.int32, (MODES, PAIRS), 0)
        == lax.broadcasted_iota(jnp.int32, (MODES, PAIRS), 1) % MODES
    )

    def pair_row(array):
        wide = jnp.dot(array, pick, precision=HIGHEST, preferred_element_type=f32)
        return jnp.sum(jnp.where(own_mode, wide, 0.0), axis=0, keepdims=True)

    decay_row = pair_row(decay)
    decay_column = jnp.transpose(jnp.broadcast_to(decay_row, (HALF, PAIRS)))
    weight_column = jnp.transpose(jnp.broadcast_to(pair_row(weight), (HALF, PAIRS)))
    to_end = (SEG - 1 - lax.broadcasted_iota(jnp.int32, (SEG, PAIRS), 0)).astype(f32)
    entering = high_low(jnp.exp(-decay_row * to_end))
    for part in range(2):
        for n in range(2):
            gather[part, :, n * FEWS : (n + 1) * FEWS] = entering[n][:, part * FEWS : (part + 1) * FEWS]
    for half in range(2):
        lanes = slice(half * HALF, (half + 1) * HALF)
        after = lax.broadcasted_iota(jnp.int32, (PAIRS, HALF), 1).astype(f32) + float(half * HALF + 1)
        high, low = high_low(weight_column * jnp.exp(-decay_column * after))
        for part in range(2):
            rows = slice(part * FEWS, (part + 1) * FEWS)
            for n, piece in enumerate((high, high, low)):
                top = FEW * SEG + n * FEWS
                reach[part, top : top + FEWS, lanes] = piece[rows]
    return decay_row


def short_filter_and_gate(table, tokens_ref, taps_ref, carried_ref, query_ref):
    f32, bf16 = jnp.float32, jnp.bfloat16
    rows = 3 * FEW
    entry = lax.broadcasted_iota(jnp.int32, (SEG, SEG), 0).astype(f32).astype(bf16)
    lane = lax.broadcasted_iota(jnp.int32, (rows, HALF), 1)
    one, zero = jnp.ones((), bf16), jnp.zeros((), bf16)

    def block(g, before):
        for part in range(PER):
            ids = tokens_ref[g, :, part * SEG : (part + 1) * SEG]
            chosen = (ids & (SEG - 1)).astype(f32).astype(bf16)
            both = dot(table, jnp.where(entry == chosen, one, zero))
            projected = jnp.where(ids >= SEG, both[rows:], both[:rows])
            at = pl.ds(pl.multiple_of((g * PER + part) * FEW, FEW), FEW)
            for half in range(2):
                lanes = slice(half * HALF, (half + 1) * HALF)
                here = projected[:, lanes]
                turned = (pltpu.roll(here, 1, axis=1), pltpu.roll(here, 2, axis=1))
                branches = (
                    taps_ref[0] * here
                    + taps_ref[1] * jnp.where(lane < 1, before[0], turned[0])
                    + taps_ref[2] * jnp.where(lane < 2, before[1], turned[1])
                )
                before = turned
                carried = branches[FEW : 2 * FEW] * branches[2 * FEW :]
                carried_ref[at, lanes] = carried.astype(bf16).astype(f32)
                query_ref[at, lanes] = branches[:FEW]
        return before

    nothing = jnp.zeros((rows, HALF), f32)
    lax.fori_loop(0, SEGS // PER, block, (nothing, nothing), unroll=UNROLL)


UNROLL = 16


def own_pairs():
    shape = (1, FEW, FEWS)
    return lax.broadcasted_iota(jnp.int32, shape, 2) // MODES == lax.broadcasted_iota(jnp.int32, shape, 1)


def segment_states(carried_ref, gather, decay_row, state_ref):
    f32, bf16 = jnp.float32, jnp.bfloat16
    enters = dot(carried_ref[...].astype(bf16), gather[...])
    enters = (enters[:, :FEWS] + enters[:, FEWS:]).reshape(SEGS, FEW, FEWS)
    added = jnp.sum(jnp.where(own_pairs(), enters, 0.0), axis=1)

    def later(x, by):
        return jnp.concatenate([jnp.zeros((by, FEWS), f32), x[: SEGS - by]], axis=0)

    state = later(added, 1)
    by = 1
    while by < SEGS:
        state = state + jnp.exp(-decay_row * float(SEG * by)) * later(state, by)
        by *= 2
    state_ref[...] = state


def outputs_of_part(q, carried_ref, query_ref, state_ref, reach, skip_ref, ready):
    f32, bf16 = jnp.float32, jnp.bfloat16
    first = pl.multiple_of(q * PART, PART)
    rows = pl.ds(pl.multiple_of(first * FEW, FEW), PART * FEW)
    carried = carried_ref[rows, :].reshape(PART, FEW, SEG)
    channel = lax.broadcasted_iota(jnp.int32, (1, FEW, SEG), 1)
    parts = [
        jnp.where(channel == ch, carried, 0.0).reshape(PART * FEW, SEG).astype(bf16) for ch in range(FEW)
    ]
    state = jnp.where(own_pairs(), state_ref[pl.ds(first, PART), :][:, None, :], 0.0)
    high, low = high_low(state.reshape(PART * FEW, FEWS))
    conv = dot(jnp.concatenate(parts + [high, low, high], axis=1), reach[...])
    gated = query_ref[rows, :] * (conv + (skip_ref[...][None] * carried).reshape(PART * FEW, SEG))
    halves = [gated[:, half * HALF : (half + 1) * HALF].reshape(PART, 1, FEW, HALF) for half in range(2)]
    block = jnp.concatenate(halves, axis=1).reshape(PLANE, PER, 2 * FEW, HALF)
    ready[pl.ds(q * PLANE, PLANE)] = block.astype(bf16)


def main_kernel(
    tok_hbm, embed_hbm, gain_hbm, weight_hbm, taps_hbm, residue_hbm, decay_hbm, skip_hbm, got_ref,
    tok, own_tokens, embed, gain, weight, taps_all, residue, decay, skip_all,
    turned_weight, got_weight, got_square, scaled, part, part_send0, part_send1, part_got0, part_got1, tokens, table,
    gather, reach, taps, skip, carried, query, state, ready,
    in_sem, w_send, w_recv, t_send, t_recv, u_send, u_recv, s_send, s_recv, p_send, p_recv, o_send, o_recv,
):
    f32, bf16 = jnp.float32, jnp.bfloat16
    i, c = lax.axis_index("ctx"), lax.axis_index("chan")
    plane, place = i // PLANE, i % PLANE

    loads = [
        pltpu.make_async_copy(src, dst, in_sem.at[n])
        for n, (src, dst) in enumerate(
            (
                (weight_hbm, weight), (tok_hbm, tok), (embed_hbm, embed), (gain_hbm, gain),
                (taps_hbm, taps_all), (residue_hbm, residue), (decay_hbm, decay), (skip_hbm, skip_all),
            )
        )
    ]
    for load in loads:
        load.start()

    barrier = pltpu.get_barrier_semaphore()

    @pl.loop(0, CTX)
    def _(j):
        row, col = c * PLANE + j % PLANE, j // PLANE

        @pl.when(jnp.logical_or(row != i, col != c))
        def _():
            pl.semaphore_signal(barrier, inc=1, device_id=(row, col), device_id_type=MESH)

    for d in range(1, CHAN):
        pl.semaphore_signal(barrier, inc=1, device_id=(i, (c + d) % CHAN), device_id_type=MESH)

    loads[0].wait()
    eights = [jnp.transpose(weight[b].astype(f32)).reshape(CTX, 2, FEW, HALF) for b in range(3)]
    order = ((0, 0), (1, 0), (2, 0), (1, 1), (0, 1), (2, 1))
    rows = jnp.concatenate([eights[b][:, part : part + 1] for b, part in order], axis=1)
    turned_weight[...] = rows.reshape(turned_weight.shape).astype(bf16)
    loads[1].wait()
    own_tokens[...] = tok[...].reshape(1, tok.shape[0])

    pl.semaphore_wait(barrier, CTX - jnp.where(plane == c, 1, 0) + CHAN - 1)

    def weight_slices(h, to, slot):
        rows = pl.ds(*WEIGHT_ROWS[h])
        lanes = pl.ds(pl.multiple_of(slot % PLANE * HALF, HALF), HALF)
        return turned_weight.at[to, rows, :], got_weight.at[slot // PLANE, rows, lanes], w_recv.at[h, slot]

    def weight_copy(h, j):
        to = (i + j) % CTX
        src, dst, sem = weight_slices(h, to, c * PLANE + place)
        return send(src, dst, w_send.at[h, j], sem, to, plane)

    def start_weights(h):
        @pl.loop(1, CTX)
        def _(j):
            weight_copy(h, j).start()

        @pl.when(plane == c)
        def _():
            pltpu.make_async_copy(*weight_slices(h, i, c * PLANE + place)).start()

        @pl.when(plane != c)
        def _():
            weight_copy(h, 0).start()

    def wait_weights(h):
        @pl.loop(0, CTX)
        def _(slot):
            pltpu.make_async_copy(*weight_slices(h, 0, slot)).wait()

    def token_copy(n):
        to = c * PLANE + (place + n) % PLANE
        return send(own_tokens, tokens.at[i], t_send.at[n], t_recv.at[place], to, plane)

    own_token_copy = pltpu.make_async_copy(own_tokens, tokens.at[i], t_recv.at[place])

    @pl.when(plane == c)
    def _():
        own_token_copy.start()

    @pl.when(plane != c)
    def _():
        token_copy(0).start()

    @pl.loop(1, PLANE)
    def _(n):
        token_copy(n).start()

    start_weights(0)

    loads[2].wait()
    loads[3].wait()
    wide = embed[...].astype(f32)
    feats = embed.shape[1]
    square_high, square_low = high_low(wide * wide)
    ones = jnp.ones((8, feats), bf16)
    squares = lax.dot_general(ones, square_high, NT, preferred_element_type=f32)
    got_square[c] = squares + lax.dot_general(ones, square_low, NT, preferred_element_type=f32)

    def square_copy(d):
        return send(got_square.at[c], got_square.at[c], s_send.at[d], s_recv.at[c], i, (c + d) % CHAN)

    for d in range(1, CHAN):
        square_copy(d).start()
    scaled[...] = (wide * gain[pl.ds(c * feats, feats)].reshape(1, feats)).astype(bf16)

    @pl.loop(0, PLANE)
    def _(n):
        pltpu.make_async_copy(own_tokens, tokens.at[c * PLANE + n], t_recv.at[n]).wait()

    def plane_copy(source, to, d):
        block = tokens.at[pl.ds(source * PLANE, PLANE)]
        return send(block, block, u_send.at[d], u_recv.at[source], i, to)

    for d in range(1, CHAN):
        plane_copy(c, (c + d) % CHAN, d).start()

    for load in loads[4:]:
        load.wait()
    lanes_from = pl.multiple_of((i // PLANE) * HALF, HALF)
    shift = lax.rem(HALF - place * OWN, HALF)
    decay_own, residue_own = load_own([decay, residue], lanes_from, shift)
    weight_own = residue_own * jnp.sqrt(decay_own)
    decay_row = filter_tables(decay_own, weight_own, gather, reach)
    for j in range(3):
        (rows,) = load_own([taps_all.at[j]], lanes_from, shift)
        padded = jnp.concatenate([rows, jnp.zeros((5, HALF), f32)], axis=0)
        columns = jnp.transpose(padded)[:OWN]
        for b in range(3):
            wide_column = jnp.broadcast_to(columns[:, b : b + 1], (OWN, HALF))
            for h in range(2):
                taps[h, j, b * FEW : (b + 1) * FEW, :] = wide_column[h * FEW : (h + 1) * FEW]
    skip_row = pltpu.roll(
        jnp.broadcast_to(skip_all[pl.ds(lanes_from, HALF)].reshape(1, HALF), (8, HALF)), shift, axis=1
    )
    skip_column = jnp.transpose(skip_row)[:OWN, 0:1]
    skip[...] = jnp.broadcast_to(skip_column, (OWN, SEG)).reshape(2, FEW, SEG)

    start_weights(1)

    near, far = (c // 2) * 2, 2 - (c // 2) * 2
    other = c + 1 - 2 * (c % 2)
    part_send, part_got = (part_send0, part_send1), (part_got0, part_got1)

    def part_copy(h, to, d):
        return send(part_send[h].at[to], part_got[h].at[c], p_send.at[h, d], p_recv.at[h, c], i, to)

    def products(h, first):
        top, count = WEIGHT_ROWS[h]
        weights = got_weight[pl.ds(first, 2), pl.ds(top, count), :].reshape(2 * count, feats)
        product = lax.dot_general(weights, scaled[...], NT, preferred_element_type=f32)
        return product.reshape(2, count, product.shape[1])

    def start_parts(h):
        top, count = WEIGHT_ROWS[h]
        part_send[h][pl.ds(far, 2)] = products(h, far).astype(bf16)
        part_copy(h, far, 0).start()
        part_copy(h, far + 1, 1).start()
        product = products(h, near)
        part[:, top : top + count, :] = product
        part_send[h][pl.ds(near, 2)] = product.astype(bf16)
        part_copy(h, other, 2).start()

    def finish_parts(h, scale):
        top, count = WEIGHT_ROWS[h]
        total = part[c % 2, top : top + count, :]
        for d in range(1, CHAN):
            source = (c + d) % CHAN
            send(
                part_send[h].at[0], part_got[h].at[source], p_send.at[h, d], p_recv.at[h, source], i, source
            ).wait_recv()
            total = total + part_got[h][source].astype(f32)
        table[top : top + count, :] = (total * scale).astype(bf16).astype(f32)

    def branches_of(h):
        rows = jnp.concatenate([table[top : top + FEW, :] for top in TABLE_ROWS[h]], axis=0)
        halves = jnp.concatenate([rows[:, :SEG], rows[:, SEG:]], axis=0).astype(bf16)
        short_filter_and_gate(halves, tokens, taps.at[h], carried.at[h], query.at[h])

    def out_slot(h, source):
        return got_ref.at[h, :, pl.ds(pl.multiple_of(source * OWN, OWN), OWN), :], o_recv.at[h, source]

    def out_copy(h, to):
        dst, sem = out_slot(h, i)
        return send(ready.at[h, to], dst, o_send.at[h, to], sem, to, c)

    def start_outputs(h):
        segment_states(carried.at[h], gather.at[h], decay_row[:, h * FEWS : (h + 1) * FEWS], state.at[h])

        @pl.loop(0, CTX // PLANE)
        def _(step):
            q = (plane + 1 + step) % (CTX // PLANE)
            outputs_of_part(
                q, carried.at[h], query.at[h], state.at[h], reach.at[h], skip.at[h], ready.at[h]
            )

            @pl.loop(0, PLANE)
            def _(n):
                to = q * PLANE + (place + n) % PLANE

                @pl.when(to != i)
                def _():
                    out_copy(h, to).start()

                @pl.when(to == i)
                def _():
                    pltpu.make_async_copy(ready.at[h, to], *out_slot(h, i)).start()

    wait_weights(0)
    start_parts(0)
    mean = got_square[c]
    for d in range(1, CHAN):
        source = (c + d) % CHAN
        send(got_square.at[c], got_square.at[source], s_send.at[d], s_recv.at[source], i, source).wait_recv()
        mean = mean + got_square[source]
    scale = lax.rsqrt(mean[0:1] * (1.0 / (CHAN * feats)) + EPS)
    for d in range(1, CHAN):
        plane_copy((c + d) % CHAN, c, d).wait_recv()
    finish_parts(0, scale)
    branches_of(0)
    wait_weights(1)
    start_parts(1)
    start_outputs(0)
    finish_parts(1, scale)
    branches_of(1)
    start_outputs(1)

    for h in range(2):

        @pl.loop(0, CTX)
        def _(source):
            pltpu.make_async_copy(ready.at[h, 0], *out_slot(h, source)).wait()

    for h in range(2):

        @pl.loop(1, CTX)
        def _(j):
            weight_copy(h, j).wait_send()
            out_copy(h, (i + j) % CTX).wait_send()

        part_copy(h, far, 0).wait_send()
        part_copy(h, far + 1, 1).wait_send()
        part_copy(h, other, 2).wait_send()

    @pl.when(plane != c)
    def _():
        weight_copy(0, 0).wait_send()
        weight_copy(1, 0).wait_send()
        token_copy(0).wait_send()

    @pl.loop(1, PLANE)
    def _(n):
        token_copy(n).wait_send()

    for d in range(1, CHAN):
        square_copy(d).wait_send()
        plane_copy(c, (c + d) % CHAN, d).wait_send()


def gathered(
    token_ids, embed_table, norm_gain, in_weight, short_filter, residue, decay_rate, skip_bias
):
    f32, bf16 = jnp.float32, jnp.bfloat16
    rows = token_ids.shape[0]
    vocab, feats = embed_table.shape
    chans = decay_rate.shape[1]
    weight = jnp.transpose(in_weight, (1, 0, 2))
    operands = (token_ids, embed_table, norm_gain, weight, short_filter, residue, decay_rate, skip_bias)
    dma, vmem = pltpu.SemaphoreType.DMA, pltpu.VMEM
    return pl.pallas_call(
        main_kernel,
        name="hyena",
        out_shape=jax.ShapeDtypeStruct((2, PER, CTX * OWN, HALF), bf16),
        in_specs=[pl.BlockSpec(memory_space=pl.ANY)] * len(operands),
        out_specs=pl.BlockSpec(memory_space=pl.ANY),
        scratch_shapes=[
            vmem(token_ids.shape, jnp.int32),
            vmem((1, rows), jnp.int32),
            vmem(embed_table.shape, bf16),
            vmem(norm_gain.shape, f32),
            vmem(weight.shape, bf16),
            vmem(short_filter.shape, f32),
            vmem(residue.shape, f32),
            vmem(decay_rate.shape, f32),
            vmem(skip_bias.shape, f32),
            vmem((CTX, 3 * OWN, in_weight.shape[0]), bf16),
            vmem((CHAN, 3 * OWN, feats), bf16),
            vmem((CHAN, 8, vocab), f32),
            vmem((vocab, feats), bf16),
            vmem((2, 3 * OWN, vocab), f32),
            vmem((CHAN, WEIGHT_ROWS[0][1], vocab), bf16),
            vmem((CHAN, WEIGHT_ROWS[1][1], vocab), bf16),
            vmem((CHAN, WEIGHT_ROWS[0][1], vocab), bf16),
            vmem((CHAN, WEIGHT_ROWS[1][1], vocab), bf16),
            vmem((CTX, 1, rows), jnp.int32),
            vmem((3 * OWN, vocab), f32),
            vmem((2, SEG, 2 * FEWS), bf16),
            vmem((2, FEW * SEG + 3 * FEWS, SEG), bf16),
            vmem((2, 3, 3 * FEW, HALF), f32),
            vmem((2, FEW, SEG), f32),
            vmem((2, SEGS * FEW, SEG), f32),
            vmem((2, SEGS * FEW, SEG), f32),
            vmem((2, SEGS, FEWS), f32),
            vmem((2, CTX, PER, 2 * FEW, HALF), bf16),
            dma((8,)),
            dma((2, CTX)), dma((2, CTX)), dma((PLANE,)), dma((PLANE,)),
            dma((CHAN,)), dma((CHAN,)), dma((CHAN,)), dma((CHAN,)), dma((2, CHAN)), dma((2, CHAN)),
            dma((2, CTX)), dma((2, CTX)),
        ],
        compiler_params=pltpu.CompilerParams(
            collective_id=0, has_side_effects=True, vmem_limit_bytes=VMEM_LIMIT
        ),
    )(*operands)


def turn_kernel(got_hbm, out_hbm, got, out, in_sem, out_sem):
    f32, bf16 = jnp.float32, jnp.bfloat16
    unit = (
        lax.broadcasted_iota(jnp.int32, (HALF, HALF), 0) == lax.broadcasted_iota(jnp.int32, (HALF, HALF), 1)
    ).astype(bf16)
    loads = [pltpu.make_async_copy(got_hbm.at[:, g], got.at[:, g], in_sem.at[g]) for g in range(PER)]
    stores = []
    for load in loads:
        load.start()
    for g in range(PER):
        loads[g].wait()
        eights = [got[h, g].astype(f32).reshape(CTX, 2, FEW, HALF) for h in range(2)]
        for half in range(2):
            rows = jnp.concatenate([eights[h][:, half : half + 1] for h in range(2)], axis=1)
            rows = rows.reshape(CTX * OWN, HALF).astype(bf16)
            top = g * SEG + half * HALF
            turned = lax.dot_general(unit, rows, NT, preferred_element_type=f32)
            out[top : top + HALF, :] = turned.astype(bf16)
        rows = pl.ds(g * SEG, SEG)
        stores.append(pltpu.make_async_copy(out.at[rows, :], out_hbm.at[rows, :], out_sem.at[g]))
        stores[g].start()
    for store in stores:
        store.wait()


def turned(got):
    bf16 = jnp.bfloat16
    shape = (PER * SEG, CTX * OWN)
    return pl.pallas_call(
        turn_kernel,
        name="turn",
        out_shape=jax.ShapeDtypeStruct(shape, bf16),
        in_specs=[pl.BlockSpec(memory_space=pl.ANY)],
        out_specs=pl.BlockSpec(memory_space=pl.ANY),
        scratch_shapes=[
            pltpu.VMEM(got.shape, bf16),
            pltpu.VMEM(shape, bf16),
            pltpu.SemaphoreType.DMA((PER,)),
            pltpu.SemaphoreType.DMA((PER,)),
        ],
        compiler_params=pltpu.CompilerParams(vmem_limit_bytes=VMEM_LIMIT),
    )(got)


def per_device(*arrays):
    return turned(gathered(*arrays))


def solution(mesh):
    return jax.shard_map(
        per_device,
        mesh=mesh,
        in_specs=(
            P("ctx"),
            P(None, "chan"),
            P(),
            P("ctx", None, "chan"),
            P(None, None, "chan"),
            P(None, "chan"),
            P(None, "chan"),
            P("chan"),
        ),
        out_specs=P("ctx", "chan"),
        check_vma=False,
    )
```

```python
import functools

import jax
import jax.numpy as jnp
from jax import lax
from jax.experimental import pallas as pl
from jax.experimental.pallas import tpu as pltpu
from jax.sharding import PartitionSpec as P

MESH = pl.DeviceIdType.MESH
EPS = 1e-06
VMEM_LIMIT = 60 * 1024 * 1024

CTX, CHAN, PLANE = 32, 4, 8
OWN = 16
SEG = 256
SEGS = 96
PER = 3
PART = 24
HALF = 128
MODES = 16
PAIRS = OWN * MODES
FEW = 8
FEWS = FEW * MODES
WEIGHT_ROWS = ((0, 32), (32, 16))
TABLE_ROWS = ((0, 8, 16), (32, 24, 40))
NT = (((1,), (1,)), ((), ()))
HIGHEST = lax.Precision.HIGHEST


def dot(a, b):
    return jnp.dot(a, b, preferred_element_type=jnp.float32)


def high_low(x):
    high = x.astype(jnp.bfloat16)
    return high, (x - high.astype(jnp.float32)).astype(jnp.bfloat16)


def send(src, dst, send_sem, recv_sem, i, c):
    return pltpu.make_async_remote_copy(
        src_ref=src, dst_ref=dst, send_sem=send_sem, recv_sem=recv_sem, device_id=(i, c), device_id_type=MESH
    )


def load_own(row_refs, lanes_from, shift):
    rows = [ref[:, pl.ds(lanes_from, HALF)] for ref in row_refs]
    return [pltpu.roll(array, shift, axis=1) for array in rows]


def filter_tables(decay, weight, gather, reach):
    f32, bf16 = jnp.float32, jnp.bfloat16
    decay_turned = jnp.transpose(decay)[:OWN]
    weight_turned = jnp.transpose(weight)[:OWN]
    lane = lax.broadcasted_iota(jnp.int32, (OWN, HALF), 1).astype(f32)
    near = jnp.zeros((OWN, HALF), f32)
    far = jnp.zeros((OWN, HALF), f32)
    for m in range(MODES):
        rate = jnp.broadcast_to(decay_turned[:, m : m + 1], (OWN, HALF))
        height = jnp.broadcast_to(weight_turned[:, m : m + 1], (OWN, HALF))
        near = near + height * jnp.exp(-rate * lane)
        far = far + height * jnp.exp(-rate * (lane + float(HALF)))
    causal = lax.broadcasted_iota(jnp.int32, (HALF, HALF), 1) >= lax.broadcasted_iota(jnp.int32, (HALF, HALF), 0)
    for ch in range(OWN):
        near_rolled = pltpu.roll(
            jnp.broadcast_to(near[ch : ch + 1], (HALF, HALF)), 0, axis=1, stride=1, stride_axis=0
        )
        far_rolled = pltpu.roll(
            jnp.broadcast_to(far[ch : ch + 1], (HALF, HALF)), 0, axis=1, stride=1, stride_axis=0
        )
        diagonal = jnp.where(causal, near_rolled, 0.0).astype(bf16)
        part, top = ch // FEW, ch % FEW * SEG
        middle, end = top + HALF, top + SEG
        reach[part, top:middle, :HALF] = diagonal
        reach[part, middle:end, HALF:] = diagonal
        reach[part, top:middle, HALF:] = jnp.where(causal, far_rolled, near_rolled).astype(bf16)
        reach[part, middle:end, :HALF] = jnp.zeros((HALF, HALF), bf16)

    pick = (
        lax.broadcasted_iota(jnp.int32, (HALF, PAIRS), 0)
        == lax.broadcasted_iota(jnp.int32, (HALF, PAIRS), 1) // MODES
    ).astype(f32)
    own_mode = (
        lax.broadcasted_iota(jnp.int32, (MODES, PAIRS), 0)
        == lax.broadcasted_iota(jnp.int32, (MODES, PAIRS), 1) % MODES
    )

    def pair_row(array):
        wide = jnp.dot(array, pick, precision=HIGHEST, preferred_element_type=f32)
        return jnp.sum(jnp.where(own_mode, wide, 0.0), axis=0, keepdims=True)

    decay_row = pair_row(decay)
    decay_column = jnp.transpose(jnp.broadcast_to(decay_row, (HALF, PAIRS)))
    weight_column = jnp.transpose(jnp.broadcast_to(pair_row(weight), (HALF, PAIRS)))
    to_end = (SEG - 1 - lax.broadcasted_iota(jnp.int32, (SEG, PAIRS), 0)).astype(f32)
    entering = high_low(jnp.exp(-decay_row * to_end))
    for part in range(2):
        for n in range(2):
            gather[part, :, n * FEWS : (n + 1) * FEWS] = entering[n][:, part * FEWS : (part + 1) * FEWS]
    for half in range(2):
        lanes = slice(half * HALF, (half + 1) * HALF)
        after = lax.broadcasted_iota(jnp.int32, (PAIRS, HALF), 1).astype(f32) + float(half * HALF + 1)
        high, low = high_low(weight_column * jnp.exp(-decay_column * after))
        for part in range(2):
            rows = slice(part * FEWS, (part + 1) * FEWS)
            for n, piece in enumerate((high, high, low)):
                top = FEW * SEG + n * FEWS
                reach[part, top : top + FEWS, lanes] = piece[rows]
    return decay_row


def short_filter_and_gate(table, tokens_ref, taps_ref, carried_ref, query_ref):
    f32, bf16 = jnp.float32, jnp.bfloat16
    rows = 3 * FEW
    entry = lax.broadcasted_iota(jnp.int32, (SEG, SEG), 0).astype(f32).astype(bf16)
    lane = lax.broadcasted_iota(jnp.int32, (rows, HALF), 1)
    one, zero = jnp.ones((), bf16), jnp.zeros((), bf16)

    def block(g, before):
        for part in range(PER):
            ids = tokens_ref[g, :, part * SEG : (part + 1) * SEG]
            chosen = (ids & (SEG - 1)).astype(f32).astype(bf16)
            both = dot(table, jnp.where(entry == chosen, one, zero))
            projected = jnp.where(ids >= SEG, both[rows:], both[:rows])
            at = pl.ds(pl.multiple_of((g * PER + part) * FEW, FEW), FEW)
            for half in range(2):
                lanes = slice(half * HALF, (half + 1) * HALF)
                here = projected[:, lanes]
                turned = (pltpu.roll(here, 1, axis=1), pltpu.roll(here, 2, axis=1))
                branches = (
                    taps_ref[0] * here
                    + taps_ref[1] * jnp.where(lane < 1, before[0], turned[0])
                    + taps_ref[2] * jnp.where(lane < 2, before[1], turned[1])
                )
                before = turned
                carried = branches[FEW : 2 * FEW] * branches[2 * FEW :]
                carried_ref[at, lanes] = carried.astype(bf16).astype(f32)
                query_ref[at, lanes] = branches[:FEW]
        return before

    nothing = jnp.zeros((rows, HALF), f32)
    lax.fori_loop(0, SEGS // PER, block, (nothing, nothing), unroll=UNROLL)


UNROLL = 16


def own_pairs():
    shape = (1, FEW, FEWS)
    return lax.broadcasted_iota(jnp.int32, shape, 2) // MODES == lax.broadcasted_iota(jnp.int32, shape, 1)


def segment_states(carried_ref, gather, decay_row, state_ref):
    f32, bf16 = jnp.float32, jnp.bfloat16
    enters = dot(carried_ref[...].astype(bf16), gather[...])
    enters = (enters[:, :FEWS] + enters[:, FEWS:]).reshape(SEGS, FEW, FEWS)
    added = jnp.sum(jnp.where(own_pairs(), enters, 0.0), axis=1)

    def later(x, by):
        return jnp.concatenate([jnp.zeros((by, FEWS), f32), x[: SEGS - by]], axis=0)

    state = later(added, 1)
    by = 1
    while by < SEGS:
        state = state + jnp.exp(-decay_row * float(SEG * by)) * later(state, by)
        by *= 2
    state_ref[...] = state


def outputs_of_part(q, carried_ref, query_ref, state_ref, reach, skip_ref, ready):
    f32, bf16 = jnp.float32, jnp.bfloat16
    first = pl.multiple_of(q * PART, PART)
    rows = pl.ds(pl.multiple_of(first * FEW, FEW), PART * FEW)
    carried = carried_ref[rows, :].reshape(PART, FEW, SEG)
    channel = lax.broadcasted_iota(jnp.int32, (1, FEW, SEG), 1)
    parts = [
        jnp.where(channel == ch, carried, 0.0).reshape(PART * FEW, SEG).astype(bf16) for ch in range(FEW)
    ]
    state = jnp.where(own_pairs(), state_ref[pl.ds(first, PART), :][:, None, :], 0.0)
    high, low = high_low(state.reshape(PART * FEW, FEWS))
    conv = dot(jnp.concatenate(parts + [high, low, high], axis=1), reach[...])
    gated = query_ref[rows, :] * (conv + (skip_ref[...][None] * carried).reshape(PART * FEW, SEG))
    halves = [gated[:, half * HALF : (half + 1) * HALF].reshape(PART, 1, FEW, HALF) for half in range(2)]
    block = jnp.concatenate(halves, axis=1).reshape(PLANE, PER, 2 * FEW, HALF)
    ready[pl.ds(q * PLANE, PLANE)] = block.astype(bf16)


def main_kernel(
    tok_hbm, embed_hbm, gain_hbm, weight_hbm, taps_hbm, residue_hbm, decay_hbm, skip_hbm, got_ref,
    tok, own_tokens, embed, gain, weight, taps_all, residue, decay, skip_all,
    turned_weight, got_weight, got_square, scaled, part, part_send0, part_send1, part_got0, part_got1, tokens, table,
    gather, reach, taps, skip, carried, query, state, ready,
    in_sem, w_send, w_recv, t_send, t_recv, u_send, u_recv, s_send, s_recv, p_send, p_recv, o_send, o_recv,
):
    f32, bf16 = jnp.float32, jnp.bfloat16
    i, c = lax.axis_index("ctx"), lax.axis_index("chan")
    plane, place = i // PLANE, i % PLANE

    loads = [
        pltpu.make_async_copy(src, dst, in_sem.at[n])
        for n, (src, dst) in enumerate(
            (
                (weight_hbm, weight), (tok_hbm, tok), (embed_hbm, embed), (gain_hbm, gain),
                (taps_hbm, taps_all), (residue_hbm, residue), (decay_hbm, decay), (skip_hbm, skip_all),
            )
        )
    ]
    for load in loads:
        load.start()

    barrier = pltpu.get_barrier_semaphore()

    @pl.loop(0, CTX)
    def _(j):
        row, col = c * PLANE + j % PLANE, j // PLANE

        @pl.when(jnp.logical_or(row != i, col != c))
        def _():
            pl.semaphore_signal(barrier, inc=1, device_id=(row, col), device_id_type=MESH)

    for d in range(1, CHAN):
        pl.semaphore_signal(barrier, inc=1, device_id=(i, (c + d) % CHAN), device_id_type=MESH)

    loads[0].wait()
    eights = [jnp.transpose(weight[b].astype(f32)).reshape(CTX, 2, FEW, HALF) for b in range(3)]
    order = ((0, 0), (1, 0), (2, 0), (1, 1), (0, 1), (2, 1))
    rows = jnp.concatenate([eights[b][:, part : part + 1] for b, part in order], axis=1)
    turned_weight[...] = rows.reshape(turned_weight.shape).astype(bf16)
    loads[1].wait()
    own_tokens[...] = tok[...].reshape(1, tok.shape[0])

    pl.semaphore_wait(barrier, CTX - jnp.where(plane == c, 1, 0) + CHAN - 1)

    def weight_slices(h, to, slot):
        rows = pl.ds(*WEIGHT_ROWS[h])
        lanes = pl.ds(pl.multiple_of(slot % PLANE * HALF, HALF), HALF)
        return turned_weight.at[to, rows, :], got_weight.at[slot // PLANE, rows, lanes], w_recv.at[h]

    def weight_copy(h, j):
        to = (i + j) % CTX
        src, dst, sem = weight_slices(h, to, c * PLANE + place)
        return send(src, dst, w_send.at[h], sem, to, plane)

    def start_weights(h):
        @pl.loop(1, CTX)
        def _(j):
            weight_copy(h, j).start()

        @pl.when(plane == c)
        def _():
            pltpu.make_async_copy(*weight_slices(h, i, c * PLANE + place)).start()

        @pl.when(plane != c)
        def _():
            weight_copy(h, 0).start()

    def wait_for(region, sem):
        pltpu.make_async_copy(region, region, sem).wait()

    def wait_weights(h):
        wait_for(got_weight.at[:, pl.ds(*WEIGHT_ROWS[h]), :], w_recv.at[h])

    def token_copy(n):
        to = c * PLANE + (place + n) % PLANE
        return send(own_tokens, tokens.at[i], t_send, t_recv, to, plane)

    start_weights(0)
    own_token_copy = pltpu.make_async_copy(own_tokens, tokens.at[i], t_recv)

    @pl.when(plane == c)
    def _():
        own_token_copy.start()

    @pl.when(plane != c)
    def _():
        token_copy(0).start()

    @pl.loop(1, PLANE)
    def _(n):
        token_copy(n).start()

    start_weights(1)

    loads[2].wait()
    loads[3].wait()
    wide = embed[...].astype(f32)
    feats = embed.shape[1]
    square_high, square_low = high_low(wide * wide)
    ones = jnp.ones((8, feats), bf16)
    squares = lax.dot_general(ones, square_high, NT, preferred_element_type=f32)
    got_square[c] = squares + lax.dot_general(ones, square_low, NT, preferred_element_type=f32)

    def square_copy(d):
        return send(got_square.at[c], got_square.at[c], s_send.at[d], s_recv.at[c], i, (c + d) % CHAN)

    for d in range(1, CHAN):
        square_copy(d).start()
    scaled[...] = (wide * gain[pl.ds(c * feats, feats)].reshape(1, feats)).astype(bf16)

    wait_for(tokens.at[pl.ds(c * PLANE, PLANE)], t_recv)

    def plane_copy(source, to, d):
        block = tokens.at[pl.ds(source * PLANE, PLANE)]
        return send(block, block, u_send.at[d], u_recv.at[source], i, to)

    for d in range(1, CHAN):
        plane_copy(c, (c + d) % CHAN, d).start()

    near, far = (c // 2) * 2, 2 - (c // 2) * 2
    other = c + 1 - 2 * (c % 2)
    part_send, part_got = (part_send0, part_send1), (part_got0, part_got1)

    def part_copy(h, to, d):
        return send(part_send[h].at[to], part_got[h].at[c], p_send.at[h, d], p_recv.at[h, c], i, to)

    def products(h, first):
        top, count = WEIGHT_ROWS[h]
        weights = got_weight[pl.ds(first, 2), pl.ds(top, count), :].reshape(2 * count, feats)
        product = lax.dot_general(weights, scaled[...], NT, preferred_element_type=f32)
        return product.reshape(2, count, product.shape[1])

    def start_parts(h):
        top, count = WEIGHT_ROWS[h]
        part_send[h][pl.ds(far, 2)] = products(h, far).astype(bf16)
        part_copy(h, far, 0).start()
        part_copy(h, far + 1, 1).start()
        product = products(h, near)
        part[:, top : top + count, :] = product
        part_send[h][pl.ds(near, 2)] = product.astype(bf16)
        part_copy(h, other, 2).start()

    def finish_parts(h, scale):
        top, count = WEIGHT_ROWS[h]
        total = part[c % 2, top : top + count, :]
        for d in range(1, CHAN):
            source = (c + d) % CHAN
            send(
                part_send[h].at[0], part_got[h].at[source], p_send.at[h, d], p_recv.at[h, source], i, source
            ).wait_recv()
            total = total + part_got[h][source].astype(f32)
        table[top : top + count, :] = (total * scale).astype(bf16).astype(f32)

    def branches_of(h):
        rows = jnp.concatenate([table[top : top + FEW, :] for top in TABLE_ROWS[h]], axis=0)
        halves = jnp.concatenate([rows[:, :SEG], rows[:, SEG:]], axis=0).astype(bf16)
        short_filter_and_gate(halves, tokens, taps.at[h], carried.at[h], query.at[h])

    def out_slot(h, source):
        return got_ref.at[h, :, pl.ds(pl.multiple_of(source * OWN, OWN), OWN), :], o_recv.at[h]

    def out_copy(h, to):
        dst, sem = out_slot(h, i)
        return send(ready.at[h, to], dst, o_send.at[h], sem, to, c)

    def start_outputs(h, decay_row):
        segment_states(carried.at[h], gather.at[h], decay_row[:, h * FEWS : (h + 1) * FEWS], state.at[h])

        @pl.loop(0, CTX // PLANE)
        def _(step):
            q = (plane + 1 + step) % (CTX // PLANE)
            outputs_of_part(
                q, carried.at[h], query.at[h], state.at[h], reach.at[h], skip.at[h], ready.at[h]
            )

            @pl.loop(0, PLANE)
            def _(n):
                to = q * PLANE + (place + n) % PLANE

                @pl.when(to != i)
                def _():
                    out_copy(h, to).start()

                @pl.when(to == i)
                def _():
                    pltpu.make_async_copy(ready.at[h, to], *out_slot(h, i)).start()

    wait_weights(0)
    start_parts(0)

    for load in loads[4:]:
        load.wait()
    lanes_from = pl.multiple_of((i // PLANE) * HALF, HALF)
    shift = lax.rem(HALF - place * OWN, HALF)
    decay_own, residue_own = load_own([decay, residue], lanes_from, shift)
    weight_own = residue_own * jnp.sqrt(decay_own)
    decay_row = filter_tables(decay_own, weight_own, gather, reach)
    for j in range(3):
        (rows,) = load_own([taps_all.at[j]], lanes_from, shift)
        padded = jnp.concatenate([rows, jnp.zeros((5, HALF), f32)], axis=0)
        columns = jnp.transpose(padded)[:OWN]
        for b in range(3):
            wide_column = jnp.broadcast_to(columns[:, b : b + 1], (OWN, HALF))
            for h in range(2):
                taps[h, j, b * FEW : (b + 1) * FEW, :] = wide_column[h * FEW : (h + 1) * FEW]
    skip_row = pltpu.roll(
        jnp.broadcast_to(skip_all[pl.ds(lanes_from, HALF)].reshape(1, HALF), (8, HALF)), shift, axis=1
    )
    skip_column = jnp.transpose(skip_row)[:OWN, 0:1]
    skip[...] = jnp.broadcast_to(skip_column, (OWN, SEG)).reshape(2, FEW, SEG)

    wait_weights(1)
    start_parts(1)
    mean = got_square[c]
    for d in range(1, CHAN):
        source = (c + d) % CHAN
        send(got_square.at[c], got_square.at[source], s_send.at[d], s_recv.at[source], i, source).wait_recv()
        mean = mean + got_square[source]
    scale = lax.rsqrt(mean[0:1] * (1.0 / (CHAN * feats)) + EPS)
    for d in range(1, CHAN):
        plane_copy((c + d) % CHAN, c, d).wait_recv()
    finish_parts(0, scale)
    branches_of(0)
    start_outputs(0, decay_row)
    finish_parts(1, scale)
    branches_of(1)
    start_outputs(1, decay_row)

    for h in range(2):
        wait_for(ready.at[h, pl.ds(0, CTX - 1)], o_send.at[h])
        part_copy(h, far, 0).wait_send()
        part_copy(h, far + 1, 1).wait_send()
        part_copy(h, other, 2).wait_send()

    def wait_sends(skipped):
        for h in range(2):
            rows = pl.ds(*WEIGHT_ROWS[h])
            wait_for(turned_weight.at[pl.ds(0, CTX - skipped), rows, :], w_send.at[h])
        wait_for(tokens.at[pl.ds(0, PLANE - skipped)], t_send)

    @pl.when(plane != c)
    def _():
        wait_sends(0)

    @pl.when(plane == c)
    def _():
        wait_sends(1)

    for d in range(1, CHAN):
        square_copy(d).wait_send()
        plane_copy(c, (c + d) % CHAN, d).wait_send()
    for h in range(2):
        wait_for(got_ref.at[h], o_recv.at[h])


def gathered(
    token_ids, embed_table, norm_gain, in_weight, short_filter, residue, decay_rate, skip_bias
):
    f32, bf16 = jnp.float32, jnp.bfloat16
    rows = token_ids.shape[0]
    vocab, feats = embed_table.shape
    chans = decay_rate.shape[1]
    weight = jnp.transpose(in_weight, (1, 0, 2))
    operands = (token_ids, embed_table, norm_gain, weight, short_filter, residue, decay_rate, skip_bias)
    dma, vmem = pltpu.SemaphoreType.DMA, pltpu.VMEM
    return pl.pallas_call(
        main_kernel,
        name="hyena",
        out_shape=jax.ShapeDtypeStruct((2, PER, CTX * OWN, HALF), bf16),
        in_specs=[pl.BlockSpec(memory_space=pl.ANY)] * len(operands),
        out_specs=pl.BlockSpec(memory_space=pl.ANY),
        scratch_shapes=[
            vmem(token_ids.shape, jnp.int32),
            vmem((1, rows), jnp.int32),
            vmem(embed_table.shape, bf16),
            vmem(norm_gain.shape, f32),
            vmem(weight.shape, bf16),
            vmem(short_filter.shape, f32),
            vmem(residue.shape, f32),
            vmem(decay_rate.shape, f32),
            vmem(skip_bias.shape, f32),
            vmem((CTX, 3 * OWN, in_weight.shape[0]), bf16),
            vmem((CHAN, 3 * OWN, feats), bf16),
            vmem((CHAN, 8, vocab), f32),
            vmem((vocab, feats), bf16),
            vmem((2, 3 * OWN, vocab), f32),
            vmem((CHAN, WEIGHT_ROWS[0][1], vocab), bf16),
            vmem((CHAN, WEIGHT_ROWS[1][1], vocab), bf16),
            vmem((CHAN, WEIGHT_ROWS[0][1], vocab), bf16),
            vmem((CHAN, WEIGHT_ROWS[1][1], vocab), bf16),
            vmem((CTX, 1, rows), jnp.int32),
            vmem((3 * OWN, vocab), f32),
            vmem((2, SEG, 2 * FEWS), bf16),
            vmem((2, FEW * SEG + 3 * FEWS, SEG), bf16),
            vmem((2, 3, 3 * FEW, HALF), f32),
            vmem((2, FEW, SEG), f32),
            vmem((2, SEGS * FEW, SEG), f32),
            vmem((2, SEGS * FEW, SEG), f32),
            vmem((2, SEGS, FEWS), f32),
            vmem((2, CTX, PER, 2 * FEW, HALF), bf16),
            dma((8,)),
            dma((2,)), dma((2,)), dma(()), dma(()),
            dma((CHAN,)), dma((CHAN,)), dma((CHAN,)), dma((CHAN,)), dma((2, CHAN)), dma((2, CHAN)),
            dma((2,)), dma((2,)),
        ],
        compiler_params=pltpu.CompilerParams(
            collective_id=0, has_side_effects=True, vmem_limit_bytes=VMEM_LIMIT
        ),
    )(*operands)


def turn_kernel(got_hbm, out_hbm, got, out, in_sem, out_sem):
    f32, bf16 = jnp.float32, jnp.bfloat16
    unit = (
        lax.broadcasted_iota(jnp.int32, (HALF, HALF), 0) == lax.broadcasted_iota(jnp.int32, (HALF, HALF), 1)
    ).astype(bf16)
    loads = [pltpu.make_async_copy(got_hbm.at[:, g], got.at[:, g], in_sem.at[g]) for g in range(PER)]
    stores = []
    for load in loads:
        load.start()
    for g in range(PER):
        loads[g].wait()
        eights = [got[h, g].astype(f32).reshape(CTX, 2, FEW, HALF) for h in range(2)]
        for half in range(2):
            rows = jnp.concatenate([eights[h][:, half : half + 1] for h in range(2)], axis=1)
            rows = rows.reshape(CTX * OWN, HALF).astype(bf16)
            top = g * SEG + half * HALF
            turned = lax.dot_general(unit, rows, NT, preferred_element_type=f32)
            out[top : top + HALF, :] = turned.astype(bf16)
        rows = pl.ds(g * SEG, SEG)
        stores.append(pltpu.make_async_copy(out.at[rows, :], out_hbm.at[rows, :], out_sem.at[g]))
        stores[g].start()
    for store in stores:
        store.wait()


def turned(got):
    bf16 = jnp.bfloat16
    shape = (PER * SEG, CTX * OWN)
    return pl.pallas_call(
        turn_kernel,
        name="turn",
        out_shape=jax.ShapeDtypeStruct(shape, bf16),
        in_specs=[pl.BlockSpec(memory_space=pl.ANY)],
        out_specs=pl.BlockSpec(memory_space=pl.ANY),
        scratch_shapes=[
            pltpu.VMEM(got.shape, bf16),
            pltpu.VMEM(shape, bf16),
            pltpu.SemaphoreType.DMA((PER,)),
            pltpu.SemaphoreType.DMA((PER,)),
        ],
        compiler_params=pltpu.CompilerParams(vmem_limit_bytes=VMEM_LIMIT),
    )(got)


def per_device(*arrays):
    return turned(gathered(*arrays))


def solution(mesh):
    return jax.shard_map(
        per_device,
        mesh=mesh,
        in_specs=(
            P("ctx"),
            P(None, "chan"),
            P(),
            P("ctx", None, "chan"),
            P(None, None, "chan"),
            P(None, "chan"),
            P(None, "chan"),
            P("chan"),
        ),
        out_specs=P("ctx", "chan"),
        check_vma=False,
    )
```

```python
import functools

import jax
import jax.numpy as jnp
from jax import lax
from jax.experimental import pallas as pl
from jax.experimental.pallas import tpu as pltpu
from jax.sharding import PartitionSpec as P

MESH = pl.DeviceIdType.MESH
EPS = 1e-06
VMEM_LIMIT = 56 * 1024 * 1024
TURN_LIMIT = 16 * 1024 * 1024

CTX, CHAN, PLANE = 32, 4, 8
OWN = 16
SEG = 256
SEGS = 96
PER = 3
PART = 24
HALF = 128
MODES = 16
PAIRS = OWN * MODES
FEW = 8
FEWS = FEW * MODES
WEIGHT_ROWS = ((0, 32), (32, 16))
TABLE_ROWS = ((0, 8, 16), (32, 24, 40))
NT = (((1,), (1,)), ((), ()))
HIGHEST = lax.Precision.HIGHEST


def dot(a, b):
    return jnp.dot(a, b, preferred_element_type=jnp.float32)


def high_low(x):
    high = x.astype(jnp.bfloat16)
    return high, (x - high.astype(jnp.float32)).astype(jnp.bfloat16)


def send(src, dst, send_sem, recv_sem, i, c):
    return pltpu.make_async_remote_copy(
        src_ref=src, dst_ref=dst, send_sem=send_sem, recv_sem=recv_sem, device_id=(i, c), device_id_type=MESH
    )


def load_own(row_refs, lanes_from, shift):
    rows = [ref[:, pl.ds(lanes_from, HALF)] for ref in row_refs]
    return [pltpu.roll(array, shift, axis=1) for array in rows]


def filter_tables(decay, weight, gather, reach):
    f32, bf16 = jnp.float32, jnp.bfloat16
    decay_turned = jnp.transpose(decay)[:OWN]
    weight_turned = jnp.transpose(weight)[:OWN]
    lane = lax.broadcasted_iota(jnp.int32, (OWN, HALF), 1).astype(f32)
    near = jnp.zeros((OWN, HALF), f32)
    far = jnp.zeros((OWN, HALF), f32)
    for m in range(MODES):
        rate = jnp.broadcast_to(decay_turned[:, m : m + 1], (OWN, HALF))
        height = jnp.broadcast_to(weight_turned[:, m : m + 1], (OWN, HALF))
        near = near + height * jnp.exp(-rate * lane)
        far = far + height * jnp.exp(-rate * (lane + float(HALF)))
    causal = lax.broadcasted_iota(jnp.int32, (HALF, HALF), 1) >= lax.broadcasted_iota(jnp.int32, (HALF, HALF), 0)
    for ch in range(OWN):
        near_rolled = pltpu.roll(
            jnp.broadcast_to(near[ch : ch + 1], (HALF, HALF)), 0, axis=1, stride=1, stride_axis=0
        )
        far_rolled = pltpu.roll(
            jnp.broadcast_to(far[ch : ch + 1], (HALF, HALF)), 0, axis=1, stride=1, stride_axis=0
        )
        diagonal = jnp.where(causal, near_rolled, 0.0).astype(bf16)
        part, top = ch // FEW, ch % FEW * SEG
        middle, end = top + HALF, top + SEG
        reach[part, top:middle, :HALF] = diagonal
        reach[part, middle:end, HALF:] = diagonal
        reach[part, top:middle, HALF:] = jnp.where(causal, far_rolled, near_rolled).astype(bf16)
        reach[part, middle:end, :HALF] = jnp.zeros((HALF, HALF), bf16)

    pick = (
        lax.broadcasted_iota(jnp.int32, (HALF, PAIRS), 0)
        == lax.broadcasted_iota(jnp.int32, (HALF, PAIRS), 1) // MODES
    ).astype(f32)
    own_mode = (
        lax.broadcasted_iota(jnp.int32, (MODES, PAIRS), 0)
        == lax.broadcasted_iota(jnp.int32, (MODES, PAIRS), 1) % MODES
    )

    def pair_row(array):
        wide = jnp.dot(array, pick, precision=HIGHEST, preferred_element_type=f32)
        return jnp.sum(jnp.where(own_mode, wide, 0.0), axis=0, keepdims=True)

    decay_row = pair_row(decay)
    decay_column = jnp.transpose(jnp.broadcast_to(decay_row, (HALF, PAIRS)))
    weight_column = jnp.transpose(jnp.broadcast_to(pair_row(weight), (HALF, PAIRS)))
    to_end = (SEG - 1 - lax.broadcasted_iota(jnp.int32, (SEG, PAIRS), 0)).astype(f32)
    entering = high_low(jnp.exp(-decay_row * to_end))
    for part in range(2):
        for n in range(2):
            gather[part, :, n * FEWS : (n + 1) * FEWS] = entering[n][:, part * FEWS : (part + 1) * FEWS]
    for half in range(2):
        lanes = slice(half * HALF, (half + 1) * HALF)
        after = lax.broadcasted_iota(jnp.int32, (PAIRS, HALF), 1).astype(f32) + float(half * HALF + 1)
        high, low = high_low(weight_column * jnp.exp(-decay_column * after))
        for part in range(2):
            rows = slice(part * FEWS, (part + 1) * FEWS)
            for n, piece in enumerate((high, high, low)):
                top = FEW * SEG + n * FEWS
                reach[part, top : top + FEWS, lanes] = piece[rows]
    return decay_row


def short_filter_and_gate(table, tokens_ref, taps_ref, carried_ref, query_ref):
    f32, bf16 = jnp.float32, jnp.bfloat16
    rows = 3 * FEW
    entry = lax.broadcasted_iota(jnp.int32, (SEG, SEG), 0).astype(f32).astype(bf16)
    lane = lax.broadcasted_iota(jnp.int32, (rows, HALF), 1)
    one, zero = jnp.ones((), bf16), jnp.zeros((), bf16)

    def block(g, before):
        for part in range(PER):
            ids = tokens_ref[g, :, part * SEG : (part + 1) * SEG]
            chosen = (ids & (SEG - 1)).astype(f32).astype(bf16)
            both = dot(table, jnp.where(entry == chosen, one, zero))
            projected = jnp.where(ids >= SEG, both[rows:], both[:rows])
            at = pl.ds(pl.multiple_of((g * PER + part) * FEW, FEW), FEW)
            for half in range(2):
                lanes = slice(half * HALF, (half + 1) * HALF)
                here = projected[:, lanes]
                turned = (pltpu.roll(here, 1, axis=1), pltpu.roll(here, 2, axis=1))
                branches = (
                    taps_ref[0] * here
                    + taps_ref[1] * jnp.where(lane < 1, before[0], turned[0])
                    + taps_ref[2] * jnp.where(lane < 2, before[1], turned[1])
                )
                before = turned
                carried = branches[FEW : 2 * FEW] * branches[2 * FEW :]
                carried_ref[at, lanes] = carried.astype(bf16).astype(f32)
                query_ref[at, lanes] = branches[:FEW]
        return before

    nothing = jnp.zeros((rows, HALF), f32)
    lax.fori_loop(0, SEGS // PER, block, (nothing, nothing), unroll=UNROLL)


UNROLL = 16


def own_pairs():
    shape = (1, FEW, FEWS)
    return lax.broadcasted_iota(jnp.int32, shape, 2) // MODES == lax.broadcasted_iota(jnp.int32, shape, 1)


def segment_states(carried_ref, gather, decay_row, state_ref):
    f32, bf16 = jnp.float32, jnp.bfloat16
    enters = dot(carried_ref[...].astype(bf16), gather[...])
    enters = (enters[:, :FEWS] + enters[:, FEWS:]).reshape(SEGS, FEW, FEWS)
    added = jnp.sum(jnp.where(own_pairs(), enters, 0.0), axis=1)

    def later(x, by):
        return jnp.concatenate([jnp.zeros((by, FEWS), f32), x[: SEGS - by]], axis=0)

    state = later(added, 1)
    by = 1
    while by < SEGS:
        state = state + jnp.exp(-decay_row * float(SEG * by)) * later(state, by)
        by *= 2
    state_ref[...] = state


def outputs_of_part(q, carried_ref, query_ref, state_ref, reach, skip_ref, ready):
    f32, bf16 = jnp.float32, jnp.bfloat16
    first = pl.multiple_of(q * PART, PART)
    rows = pl.ds(pl.multiple_of(first * FEW, FEW), PART * FEW)
    carried = carried_ref[rows, :].reshape(PART, FEW, SEG)
    channel = lax.broadcasted_iota(jnp.int32, (1, FEW, SEG), 1)
    parts = [
        jnp.where(channel == ch, carried, 0.0).reshape(PART * FEW, SEG).astype(bf16) for ch in range(FEW)
    ]
    state = jnp.where(own_pairs(), state_ref[pl.ds(first, PART), :][:, None, :], 0.0)
    high, low = high_low(state.reshape(PART * FEW, FEWS))
    conv = dot(jnp.concatenate(parts + [high, low, high], axis=1), reach[...])
    gated = query_ref[rows, :] * (conv + (skip_ref[...][None] * carried).reshape(PART * FEW, SEG))
    halves = [gated[:, half * HALF : (half + 1) * HALF].reshape(PART, 1, FEW, HALF) for half in range(2)]
    block = jnp.concatenate(halves, axis=1).reshape(PLANE, PER, 2 * FEW, HALF)
    ready[pl.ds(q * PLANE, PLANE)] = block.astype(bf16)


def main_kernel(
    tok_hbm, embed_hbm, gain_hbm, weight_hbm, taps_hbm, residue_hbm, decay_hbm, skip_hbm, got_ref,
    tok, own_tokens, embed, gain, weight, taps_all, residue, decay, skip_all,
    turned_weight, got_weight, got_square, scaled, part, part_send0, part_send1, part_got0, part_got1, tokens, table,
    gather, reach, taps, skip, carried, query, state, ready,
    in_sem, w_send, w_recv, t_send, t_recv, u_send, u_recv, s_send, s_recv, p_send, p_recv, o_send, o_recv,
):
    f32, bf16 = jnp.float32, jnp.bfloat16
    i, c = lax.axis_index("ctx"), lax.axis_index("chan")
    plane, place = i // PLANE, i % PLANE

    loads = [
        pltpu.make_async_copy(src, dst, in_sem.at[n])
        for n, (src, dst) in enumerate(
            (
                (weight_hbm, weight), (tok_hbm, tok), (embed_hbm, embed), (gain_hbm, gain),
                (taps_hbm, taps_all), (residue_hbm, residue), (decay_hbm, decay), (skip_hbm, skip_all),
            )
        )
    ]
    for load in loads:
        load.start()

    barrier = pltpu.get_barrier_semaphore()

    @pl.loop(0, CTX)
    def _(j):
        row, col = c * PLANE + j % PLANE, j // PLANE

        @pl.when(jnp.logical_or(row != i, col != c))
        def _():
            pl.semaphore_signal(barrier, inc=1, device_id=(row, col), device_id_type=MESH)

    for d in range(1, CHAN):
        pl.semaphore_signal(barrier, inc=1, device_id=(i, (c + d) % CHAN), device_id_type=MESH)

    loads[0].wait()
    eights = [jnp.transpose(weight[b].astype(f32)).reshape(CTX, 2, FEW, HALF) for b in range(3)]
    order = ((0, 0), (1, 0), (2, 0), (1, 1), (0, 1), (2, 1))
    rows = jnp.concatenate([eights[b][:, part : part + 1] for b, part in order], axis=1)
    turned_weight[...] = rows.reshape(turned_weight.shape).astype(bf16)
    loads[1].wait()
    own_tokens[...] = tok[...].reshape(1, tok.shape[0])

    pl.semaphore_wait(barrier, CTX - jnp.where(plane == c, 1, 0) + CHAN - 1)

    def weight_slices(h, to, slot):
        rows = pl.ds(*WEIGHT_ROWS[h])
        lanes = pl.ds(pl.multiple_of(slot % PLANE * HALF, HALF), HALF)
        return turned_weight.at[to, rows, :], got_weight.at[slot // PLANE, rows, lanes], w_recv.at[h]

    def weight_copy(h, j):
        to = (i + j) % CTX
        src, dst, sem = weight_slices(h, to, c * PLANE + place)
        return send(src, dst, w_send.at[h], sem, to, plane)

    def start_weights(h):
        @pl.loop(1, CTX)
        def _(j):
            weight_copy(h, j).start()

        @pl.when(plane == c)
        def _():
            pltpu.make_async_copy(*weight_slices(h, i, c * PLANE + place)).start()

        @pl.when(plane != c)
        def _():
            weight_copy(h, 0).start()

    def wait_for(region, sem):
        pltpu.make_async_copy(region, region, sem).wait()

    def wait_weights(h):
        wait_for(got_weight.at[:, pl.ds(*WEIGHT_ROWS[h]), :], w_recv.at[h])

    def token_copy(n):
        to = c * PLANE + (place + n) % PLANE
        return send(own_tokens, tokens.at[i], t_send, t_recv, to, plane)

    own_token_copy = pltpu.make_async_copy(own_tokens, tokens.at[i], t_recv)

    @pl.when(plane == c)
    def _():
        own_token_copy.start()

    @pl.when(plane != c)
    def _():
        token_copy(0).start()

    @pl.loop(1, PLANE)
    def _(n):
        token_copy(n).start()

    start_weights(0)

    loads[2].wait()
    loads[3].wait()
    wide = embed[...].astype(f32)
    feats = embed.shape[1]
    square_high, square_low = high_low(wide * wide)
    ones = jnp.ones((8, feats), bf16)
    squares = lax.dot_general(ones, square_high, NT, preferred_element_type=f32)
    got_square[c] = squares + lax.dot_general(ones, square_low, NT, preferred_element_type=f32)

    wait_for(tokens.at[pl.ds(c * PLANE, PLANE)], t_recv)

    def plane_copy(source, to, d):
        block = tokens.at[pl.ds(source * PLANE, PLANE)]
        return send(block, block, u_send.at[d], u_recv.at[source], i, to)

    for d in range(1, CHAN):
        plane_copy(c, (c + d) % CHAN, d).start()

    def square_copy(d):
        return send(got_square.at[c], got_square.at[c], s_send.at[d], s_recv.at[c], i, (c + d) % CHAN)

    for d in range(1, CHAN):
        square_copy(d).start()
    scaled[...] = (wide * gain[pl.ds(c * feats, feats)].reshape(1, feats)).astype(bf16)

    start_weights(1)
    near, far = (c // 2) * 2, 2 - (c // 2) * 2
    other = c + 1 - 2 * (c % 2)
    part_send, part_got = (part_send0, part_send1), (part_got0, part_got1)

    def part_copy(h, to, d):
        return send(part_send[h].at[to], part_got[h].at[c], p_send.at[h, d], p_recv.at[h, c], i, to)

    def products(h, first):
        top, count = WEIGHT_ROWS[h]
        weights = got_weight[pl.ds(first, 2), pl.ds(top, count), :].reshape(2 * count, feats)
        product = lax.dot_general(weights, scaled[...], NT, preferred_element_type=f32)
        return product.reshape(2, count, product.shape[1])

    def start_parts(h):
        top, count = WEIGHT_ROWS[h]
        part_send[h][pl.ds(far, 2)] = products(h, far).astype(bf16)
        part_copy(h, far, 0).start()
        part_copy(h, far + 1, 1).start()
        product = products(h, near)
        part[:, top : top + count, :] = product
        part_send[h][pl.ds(near, 2)] = product.astype(bf16)
        part_copy(h, other, 2).start()

    def finish_parts(h, scale):
        top, count = WEIGHT_ROWS[h]
        total = part[c % 2, top : top + count, :]
        for d in range(1, CHAN):
            source = (c + d) % CHAN
            send(
                part_send[h].at[0], part_got[h].at[source], p_send.at[h, d], p_recv.at[h, source], i, source
            ).wait_recv()
            total = total + part_got[h][source].astype(f32)
        table[top : top + count, :] = (total * scale).astype(bf16).astype(f32)

    def branches_of(h):
        rows = jnp.concatenate([table[top : top + FEW, :] for top in TABLE_ROWS[h]], axis=0)
        halves = jnp.concatenate([rows[:, :SEG], rows[:, SEG:]], axis=0).astype(bf16)
        short_filter_and_gate(halves, tokens, taps.at[h], carried.at[h], query.at[h])

    def out_slot(h, source):
        return got_ref.at[h, :, pl.ds(pl.multiple_of(source * OWN, OWN), OWN), :], o_recv.at[h]

    def out_copy(h, to):
        dst, sem = out_slot(h, i)
        return send(ready.at[h, to], dst, o_send.at[h], sem, to, c)

    def start_outputs(h, decay_row):
        segment_states(carried.at[h], gather.at[h], decay_row[:, h * FEWS : (h + 1) * FEWS], state.at[h])

        @pl.loop(0, CTX // PLANE)
        def _(step):
            q = (plane + 1 + step) % (CTX // PLANE)
            outputs_of_part(
                q, carried.at[h], query.at[h], state.at[h], reach.at[h], skip.at[h], ready.at[h]
            )

            @pl.loop(0, PLANE)
            def _(n):
                to = q * PLANE + (place + n) % PLANE

                @pl.when(to != i)
                def _():
                    out_copy(h, to).start()

                @pl.when(to == i)
                def _():
                    pltpu.make_async_copy(ready.at[h, to], *out_slot(h, i)).start()

    wait_weights(0)
    start_parts(0)

    for load in loads[4:]:
        load.wait()
    lanes_from = pl.multiple_of((i // PLANE) * HALF, HALF)
    shift = lax.rem(HALF - place * OWN, HALF)
    decay_own, residue_own = load_own([decay, residue], lanes_from, shift)
    weight_own = residue_own * jnp.sqrt(decay_own)
    decay_row = filter_tables(decay_own, weight_own, gather, reach)
    for j in range(3):
        (rows,) = load_own([taps_all.at[j]], lanes_from, shift)
        padded = jnp.concatenate([rows, jnp.zeros((5, HALF), f32)], axis=0)
        columns = jnp.transpose(padded)[:OWN]
        for b in range(3):
            wide_column = jnp.broadcast_to(columns[:, b : b + 1], (OWN, HALF))
            for h in range(2):
                taps[h, j, b * FEW : (b + 1) * FEW, :] = wide_column[h * FEW : (h + 1) * FEW]
    skip_row = pltpu.roll(
        jnp.broadcast_to(skip_all[pl.ds(lanes_from, HALF)].reshape(1, HALF), (8, HALF)), shift, axis=1
    )
    skip_column = jnp.transpose(skip_row)[:OWN, 0:1]
    skip[...] = jnp.broadcast_to(skip_column, (OWN, SEG)).reshape(2, FEW, SEG)

    wait_weights(1)
    start_parts(1)
    mean = got_square[c]
    for d in range(1, CHAN):
        source = (c + d) % CHAN
        send(got_square.at[c], got_square.at[source], s_send.at[d], s_recv.at[source], i, source).wait_recv()
        mean = mean + got_square[source]
    scale = lax.rsqrt(mean[0:1] * (1.0 / (CHAN * feats)) + EPS)
    for d in range(1, CHAN):
        plane_copy((c + d) % CHAN, c, d).wait_recv()
    finish_parts(0, scale)
    branches_of(0)
    start_outputs(0, decay_row)
    finish_parts(1, scale)
    branches_of(1)
    start_outputs(1, decay_row)

    for h in range(2):
        wait_for(ready.at[h, pl.ds(0, CTX - 1)], o_send.at[h])
        part_copy(h, far, 0).wait_send()
        part_copy(h, far + 1, 1).wait_send()
        part_copy(h, other, 2).wait_send()

    def wait_sends(skipped):
        for h in range(2):
            rows = pl.ds(*WEIGHT_ROWS[h])
            wait_for(turned_weight.at[pl.ds(0, CTX - skipped), rows, :], w_send.at[h])
        wait_for(tokens.at[pl.ds(0, PLANE - skipped)], t_send)

    @pl.when(plane != c)
    def _():
        wait_sends(0)

    @pl.when(plane == c)
    def _():
        wait_sends(1)

    for d in range(1, CHAN):
        square_copy(d).wait_send()
        plane_copy(c, (c + d) % CHAN, d).wait_send()
    for h in range(2):
        wait_for(got_ref.at[h], o_recv.at[h])


def gathered(
    token_ids, embed_table, norm_gain, in_weight, short_filter, residue, decay_rate, skip_bias
):
    f32, bf16 = jnp.float32, jnp.bfloat16
    rows = token_ids.shape[0]
    vocab, feats = embed_table.shape
    chans = decay_rate.shape[1]
    weight = jnp.transpose(in_weight, (1, 0, 2))
    operands = (token_ids, embed_table, norm_gain, weight, short_filter, residue, decay_rate, skip_bias)
    dma, vmem = pltpu.SemaphoreType.DMA, pltpu.VMEM
    return pl.pallas_call(
        main_kernel,
        name="hyena",
        out_shape=pltpu.VMEM((2, PER, CTX * OWN, HALF), bf16),
        in_specs=[pl.BlockSpec(memory_space=pl.ANY)] * len(operands),
        out_specs=pl.BlockSpec(memory_space=pl.ANY),
        scratch_shapes=[
            vmem(token_ids.shape, jnp.int32),
            vmem((1, rows), jnp.int32),
            vmem(embed_table.shape, bf16),
            vmem(norm_gain.shape, f32),
            vmem(weight.shape, bf16),
            vmem(short_filter.shape, f32),
            vmem(residue.shape, f32),
            vmem(decay_rate.shape, f32),
            vmem(skip_bias.shape, f32),
            vmem((CTX, 3 * OWN, in_weight.shape[0]), bf16),
            vmem((CHAN, 3 * OWN, feats), bf16),
            vmem((CHAN, 8, vocab), f32),
            vmem((vocab, feats), bf16),
            vmem((2, 3 * OWN, vocab), f32),
            vmem((CHAN, WEIGHT_ROWS[0][1], vocab), bf16),
            vmem((CHAN, WEIGHT_ROWS[1][1], vocab), bf16),
            vmem((CHAN, WEIGHT_ROWS[0][1], vocab), bf16),
            vmem((CHAN, WEIGHT_ROWS[1][1], vocab), bf16),
            vmem((CTX, 1, rows), jnp.int32),
            vmem((3 * OWN, vocab), f32),
            vmem((2, SEG, 2 * FEWS), bf16),
            vmem((2, FEW * SEG + 3 * FEWS, SEG), bf16),
            vmem((2, 3, 3 * FEW, HALF), f32),
            vmem((2, FEW, SEG), f32),
            vmem((2, SEGS * FEW, SEG), f32),
            vmem((2, SEGS * FEW, SEG), f32),
            vmem((2, SEGS, FEWS), f32),
            vmem((2, CTX, PER, 2 * FEW, HALF), bf16),
            dma((8,)),
            dma((2,)), dma((2,)), dma(()), dma(()),
            dma((CHAN,)), dma((CHAN,)), dma((CHAN,)), dma((CHAN,)), dma((2, CHAN)), dma((2, CHAN)),
            dma((2,)), dma((2,)),
        ],
        compiler_params=pltpu.CompilerParams(
            collective_id=0, has_side_effects=True, vmem_limit_bytes=VMEM_LIMIT
        ),
    )(*operands)


def turn_kernel(got, out_hbm, out, out_sem):
    f32, bf16 = jnp.float32, jnp.bfloat16
    unit = (
        lax.broadcasted_iota(jnp.int32, (HALF, HALF), 0) == lax.broadcasted_iota(jnp.int32, (HALF, HALF), 1)
    ).astype(bf16)
    stores = []
    for g in range(PER):
        eights = [got[h, g].astype(f32).reshape(CTX, 2, FEW, HALF) for h in range(2)]
        for half in range(2):
            rows = jnp.concatenate([eights[h][:, half : half + 1] for h in range(2)], axis=1)
            rows = rows.reshape(CTX * OWN, HALF).astype(bf16)
            top = g * SEG + half * HALF
            turned = lax.dot_general(unit, rows, NT, preferred_element_type=f32)
            out[top : top + HALF, :] = turned.astype(bf16)
        rows = pl.ds(g * SEG, SEG)
        stores.append(pltpu.make_async_copy(out.at[rows, :], out_hbm.at[rows, :], out_sem.at[g]))
        stores[g].start()
    for store in stores:
        store.wait()


def turned(got):
    bf16 = jnp.bfloat16
    shape = (PER * SEG, CTX * OWN)
    return pl.pallas_call(
        turn_kernel,
        name="turn",
        out_shape=jax.ShapeDtypeStruct(shape, bf16),
        in_specs=[pl.BlockSpec(memory_space=pltpu.VMEM)],
        out_specs=pl.BlockSpec(memory_space=pl.ANY),
        scratch_shapes=[pltpu.VMEM(shape, bf16), pltpu.SemaphoreType.DMA((PER,))],
        compiler_params=pltpu.CompilerParams(vmem_limit_bytes=TURN_LIMIT),
    )(got)


def per_device(*arrays):
    return turned(gathered(*arrays))


def solution(mesh):
    return jax.shard_map(
        per_device,
        mesh=mesh,
        in_specs=(
            P("ctx"),
            P(None, "chan"),
            P(),
            P("ctx", None, "chan"),
            P(None, None, "chan"),
            P(None, "chan"),
            P(None, "chan"),
            P("chan"),
        ),
        out_specs=P("ctx", "chan"),
        check_vma=False,
    )
```

```python
import functools

import jax
import jax.numpy as jnp
from jax import lax
from jax.experimental import pallas as pl
from jax.experimental.pallas import tpu as pltpu
from jax.sharding import PartitionSpec as P

MESH = pl.DeviceIdType.MESH
EPS = 1e-06
VMEM_LIMIT = 56 * 1024 * 1024
TURN_LIMIT = 16 * 1024 * 1024

CTX, CHAN, PLANE = 32, 4, 8
OWN = 16
SEG = 256
SEGS = 96
PER = 3
PART = 24
HALF = 128
MODES = 16
PAIRS = OWN * MODES
FEW = 8
FEWS = FEW * MODES
WEIGHT_ROWS = ((0, 32), (32, 16))
TABLE_ROWS = ((0, 8, 16), (32, 24, 40))
NT = (((1,), (1,)), ((), ()))
HIGHEST = lax.Precision.HIGHEST


def dot(a, b):
    return jnp.dot(a, b, preferred_element_type=jnp.float32)


def high_low(x):
    high = x.astype(jnp.bfloat16)
    return high, (x - high.astype(jnp.float32)).astype(jnp.bfloat16)


def send(src, dst, send_sem, recv_sem, i, c):
    return pltpu.make_async_remote_copy(
        src_ref=src, dst_ref=dst, send_sem=send_sem, recv_sem=recv_sem, device_id=(i, c), device_id_type=MESH
    )


def load_own(row_refs, lanes_from, shift):
    rows = [ref[:, pl.ds(lanes_from, HALF)] for ref in row_refs]
    return [pltpu.roll(array, shift, axis=1) for array in rows]


def filter_tables(decay, weight, gather, reach):
    f32, bf16 = jnp.float32, jnp.bfloat16
    decay_turned = jnp.transpose(decay)[:OWN]
    weight_turned = jnp.transpose(weight)[:OWN]
    lane = lax.broadcasted_iota(jnp.int32, (OWN, HALF), 1).astype(f32)
    near = jnp.zeros((OWN, HALF), f32)
    far = jnp.zeros((OWN, HALF), f32)
    for m in range(MODES):
        rate = jnp.broadcast_to(decay_turned[:, m : m + 1], (OWN, HALF))
        height = jnp.broadcast_to(weight_turned[:, m : m + 1], (OWN, HALF))
        near = near + height * jnp.exp(-rate * lane)
        far = far + height * jnp.exp(-rate * (lane + float(HALF)))
    causal = lax.broadcasted_iota(jnp.int32, (HALF, HALF), 1) >= lax.broadcasted_iota(jnp.int32, (HALF, HALF), 0)
    for ch in range(OWN):
        near_rolled = pltpu.roll(
            jnp.broadcast_to(near[ch : ch + 1], (HALF, HALF)), 0, axis=1, stride=1, stride_axis=0
        )
        far_rolled = pltpu.roll(
            jnp.broadcast_to(far[ch : ch + 1], (HALF, HALF)), 0, axis=1, stride=1, stride_axis=0
        )
        diagonal = jnp.where(causal, near_rolled, 0.0).astype(bf16)
        part, top = ch // FEW, ch % FEW * SEG
        middle, end = top + HALF, top + SEG
        reach[part, top:middle, :HALF] = diagonal
        reach[part, middle:end, HALF:] = diagonal
        reach[part, top:middle, HALF:] = jnp.where(causal, far_rolled, near_rolled).astype(bf16)
        reach[part, middle:end, :HALF] = jnp.zeros((HALF, HALF), bf16)

    pick = (
        lax.broadcasted_iota(jnp.int32, (HALF, PAIRS), 0)
        == lax.broadcasted_iota(jnp.int32, (HALF, PAIRS), 1) // MODES
    ).astype(f32)
    own_mode = (
        lax.broadcasted_iota(jnp.int32, (MODES, PAIRS), 0)
        == lax.broadcasted_iota(jnp.int32, (MODES, PAIRS), 1) % MODES
    )

    def pair_row(array):
        wide = jnp.dot(array, pick, precision=HIGHEST, preferred_element_type=f32)
        return jnp.sum(jnp.where(own_mode, wide, 0.0), axis=0, keepdims=True)

    decay_row = pair_row(decay)
    decay_column = jnp.transpose(jnp.broadcast_to(decay_row, (HALF, PAIRS)))
    weight_column = jnp.transpose(jnp.broadcast_to(pair_row(weight), (HALF, PAIRS)))
    to_end = (SEG - 1 - lax.broadcasted_iota(jnp.int32, (SEG, PAIRS), 0)).astype(f32)
    entering = high_low(jnp.exp(-decay_row * to_end))
    for part in range(2):
        for n in range(2):
            gather[part, :, n * FEWS : (n + 1) * FEWS] = entering[n][:, part * FEWS : (part + 1) * FEWS]
    for half in range(2):
        lanes = slice(half * HALF, (half + 1) * HALF)
        after = lax.broadcasted_iota(jnp.int32, (PAIRS, HALF), 1).astype(f32) + float(half * HALF + 1)
        high, low = high_low(weight_column * jnp.exp(-decay_column * after))
        for part in range(2):
            rows = slice(part * FEWS, (part + 1) * FEWS)
            for n, piece in enumerate((high, high, low)):
                top = FEW * SEG + n * FEWS
                reach[part, top : top + FEWS, lanes] = piece[rows]
    return decay_row


def short_filter_and_gate(table, tokens_ref, taps_ref, carried_ref, query_ref):
    f32, bf16 = jnp.float32, jnp.bfloat16
    rows = 3 * FEW
    entry = lax.broadcasted_iota(jnp.int32, (HALF, SEG), 0).astype(f32).astype(bf16)
    lane = lax.broadcasted_iota(jnp.int32, (rows, HALF), 1)
    one, zero = jnp.ones((), bf16), jnp.zeros((), bf16)

    def block(g, before):
        for part in range(PER):
            ids = tokens_ref[g, :, part * SEG : (part + 1) * SEG]
            chosen = (ids & (HALF - 1)).astype(f32).astype(bf16)
            each = dot(table, jnp.where(entry == chosen, one, zero)).reshape(4, rows, SEG)
            odd, upper = (ids & HALF) != 0, (ids & SEG) != 0
            projected = jnp.where(upper, jnp.where(odd, each[3], each[2]), jnp.where(odd, each[1], each[0]))
            at = pl.ds(pl.multiple_of((g * PER + part) * FEW, FEW), FEW)
            for half in range(2):
                lanes = slice(half * HALF, (half + 1) * HALF)
                here = projected[:, lanes]
                turned = (pltpu.roll(here, 1, axis=1), pltpu.roll(here, 2, axis=1))
                branches = (
                    taps_ref[0] * here
                    + taps_ref[1] * jnp.where(lane < 1, before[0], turned[0])
                    + taps_ref[2] * jnp.where(lane < 2, before[1], turned[1])
                )
                before = turned
                carried = branches[FEW : 2 * FEW] * branches[2 * FEW :]
                carried_ref[at, lanes] = carried.astype(bf16).astype(f32)
                query_ref[at, lanes] = branches[:FEW]
        return before

    nothing = jnp.zeros((rows, HALF), f32)
    lax.fori_loop(0, SEGS // PER, block, (nothing, nothing), unroll=UNROLL)


UNROLL = 16


def own_pairs():
    shape = (1, FEW, FEWS)
    return lax.broadcasted_iota(jnp.int32, shape, 2) // MODES == lax.broadcasted_iota(jnp.int32, shape, 1)


def segment_states(carried_ref, gather, decay_row, state_ref):
    f32, bf16 = jnp.float32, jnp.bfloat16
    enters = dot(carried_ref[...].astype(bf16), gather[...])
    enters = (enters[:, :FEWS] + enters[:, FEWS:]).reshape(SEGS, FEW, FEWS)
    added = jnp.sum(jnp.where(own_pairs(), enters, 0.0), axis=1)

    def later(x, by):
        return jnp.concatenate([jnp.zeros((by, FEWS), f32), x[: SEGS - by]], axis=0)

    state = later(added, 1)
    by = 1
    while by < SEGS:
        state = state + jnp.exp(-decay_row * float(SEG * by)) * later(state, by)
        by *= 2
    state_ref[...] = state


def outputs_of_part(q, carried_ref, query_ref, state_ref, reach, skip_ref, ready):
    f32, bf16 = jnp.float32, jnp.bfloat16
    first = pl.multiple_of(q * PART, PART)
    rows = pl.ds(pl.multiple_of(first * FEW, FEW), PART * FEW)
    carried = carried_ref[rows, :].reshape(PART, FEW, SEG)
    channel = lax.broadcasted_iota(jnp.int32, (1, FEW, SEG), 1)
    parts = [
        jnp.where(channel == ch, carried, 0.0).reshape(PART * FEW, SEG).astype(bf16) for ch in range(FEW)
    ]
    state = jnp.where(own_pairs(), state_ref[pl.ds(first, PART), :][:, None, :], 0.0)
    high, low = high_low(state.reshape(PART * FEW, FEWS))
    conv = dot(jnp.concatenate(parts + [high, low, high], axis=1), reach[...])
    gated = query_ref[rows, :] * (conv + (skip_ref[...][None] * carried).reshape(PART * FEW, SEG))
    halves = [gated[:, half * HALF : (half + 1) * HALF].reshape(PART, 1, FEW, HALF) for half in range(2)]
    block = jnp.concatenate(halves, axis=1).reshape(PLANE, PER, 2 * FEW, HALF)
    ready[pl.ds(q * PLANE, PLANE)] = block.astype(bf16)


def main_kernel(
    tok_hbm, embed_hbm, gain_hbm, weight_hbm, taps_hbm, residue_hbm, decay_hbm, skip_hbm, got_ref,
    tok, own_tokens, embed, gain, weight, taps_all, residue, decay, skip_all,
    turned_weight, got_weight, got_square, scaled, part, part_send0, part_send1, part_got0, part_got1, tokens, table,
    gather, reach, taps, skip, carried, query, state, ready,
    in_sem, w_send, w_recv, t_send, t_recv, u_send, u_recv, s_send, s_recv, p_send, p_recv, o_send, o_recv,
):
    f32, bf16 = jnp.float32, jnp.bfloat16
    i, c = lax.axis_index("ctx"), lax.axis_index("chan")
    plane, place = i // PLANE, i % PLANE

    loads = [
        pltpu.make_async_copy(src, dst, in_sem.at[n])
        for n, (src, dst) in enumerate(
            (
                (weight_hbm, weight), (tok_hbm, tok), (embed_hbm, embed), (gain_hbm, gain),
                (taps_hbm, taps_all), (residue_hbm, residue), (decay_hbm, decay), (skip_hbm, skip_all),
            )
        )
    ]
    for load in loads:
        load.start()

    barrier = pltpu.get_barrier_semaphore()

    @pl.loop(0, CTX)
    def _(j):
        row, col = c * PLANE + j % PLANE, j // PLANE

        @pl.when(jnp.logical_or(row != i, col != c))
        def _():
            pl.semaphore_signal(barrier, inc=1, device_id=(row, col), device_id_type=MESH)

    for d in range(1, CHAN):
        pl.semaphore_signal(barrier, inc=1, device_id=(i, (c + d) % CHAN), device_id_type=MESH)

    loads[0].wait()
    eights = [jnp.transpose(weight[b].astype(f32)).reshape(CTX, 2, FEW, HALF) for b in range(3)]
    order = ((0, 0), (1, 0), (2, 0), (1, 1), (0, 1), (2, 1))
    rows = jnp.concatenate([eights[b][:, part : part + 1] for b, part in order], axis=1)
    turned_weight[...] = rows.reshape(turned_weight.shape).astype(bf16)
    loads[1].wait()
    own_tokens[...] = tok[...].reshape(1, tok.shape[0])

    pl.semaphore_wait(barrier, CTX - jnp.where(plane == c, 1, 0) + CHAN - 1)

    def weight_slices(h, to, slot):
        rows = pl.ds(*WEIGHT_ROWS[h])
        lanes = pl.ds(pl.multiple_of(slot % PLANE * HALF, HALF), HALF)
        return turned_weight.at[to, rows, :], got_weight.at[slot // PLANE, rows, lanes], w_recv.at[h]

    def weight_copy(h, j):
        to = (i + j) % CTX
        src, dst, sem = weight_slices(h, to, c * PLANE + place)
        return send(src, dst, w_send.at[h], sem, to, plane)

    def start_weights(h):
        @pl.loop(1, CTX)
        def _(j):
            weight_copy(h, j).start()

        @pl.when(plane == c)
        def _():
            pltpu.make_async_copy(*weight_slices(h, i, c * PLANE + place)).start()

        @pl.when(plane != c)
        def _():
            weight_copy(h, 0).start()

    def wait_for(region, sem):
        pltpu.make_async_copy(region, region, sem).wait()

    def wait_weights(h):
        wait_for(got_weight.at[:, pl.ds(*WEIGHT_ROWS[h]), :], w_recv.at[h])

    def token_copy(n):
        to = c * PLANE + (place + n) % PLANE
        return send(own_tokens, tokens.at[i], t_send, t_recv, to, plane)

    own_token_copy = pltpu.make_async_copy(own_tokens, tokens.at[i], t_recv)

    @pl.when(plane == c)
    def _():
        own_token_copy.start()

    @pl.when(plane != c)
    def _():
        token_copy(0).start()

    @pl.loop(1, PLANE)
    def _(n):
        token_copy(n).start()

    start_weights(0)

    loads[2].wait()
    loads[3].wait()
    wide = embed[...].astype(f32)
    feats = embed.shape[1]
    square_high, square_low = high_low(wide * wide)
    ones = jnp.ones((8, feats), bf16)
    squares = lax.dot_general(ones, square_high, NT, preferred_element_type=f32)
    got_square[c] = squares + lax.dot_general(ones, square_low, NT, preferred_element_type=f32)

    wait_for(tokens.at[pl.ds(c * PLANE, PLANE)], t_recv)

    def plane_copy(source, to, d):
        block = tokens.at[pl.ds(source * PLANE, PLANE)]
        return send(block, block, u_send.at[d], u_recv.at[source], i, to)

    for d in range(1, CHAN):
        plane_copy(c, (c + d) % CHAN, d).start()

    def square_copy(d):
        return send(got_square.at[c], got_square.at[c], s_send.at[d], s_recv.at[c], i, (c + d) % CHAN)

    for d in range(1, CHAN):
        square_copy(d).start()
    scaled[...] = (wide * gain[pl.ds(c * feats, feats)].reshape(1, feats)).astype(bf16)

    start_weights(1)
    near, far = (c // 2) * 2, 2 - (c // 2) * 2
    other = c + 1 - 2 * (c % 2)
    part_send, part_got = (part_send0, part_send1), (part_got0, part_got1)

    def part_copy(h, to, d):
        return send(part_send[h].at[to], part_got[h].at[c], p_send.at[h, d], p_recv.at[h, c], i, to)

    def products(h, first):
        top, count = WEIGHT_ROWS[h]
        weights = got_weight[pl.ds(first, 2), pl.ds(top, count), :].reshape(2 * count, feats)
        product = lax.dot_general(weights, scaled[...], NT, preferred_element_type=f32)
        return product.reshape(2, count, product.shape[1])

    def start_parts(h):
        top, count = WEIGHT_ROWS[h]
        part_send[h][pl.ds(far, 2)] = products(h, far).astype(bf16)
        part_copy(h, far, 0).start()
        part_copy(h, far + 1, 1).start()
        product = products(h, near)
        part[:, top : top + count, :] = product
        part_send[h][pl.ds(near, 2)] = product.astype(bf16)
        part_copy(h, other, 2).start()

    def finish_parts(h, scale):
        top, count = WEIGHT_ROWS[h]
        total = part[c % 2, top : top + count, :]
        for d in range(1, CHAN):
            source = (c + d) % CHAN
            send(
                part_send[h].at[0], part_got[h].at[source], p_send.at[h, d], p_recv.at[h, source], i, source
            ).wait_recv()
            total = total + part_got[h][source].astype(f32)
        table[top : top + count, :] = (total * scale).astype(bf16).astype(f32)

    def branches_of(h):
        rows = jnp.concatenate([table[top : top + FEW, :] for top in TABLE_ROWS[h]], axis=0)
        quarters = jnp.concatenate([rows[:, n * HALF : (n + 1) * HALF] for n in range(4)], axis=0)
        short_filter_and_gate(quarters.astype(bf16), tokens, taps.at[h], carried.at[h], query.at[h])

    def out_slot(h, source):
        return got_ref.at[h, :, pl.ds(pl.multiple_of(source * OWN, OWN), OWN), :], o_recv.at[h]

    def out_copy(h, to):
        dst, sem = out_slot(h, i)
        return send(ready.at[h, to], dst, o_send.at[h], sem, to, c)

    def start_outputs(h, decay_row):
        segment_states(carried.at[h], gather.at[h], decay_row[:, h * FEWS : (h + 1) * FEWS], state.at[h])

        @pl.loop(0, CTX // PLANE)
        def _(step):
            q = (plane + 1 + step) % (CTX // PLANE)
            outputs_of_part(
                q, carried.at[h], query.at[h], state.at[h], reach.at[h], skip.at[h], ready.at[h]
            )

            @pl.loop(0, PLANE)
            def _(n):
                to = q * PLANE + (place + n) % PLANE

                @pl.when(to != i)
                def _():
                    out_copy(h, to).start()

                @pl.when(to == i)
                def _():
                    pltpu.make_async_copy(ready.at[h, to], *out_slot(h, i)).start()

    wait_weights(0)
    start_parts(0)

    for load in loads[4:]:
        load.wait()
    lanes_from = pl.multiple_of((i // PLANE) * HALF, HALF)
    shift = lax.rem(HALF - place * OWN, HALF)
    decay_own, residue_own = load_own([decay, residue], lanes_from, shift)
    weight_own = residue_own * jnp.sqrt(decay_own)
    decay_row = filter_tables(decay_own, weight_own, gather, reach)
    for j in range(3):
        (rows,) = load_own([taps_all.at[j]], lanes_from, shift)
        padded = jnp.concatenate([rows, jnp.zeros((5, HALF), f32)], axis=0)
        columns = jnp.transpose(padded)[:OWN]
        for b in range(3):
            wide_column = jnp.broadcast_to(columns[:, b : b + 1], (OWN, HALF))
            for h in range(2):
                taps[h, j, b * FEW : (b + 1) * FEW, :] = wide_column[h * FEW : (h + 1) * FEW]
    skip_row = pltpu.roll(
        jnp.broadcast_to(skip_all[pl.ds(lanes_from, HALF)].reshape(1, HALF), (8, HALF)), shift, axis=1
    )
    skip_column = jnp.transpose(skip_row)[:OWN, 0:1]
    skip[...] = jnp.broadcast_to(skip_column, (OWN, SEG)).reshape(2, FEW, SEG)

    wait_weights(1)
    start_parts(1)
    mean = got_square[c]
    for d in range(1, CHAN):
        source = (c + d) % CHAN
        send(got_square.at[c], got_square.at[source], s_send.at[d], s_recv.at[source], i, source).wait_recv()
        mean = mean + got_square[source]
    scale = lax.rsqrt(mean[0:1] * (1.0 / (CHAN * feats)) + EPS)
    for d in range(1, CHAN):
        plane_copy((c + d) % CHAN, c, d).wait_recv()
    finish_parts(0, scale)
    branches_of(0)
    start_outputs(0, decay_row)
    finish_parts(1, scale)
    branches_of(1)
    start_outputs(1, decay_row)

    for h in range(2):
        wait_for(ready.at[h, pl.ds(0, CTX - 1)], o_send.at[h])
        part_copy(h, far, 0).wait_send()
        part_copy(h, far + 1, 1).wait_send()
        part_copy(h, other, 2).wait_send()

    def wait_sends(skipped):
        for h in range(2):
            rows = pl.ds(*WEIGHT_ROWS[h])
            wait_for(turned_weight.at[pl.ds(0, CTX - skipped), rows, :], w_send.at[h])
        wait_for(tokens.at[pl.ds(0, PLANE - skipped)], t_send)

    @pl.when(plane != c)
    def _():
        wait_sends(0)

    @pl.when(plane == c)
    def _():
        wait_sends(1)

    for d in range(1, CHAN):
        square_copy(d).wait_send()
        plane_copy(c, (c + d) % CHAN, d).wait_send()
    for h in range(2):
        wait_for(got_ref.at[h], o_recv.at[h])


def gathered(
    token_ids, embed_table, norm_gain, in_weight, short_filter, residue, decay_rate, skip_bias
):
    f32, bf16 = jnp.float32, jnp.bfloat16
    rows = token_ids.shape[0]
    vocab, feats = embed_table.shape
    chans = decay_rate.shape[1]
    weight = jnp.transpose(in_weight, (1, 0, 2))
    operands = (token_ids, embed_table, norm_gain, weight, short_filter, residue, decay_rate, skip_bias)
    dma, vmem = pltpu.SemaphoreType.DMA, pltpu.VMEM
    return pl.pallas_call(
        main_kernel,
        name="hyena",
        out_shape=pltpu.VMEM((2, PER, CTX * OWN, HALF), bf16),
        in_specs=[pl.BlockSpec(memory_space=pl.ANY)] * len(operands),
        out_specs=pl.BlockSpec(memory_space=pl.ANY),
        scratch_shapes=[
            vmem(token_ids.shape, jnp.int32),
            vmem((1, rows), jnp.int32),
            vmem(embed_table.shape, bf16),
            vmem(norm_gain.shape, f32),
            vmem(weight.shape, bf16),
            vmem(short_filter.shape, f32),
            vmem(residue.shape, f32),
            vmem(decay_rate.shape, f32),
            vmem(skip_bias.shape, f32),
            vmem((CTX, 3 * OWN, in_weight.shape[0]), bf16),
            vmem((CHAN, 3 * OWN, feats), bf16),
            vmem((CHAN, 8, vocab), f32),
            vmem((vocab, feats), bf16),
            vmem((2, 3 * OWN, vocab), f32),
            vmem((CHAN, WEIGHT_ROWS[0][1], vocab), bf16),
            vmem((CHAN, WEIGHT_ROWS[1][1], vocab), bf16),
            vmem((CHAN, WEIGHT_ROWS[0][1], vocab), bf16),
            vmem((CHAN, WEIGHT_ROWS[1][1], vocab), bf16),
            vmem((CTX, 1, rows), jnp.int32),
            vmem((3 * OWN, vocab), f32),
            vmem((2, SEG, 2 * FEWS), bf16),
            vmem((2, FEW * SEG + 3 * FEWS, SEG), bf16),
            vmem((2, 3, 3 * FEW, HALF), f32),
            vmem((2, FEW, SEG), f32),
            vmem((2, SEGS * FEW, SEG), f32),
            vmem((2, SEGS * FEW, SEG), f32),
            vmem((2, SEGS, FEWS), f32),
            vmem((2, CTX, PER, 2 * FEW, HALF), bf16),
            dma((8,)),
            dma((2,)), dma((2,)), dma(()), dma(()),
            dma((CHAN,)), dma((CHAN,)), dma((CHAN,)), dma((CHAN,)), dma((2, CHAN)), dma((2, CHAN)),
            dma((2,)), dma((2,)),
        ],
        compiler_params=pltpu.CompilerParams(
            collective_id=0, has_side_effects=True, vmem_limit_bytes=VMEM_LIMIT
        ),
    )(*operands)


def turn_kernel(got, out_hbm, out, out_sem):
    f32, bf16 = jnp.float32, jnp.bfloat16
    unit = (
        lax.broadcasted_iota(jnp.int32, (HALF, HALF), 0) == lax.broadcasted_iota(jnp.int32, (HALF, HALF), 1)
    ).astype(bf16)
    stores = []
    for g in range(PER):
        eights = [got[h, g].astype(f32).reshape(CTX, 2, FEW, HALF) for h in range(2)]
        for half in range(2):
            rows = jnp.concatenate([eights[h][:, half : half + 1] for h in range(2)], axis=1)
            rows = rows.reshape(CTX * OWN, HALF).astype(bf16)
            top = g * SEG + half * HALF
            turned = lax.dot_general(unit, rows, NT, preferred_element_type=f32)
            out[top : top + HALF, :] = turned.astype(bf16)
        rows = pl.ds(g * SEG, SEG)
        stores.append(pltpu.make_async_copy(out.at[rows, :], out_hbm.at[rows, :], out_sem.at[g]))
        stores[g].start()
    for store in stores:
        store.wait()


def turned(got):
    bf16 = jnp.bfloat16
    shape = (PER * SEG, CTX * OWN)
    return pl.pallas_call(
        turn_kernel,
        name="turn",
        out_shape=jax.ShapeDtypeStruct(shape, bf16),
        in_specs=[pl.BlockSpec(memory_space=pltpu.VMEM)],
        out_specs=pl.BlockSpec(memory_space=pl.ANY),
        scratch_shapes=[pltpu.VMEM(shape, bf16), pltpu.SemaphoreType.DMA((PER,))],
        compiler_params=pltpu.CompilerParams(vmem_limit_bytes=TURN_LIMIT),
    )(got)


def per_device(*arrays):
    return turned(gathered(*arrays))


def solution(mesh):
    return jax.shard_map(
        per_device,
        mesh=mesh,
        in_specs=(
            P("ctx"),
            P(None, "chan"),
            P(),
            P("ctx", None, "chan"),
            P(None, None, "chan"),
            P(None, "chan"),
            P(None, "chan"),
            P("chan"),
        ),
        out_specs=P("ctx", "chan"),
        check_vma=False,
    )
```

```python
import functools

import jax
import jax.numpy as jnp
from jax import lax
from jax.experimental import pallas as pl
from jax.experimental.pallas import tpu as pltpu
from jax.sharding import PartitionSpec as P

MESH = pl.DeviceIdType.MESH
EPS = 1e-06
VMEM_LIMIT = 56 * 1024 * 1024
TURN_LIMIT = 16 * 1024 * 1024

CTX, CHAN, PLANE = 32, 4, 8
OWN = 16
SEG = 256
SEGS = 96
PER = 3
PART = 24
HALF = 128
MODES = 16
PAIRS = OWN * MODES
FEW = 8
FEWS = FEW * MODES
WEIGHT_ROWS = ((0, 32), (32, 16))
TABLE_ROWS = ((0, 8, 16), (32, 24, 40))
NT = (((1,), (1,)), ((), ()))
HIGHEST = lax.Precision.HIGHEST


def dot(a, b):
    return jnp.dot(a, b, preferred_element_type=jnp.float32)


def high_low(x):
    high = x.astype(jnp.bfloat16)
    return high, (x - high.astype(jnp.float32)).astype(jnp.bfloat16)


def send(src, dst, send_sem, recv_sem, i, c):
    return pltpu.make_async_remote_copy(
        src_ref=src, dst_ref=dst, send_sem=send_sem, recv_sem=recv_sem, device_id=(i, c), device_id_type=MESH
    )


def load_own(row_refs, lanes_from, shift):
    rows = [ref[:, pl.ds(lanes_from, HALF)] for ref in row_refs]
    return [pltpu.roll(array, shift, axis=1) for array in rows]


def filter_tables(decay, weight, gather, reach):
    f32, bf16 = jnp.float32, jnp.bfloat16
    decay_turned = jnp.transpose(decay)[:OWN]
    weight_turned = jnp.transpose(weight)[:OWN]
    lane = lax.broadcasted_iota(jnp.int32, (OWN, HALF), 1).astype(f32)
    near = jnp.zeros((OWN, HALF), f32)
    far = jnp.zeros((OWN, HALF), f32)
    for m in range(MODES):
        rate = jnp.broadcast_to(decay_turned[:, m : m + 1], (OWN, HALF))
        height = jnp.broadcast_to(weight_turned[:, m : m + 1], (OWN, HALF))
        near = near + height * jnp.exp(-rate * lane)
        far = far + height * jnp.exp(-rate * (lane + float(HALF)))
    causal = lax.broadcasted_iota(jnp.int32, (HALF, HALF), 1) >= lax.broadcasted_iota(jnp.int32, (HALF, HALF), 0)
    for ch in range(OWN):
        near_rolled = pltpu.roll(
            jnp.broadcast_to(near[ch : ch + 1], (HALF, HALF)), 0, axis=1, stride=1, stride_axis=0
        )
        far_rolled = pltpu.roll(
            jnp.broadcast_to(far[ch : ch + 1], (HALF, HALF)), 0, axis=1, stride=1, stride_axis=0
        )
        diagonal = jnp.where(causal, near_rolled, 0.0).astype(bf16)
        part, top = ch // FEW, ch % FEW * SEG
        middle, end = top + HALF, top + SEG
        reach[part, top:middle, :HALF] = diagonal
        reach[part, middle:end, HALF:] = diagonal
        reach[part, top:middle, HALF:] = jnp.where(causal, far_rolled, near_rolled).astype(bf16)
        reach[part, middle:end, :HALF] = jnp.zeros((HALF, HALF), bf16)

    pick = (
        lax.broadcasted_iota(jnp.int32, (HALF, PAIRS), 0)
        == lax.broadcasted_iota(jnp.int32, (HALF, PAIRS), 1) // MODES
    ).astype(f32)
    own_mode = (
        lax.broadcasted_iota(jnp.int32, (MODES, PAIRS), 0)
        == lax.broadcasted_iota(jnp.int32, (MODES, PAIRS), 1) % MODES
    )

    def pair_row(array):
        wide = jnp.dot(array, pick, precision=HIGHEST, preferred_element_type=f32)
        return jnp.sum(jnp.where(own_mode, wide, 0.0), axis=0, keepdims=True)

    decay_row = pair_row(decay)
    decay_column = jnp.transpose(jnp.broadcast_to(decay_row, (HALF, PAIRS)))
    weight_column = jnp.transpose(jnp.broadcast_to(pair_row(weight), (HALF, PAIRS)))
    to_end = (SEG - 1 - lax.broadcasted_iota(jnp.int32, (SEG, PAIRS), 0)).astype(f32)
    entering = high_low(jnp.exp(-decay_row * to_end))
    for part in range(2):
        for n in range(2):
            gather[part, :, n * FEWS : (n + 1) * FEWS] = entering[n][:, part * FEWS : (part + 1) * FEWS]
    for half in range(2):
        lanes = slice(half * HALF, (half + 1) * HALF)
        after = lax.broadcasted_iota(jnp.int32, (PAIRS, HALF), 1).astype(f32) + float(half * HALF + 1)
        high, low = high_low(weight_column * jnp.exp(-decay_column * after))
        for part in range(2):
            rows = slice(part * FEWS, (part + 1) * FEWS)
            for n, piece in enumerate((high, high, low)):
                top = FEW * SEG + n * FEWS
                reach[part, top : top + FEWS, lanes] = piece[rows]
    return decay_row


def short_filter_and_gate(table, tokens_ref, taps_ref, carried_ref, query_ref):
    f32, bf16 = jnp.float32, jnp.bfloat16
    rows = 3 * FEW
    entry = lax.broadcasted_iota(jnp.int32, (HALF, SEG), 0).astype(f32).astype(bf16)
    lane = lax.broadcasted_iota(jnp.int32, (rows, HALF), 1)
    one, zero = jnp.ones((), bf16), jnp.zeros((), bf16)

    def block(g, before):
        for part in range(PER):
            ids = tokens_ref[g, :, part * SEG : (part + 1) * SEG]
            chosen = (ids & (HALF - 1)).astype(f32).astype(bf16)
            each = dot(table, jnp.where(entry == chosen, one, zero)).reshape(4, rows, SEG)
            odd, upper = (ids & HALF) != 0, (ids & SEG) != 0
            projected = jnp.where(upper, jnp.where(odd, each[3], each[2]), jnp.where(odd, each[1], each[0]))
            at = pl.ds(pl.multiple_of((g * PER + part) * FEW, FEW), FEW)
            for half in range(2):
                lanes = slice(half * HALF, (half + 1) * HALF)
                here = projected[:, lanes]
                turned = (pltpu.roll(here, 1, axis=1), pltpu.roll(here, 2, axis=1))
                branches = (
                    taps_ref[0] * here
                    + taps_ref[1] * jnp.where(lane < 1, before[0], turned[0])
                    + taps_ref[2] * jnp.where(lane < 2, before[1], turned[1])
                )
                before = turned
                carried = branches[FEW : 2 * FEW] * branches[2 * FEW :]
                carried_ref[half, at, :] = carried.astype(bf16).astype(f32)
                query_ref[half, at, :] = branches[:FEW]
        return before

    nothing = jnp.zeros((rows, HALF), f32)
    lax.fori_loop(0, SEGS // PER, block, (nothing, nothing), unroll=UNROLL)


UNROLL = 16


def both_halves(ref, rows):
    return jnp.concatenate([ref[half, rows, :] for half in range(2)], axis=1)


def own_pairs():
    shape = (1, FEW, FEWS)
    return lax.broadcasted_iota(jnp.int32, shape, 2) // MODES == lax.broadcasted_iota(jnp.int32, shape, 1)


def segment_states(carried_ref, gather, decay_row, state_ref):
    f32, bf16 = jnp.float32, jnp.bfloat16
    enters = dot(both_halves(carried_ref, slice(None)).astype(bf16), gather[...])
    enters = (enters[:, :FEWS] + enters[:, FEWS:]).reshape(SEGS, FEW, FEWS)
    added = jnp.sum(jnp.where(own_pairs(), enters, 0.0), axis=1)

    def later(x, by):
        return jnp.concatenate([jnp.zeros((by, FEWS), f32), x[: SEGS - by]], axis=0)

    state = later(added, 1)
    by = 1
    while by < SEGS:
        state = state + jnp.exp(-decay_row * float(SEG * by)) * later(state, by)
        by *= 2
    state_ref[...] = state


def inside_segments(carried_ref, reach, conv_ref):
    for ch in range(FEW):
        rows = pl.ds(ch, SEGS, stride=FEW)
        conv = dot(both_halves(carried_ref, rows).astype(jnp.bfloat16), reach[ch * SEG : (ch + 1) * SEG, :])
        for half in range(2):
            conv_ref[half, rows, :] = conv[:, half * HALF : (half + 1) * HALF]


def outputs_of_part(q, carried_ref, query_ref, state_ref, conv_ref, reach, skip_ref, ready):
    first = pl.multiple_of(q * PART, PART)
    rows = pl.ds(pl.multiple_of(first * FEW, FEW), PART * FEW)
    state = jnp.where(own_pairs(), state_ref[pl.ds(first, PART), :][:, None, :], 0.0)
    high, low = high_low(state.reshape(PART * FEW, FEWS))
    reached = dot(jnp.concatenate([high, low, high], axis=1), reach[FEW * SEG :, :])
    halves = []
    for half in range(2):
        lanes = slice(half * HALF, (half + 1) * HALF)
        carried = carried_ref[half, rows, :].reshape(PART, FEW, HALF)
        direct = (skip_ref[:, lanes][None] * carried).reshape(PART * FEW, HALF)
        gated = query_ref[half, rows, :] * (conv_ref[half, rows, :] + reached[:, lanes] + direct)
        halves.append(gated.reshape(PART, 1, FEW, HALF))
    block = jnp.concatenate(halves, axis=1).reshape(PLANE, PER, 2 * FEW, HALF)
    ready[pl.ds(q * PLANE, PLANE)] = block.astype(jnp.bfloat16)


def main_kernel(
    tok_hbm, embed_hbm, gain_hbm, weight_hbm, taps_hbm, residue_hbm, decay_hbm, skip_hbm, got_ref,
    tok, own_tokens, embed, gain, weight, taps_all, residue, decay, skip_all,
    turned_weight, got_weight, got_square, scaled, part, part_send0, part_send1, part_got0, part_got1, tokens, table,
    gather, reach, taps, skip, carried, query, state, conv, ready,
    in_sem, w_send, w_recv, t_send, t_recv, u_send, u_recv, s_send, s_recv, p_send, p_recv, o_send, o_recv,
):
    f32, bf16 = jnp.float32, jnp.bfloat16
    i, c = lax.axis_index("ctx"), lax.axis_index("chan")
    plane, place = i // PLANE, i % PLANE

    loads = [
        pltpu.make_async_copy(src, dst, in_sem.at[n])
        for n, (src, dst) in enumerate(
            (
                (weight_hbm, weight), (tok_hbm, tok), (embed_hbm, embed), (gain_hbm, gain),
                (taps_hbm, taps_all), (residue_hbm, residue), (decay_hbm, decay), (skip_hbm, skip_all),
            )
        )
    ]
    for load in loads:
        load.start()

    barrier = pltpu.get_barrier_semaphore()

    @pl.loop(0, CTX)
    def _(j):
        row, col = c * PLANE + j % PLANE, j // PLANE

        @pl.when(jnp.logical_or(row != i, col != c))
        def _():
            pl.semaphore_signal(barrier, inc=1, device_id=(row, col), device_id_type=MESH)

    for d in range(1, CHAN):
        pl.semaphore_signal(barrier, inc=1, device_id=(i, (c + d) % CHAN), device_id_type=MESH)

    loads[0].wait()
    eights = [jnp.transpose(weight[b].astype(f32)).reshape(CTX, 2, FEW, HALF) for b in range(3)]
    order = ((0, 0), (1, 0), (2, 0), (1, 1), (0, 1), (2, 1))
    rows = jnp.concatenate([eights[b][:, part : part + 1] for b, part in order], axis=1)
    turned_weight[...] = rows.reshape(turned_weight.shape).astype(bf16)
    loads[1].wait()
    own_tokens[...] = tok[...].reshape(1, tok.shape[0])

    pl.semaphore_wait(barrier, CTX - jnp.where(plane == c, 1, 0) + CHAN - 1)

    def weight_slices(h, to, slot):
        rows = pl.ds(*WEIGHT_ROWS[h])
        lanes = pl.ds(pl.multiple_of(slot % PLANE * HALF, HALF), HALF)
        return turned_weight.at[to, rows, :], got_weight.at[slot // PLANE, rows, lanes], w_recv.at[h]

    def weight_copy(h, j):
        to = (i + j) % CTX
        src, dst, sem = weight_slices(h, to, c * PLANE + place)
        return send(src, dst, w_send.at[h], sem, to, plane)

    def start_weights(h):
        @pl.loop(1, CTX)
        def _(j):
            weight_copy(h, j).start()

        @pl.when(plane == c)
        def _():
            pltpu.make_async_copy(*weight_slices(h, i, c * PLANE + place)).start()

        @pl.when(plane != c)
        def _():
            weight_copy(h, 0).start()

    def wait_for(region, sem):
        pltpu.make_async_copy(region, region, sem).wait()

    def wait_weights(h):
        wait_for(got_weight.at[:, pl.ds(*WEIGHT_ROWS[h]), :], w_recv.at[h])

    def token_copy(n):
        to = c * PLANE + (place + n) % PLANE
        return send(own_tokens, tokens.at[i], t_send, t_recv, to, plane)

    own_token_copy = pltpu.make_async_copy(own_tokens, tokens.at[i], t_recv)

    @pl.when(plane == c)
    def _():
        own_token_copy.start()

    @pl.when(plane != c)
    def _():
        token_copy(0).start()

    @pl.loop(1, PLANE)
    def _(n):
        token_copy(n).start()

    start_weights(0)

    loads[2].wait()
    loads[3].wait()
    wide = embed[...].astype(f32)
    feats = embed.shape[1]
    square_high, square_low = high_low(wide * wide)
    ones = jnp.ones((8, feats), bf16)
    squares = lax.dot_general(ones, square_high, NT, preferred_element_type=f32)
    got_square[c] = squares + lax.dot_general(ones, square_low, NT, preferred_element_type=f32)

    wait_for(tokens.at[pl.ds(c * PLANE, PLANE)], t_recv)

    def plane_copy(source, to, d):
        block = tokens.at[pl.ds(source * PLANE, PLANE)]
        return send(block, block, u_send.at[d], u_recv.at[source], i, to)

    for d in range(1, CHAN):
        plane_copy(c, (c + d) % CHAN, d).start()

    def square_copy(d):
        return send(got_square.at[c], got_square.at[c], s_send.at[d], s_recv.at[c], i, (c + d) % CHAN)

    for d in range(1, CHAN):
        square_copy(d).start()
    scaled[...] = (wide * gain[pl.ds(c * feats, feats)].reshape(1, feats)).astype(bf16)

    start_weights(1)
    near, far = (c // 2) * 2, 2 - (c // 2) * 2
    other = c + 1 - 2 * (c % 2)
    part_send, part_got = (part_send0, part_send1), (part_got0, part_got1)

    def part_copy(h, to, d):
        return send(part_send[h].at[to], part_got[h].at[c], p_send.at[h, d], p_recv.at[h, c], i, to)

    def products(h, first):
        top, count = WEIGHT_ROWS[h]
        weights = got_weight[pl.ds(first, 2), pl.ds(top, count), :].reshape(2 * count, feats)
        product = lax.dot_general(weights, scaled[...], NT, preferred_element_type=f32)
        return product.reshape(2, count, product.shape[1])

    def start_parts(h):
        top, count = WEIGHT_ROWS[h]
        part_send[h][pl.ds(far, 2)] = products(h, far).astype(bf16)
        part_copy(h, far, 0).start()
        part_copy(h, far + 1, 1).start()
        product = products(h, near)
        part[:, top : top + count, :] = product
        part_send[h][pl.ds(near, 2)] = product.astype(bf16)
        part_copy(h, other, 2).start()

    def finish_parts(h, scale):
        top, count = WEIGHT_ROWS[h]
        total = part[c % 2, top : top + count, :]
        for d in range(1, CHAN):
            source = (c + d) % CHAN
            send(
                part_send[h].at[0], part_got[h].at[source], p_send.at[h, d], p_recv.at[h, source], i, source
            ).wait_recv()
            total = total + part_got[h][source].astype(f32)
        table[top : top + count, :] = (total * scale).astype(bf16).astype(f32)

    def branches_of(h):
        rows = jnp.concatenate([table[top : top + FEW, :] for top in TABLE_ROWS[h]], axis=0)
        quarters = jnp.concatenate([rows[:, n * HALF : (n + 1) * HALF] for n in range(4)], axis=0)
        short_filter_and_gate(quarters.astype(bf16), tokens, taps.at[h], carried.at[h], query.at[h])

    def out_slot(h, source):
        return got_ref.at[h, :, pl.ds(pl.multiple_of(source * OWN, OWN), OWN), :], o_recv.at[h]

    def out_copy(h, to):
        dst, sem = out_slot(h, i)
        return send(ready.at[h, to], dst, o_send.at[h], sem, to, c)

    def start_outputs(h, decay_row):
        segment_states(carried.at[h], gather.at[h], decay_row[:, h * FEWS : (h + 1) * FEWS], state.at[h])

        inside_segments(carried.at[h], reach.at[h], conv)

        @pl.loop(0, CTX // PLANE)
        def _(step):
            q = (plane + 1 + step) % (CTX // PLANE)
            outputs_of_part(
                q, carried.at[h], query.at[h], state.at[h], conv, reach.at[h], skip.at[h], ready.at[h]
            )

            @pl.loop(0, PLANE)
            def _(n):
                to = q * PLANE + (place + n) % PLANE

                @pl.when(to != i)
                def _():
                    out_copy(h, to).start()

                @pl.when(to == i)
                def _():
                    pltpu.make_async_copy(ready.at[h, to], *out_slot(h, i)).start()

    wait_weights(0)
    start_parts(0)

    for load in loads[4:]:
        load.wait()
    lanes_from = pl.multiple_of((i // PLANE) * HALF, HALF)
    shift = lax.rem(HALF - place * OWN, HALF)
    decay_own, residue_own = load_own([decay, residue], lanes_from, shift)
    weight_own = residue_own * jnp.sqrt(decay_own)
    decay_row = filter_tables(decay_own, weight_own, gather, reach)
    for j in range(3):
        (rows,) = load_own([taps_all.at[j]], lanes_from, shift)
        padded = jnp.concatenate([rows, jnp.zeros((5, HALF), f32)], axis=0)
        columns = jnp.transpose(padded)[:OWN]
        for b in range(3):
            wide_column = jnp.broadcast_to(columns[:, b : b + 1], (OWN, HALF))
            for h in range(2):
                taps[h, j, b * FEW : (b + 1) * FEW, :] = wide_column[h * FEW : (h + 1) * FEW]
    skip_row = pltpu.roll(
        jnp.broadcast_to(skip_all[pl.ds(lanes_from, HALF)].reshape(1, HALF), (8, HALF)), shift, axis=1
    )
    skip_column = jnp.transpose(skip_row)[:OWN, 0:1]
    skip[...] = jnp.broadcast_to(skip_column, (OWN, SEG)).reshape(2, FEW, SEG)

    wait_weights(1)
    start_parts(1)
    mean = got_square[c]
    for d in range(1, CHAN):
        source = (c + d) % CHAN
        send(got_square.at[c], got_square.at[source], s_send.at[d], s_recv.at[source], i, source).wait_recv()
        mean = mean + got_square[source]
    scale = lax.rsqrt(mean[0:1] * (1.0 / (CHAN * feats)) + EPS)
    for d in range(1, CHAN):
        plane_copy((c + d) % CHAN, c, d).wait_recv()
    finish_parts(0, scale)
    branches_of(0)
    start_outputs(0, decay_row)
    finish_parts(1, scale)
    branches_of(1)
    start_outputs(1, decay_row)

    for h in range(2):
        wait_for(ready.at[h, pl.ds(0, CTX - 1)], o_send.at[h])
        part_copy(h, far, 0).wait_send()
        part_copy(h, far + 1, 1).wait_send()
        part_copy(h, other, 2).wait_send()

    def wait_sends(skipped):
        for h in range(2):
            rows = pl.ds(*WEIGHT_ROWS[h])
            wait_for(turned_weight.at[pl.ds(0, CTX - skipped), rows, :], w_send.at[h])
        wait_for(tokens.at[pl.ds(0, PLANE - skipped)], t_send)

    @pl.when(plane != c)
    def _():
        wait_sends(0)

    @pl.when(plane == c)
    def _():
        wait_sends(1)

    for d in range(1, CHAN):
        square_copy(d).wait_send()
        plane_copy(c, (c + d) % CHAN, d).wait_send()
    for h in range(2):
        wait_for(got_ref.at[h], o_recv.at[h])


def gathered(
    token_ids, embed_table, norm_gain, in_weight, short_filter, residue, decay_rate, skip_bias
):
    f32, bf16 = jnp.float32, jnp.bfloat16
    rows = token_ids.shape[0]
    vocab, feats = embed_table.shape
    chans = decay_rate.shape[1]
    weight = jnp.transpose(in_weight, (1, 0, 2))
    operands = (token_ids, embed_table, norm_gain, weight, short_filter, residue, decay_rate, skip_bias)
    dma, vmem = pltpu.SemaphoreType.DMA, pltpu.VMEM
    return pl.pallas_call(
        main_kernel,
        name="hyena",
        out_shape=pltpu.VMEM((2, PER, CTX * OWN, HALF), bf16),
        in_specs=[pl.BlockSpec(memory_space=pl.ANY)] * len(operands),
        out_specs=pl.BlockSpec(memory_space=pl.ANY),
        scratch_shapes=[
            vmem(token_ids.shape, jnp.int32),
            vmem((1, rows), jnp.int32),
            vmem(embed_table.shape, bf16),
            vmem(norm_gain.shape, f32),
            vmem(weight.shape, bf16),
            vmem(short_filter.shape, f32),
            vmem(residue.shape, f32),
            vmem(decay_rate.shape, f32),
            vmem(skip_bias.shape, f32),
            vmem((CTX, 3 * OWN, in_weight.shape[0]), bf16),
            vmem((CHAN, 3 * OWN, feats), bf16),
            vmem((CHAN, 8, vocab), f32),
            vmem((vocab, feats), bf16),
            vmem((2, 3 * OWN, vocab), f32),
            vmem((CHAN, WEIGHT_ROWS[0][1], vocab), bf16),
            vmem((CHAN, WEIGHT_ROWS[1][1], vocab), bf16),
            vmem((CHAN, WEIGHT_ROWS[0][1], vocab), bf16),
            vmem((CHAN, WEIGHT_ROWS[1][1], vocab), bf16),
            vmem((CTX, 1, rows), jnp.int32),
            vmem((3 * OWN, vocab), f32),
            vmem((2, SEG, 2 * FEWS), bf16),
            vmem((2, FEW * SEG + 3 * FEWS, SEG), bf16),
            vmem((2, 3, 3 * FEW, HALF), f32),
            vmem((2, FEW, SEG), f32),
            vmem((2, 2, SEGS * FEW, HALF), f32),
            vmem((2, 2, SEGS * FEW, HALF), f32),
            vmem((2, SEGS, FEWS), f32),
            vmem((2, SEGS * FEW, HALF), f32),
            vmem((2, CTX, PER, 2 * FEW, HALF), bf16),
            dma((8,)),
            dma((2,)), dma((2,)), dma(()), dma(()),
            dma((CHAN,)), dma((CHAN,)), dma((CHAN,)), dma((CHAN,)), dma((2, CHAN)), dma((2, CHAN)),
            dma((2,)), dma((2,)),
        ],
        compiler_params=pltpu.CompilerParams(
            collective_id=0, has_side_effects=True, vmem_limit_bytes=VMEM_LIMIT
        ),
    )(*operands)


def turn_kernel(got, out_hbm, out, out_sem):
    f32, bf16 = jnp.float32, jnp.bfloat16
    unit = (
        lax.broadcasted_iota(jnp.int32, (HALF, HALF), 0) == lax.broadcasted_iota(jnp.int32, (HALF, HALF), 1)
    ).astype(bf16)
    stores = []
    for g in range(PER):
        eights = [got[h, g].astype(f32).reshape(CTX, 2, FEW, HALF) for h in range(2)]
        for half in range(2):
            rows = jnp.concatenate([eights[h][:, half : half + 1] for h in range(2)], axis=1)
            rows = rows.reshape(CTX * OWN, HALF).astype(bf16)
            top = g * SEG + half * HALF
            turned = lax.dot_general(unit, rows, NT, preferred_element_type=f32)
            out[top : top + HALF, :] = turned.astype(bf16)
        rows = pl.ds(g * SEG, SEG)
        stores.append(pltpu.make_async_copy(out.at[rows, :], out_hbm.at[rows, :], out_sem.at[g]))
        stores[g].start()
    for store in stores:
        store.wait()


def turned(got):
    bf16 = jnp.bfloat16
    shape = (PER * SEG, CTX * OWN)
    return pl.pallas_call(
        turn_kernel,
        name="turn",
        out_shape=jax.ShapeDtypeStruct(shape, bf16),
        in_specs=[pl.BlockSpec(memory_space=pltpu.VMEM)],
        out_specs=pl.BlockSpec(memory_space=pl.ANY),
        scratch_shapes=[pltpu.VMEM(shape, bf16), pltpu.SemaphoreType.DMA((PER,))],
        compiler_params=pltpu.CompilerParams(vmem_limit_bytes=TURN_LIMIT),
    )(got)


def per_device(*arrays):
    return turned(gathered(*arrays))


def solution(mesh):
    return jax.shard_map(
        per_device,
        mesh=mesh,
        in_specs=(
            P("ctx"),
            P(None, "chan"),
            P(),
            P("ctx", None, "chan"),
            P(None, None, "chan"),
            P(None, "chan"),
            P(None, "chan"),
            P("chan"),
        ),
        out_specs=P("ctx", "chan"),
        check_vma=False,
    )
```

```python
import functools

import jax
import jax.numpy as jnp
from jax import lax
from jax.experimental import pallas as pl
from jax.experimental.pallas import tpu as pltpu
from jax.sharding import PartitionSpec as P

MESH = pl.DeviceIdType.MESH
EPS = 1e-06
VMEM_LIMIT = 56 * 1024 * 1024
TURN_LIMIT = 16 * 1024 * 1024

CTX, CHAN, PLANE = 32, 4, 8
OWN = 16
SEG = 256
SEGS = 96
PER = 3
PART = 24
HALF = 128
MODES = 16
PAIRS = OWN * MODES
FEW = 8
FEWS = FEW * MODES
WEIGHT_ROWS = ((0, 32), (32, 16))
TABLE_ROWS = ((0, 8, 16), (32, 24, 40))
NT = (((1,), (1,)), ((), ()))
HIGHEST = lax.Precision.HIGHEST


def dot(a, b):
    return jnp.dot(a, b, preferred_element_type=jnp.float32)


def high_low(x):
    high = x.astype(jnp.bfloat16)
    return high, (x - high.astype(jnp.float32)).astype(jnp.bfloat16)


def send(src, dst, send_sem, recv_sem, i, c):
    return pltpu.make_async_remote_copy(
        src_ref=src, dst_ref=dst, send_sem=send_sem, recv_sem=recv_sem, device_id=(i, c), device_id_type=MESH
    )


def load_own(row_refs, lanes_from, shift):
    rows = [ref[:, pl.ds(lanes_from, HALF)] for ref in row_refs]
    return [pltpu.roll(array, shift, axis=1) for array in rows]


def filter_tables(decay, weight, gather, reach):
    f32, bf16 = jnp.float32, jnp.bfloat16
    decay_turned = jnp.transpose(decay)[:OWN]
    weight_turned = jnp.transpose(weight)[:OWN]
    lane = lax.broadcasted_iota(jnp.int32, (OWN, HALF), 1).astype(f32)
    near = jnp.zeros((OWN, HALF), f32)
    far = jnp.zeros((OWN, HALF), f32)
    for m in range(MODES):
        rate = jnp.broadcast_to(decay_turned[:, m : m + 1], (OWN, HALF))
        height = jnp.broadcast_to(weight_turned[:, m : m + 1], (OWN, HALF))
        near = near + height * jnp.exp(-rate * lane)
        far = far + height * jnp.exp(-rate * (lane + float(HALF)))
    causal = lax.broadcasted_iota(jnp.int32, (HALF, HALF), 1) >= lax.broadcasted_iota(jnp.int32, (HALF, HALF), 0)
    for ch in range(OWN):
        near_rolled = pltpu.roll(
            jnp.broadcast_to(near[ch : ch + 1], (HALF, HALF)), 0, axis=1, stride=1, stride_axis=0
        )
        far_rolled = pltpu.roll(
            jnp.broadcast_to(far[ch : ch + 1], (HALF, HALF)), 0, axis=1, stride=1, stride_axis=0
        )
        diagonal = jnp.where(causal, near_rolled, 0.0).astype(bf16)
        part, top = ch // FEW, ch % FEW * SEG
        middle, end = top + HALF, top + SEG
        reach[part, top:middle, :HALF] = diagonal
        reach[part, middle:end, HALF:] = diagonal
        reach[part, top:middle, HALF:] = jnp.where(causal, far_rolled, near_rolled).astype(bf16)
        reach[part, middle:end, :HALF] = jnp.zeros((HALF, HALF), bf16)

    pick = (
        lax.broadcasted_iota(jnp.int32, (HALF, PAIRS), 0)
        == lax.broadcasted_iota(jnp.int32, (HALF, PAIRS), 1) // MODES
    ).astype(f32)
    own_mode = (
        lax.broadcasted_iota(jnp.int32, (MODES, PAIRS), 0)
        == lax.broadcasted_iota(jnp.int32, (MODES, PAIRS), 1) % MODES
    )

    def pair_row(array):
        wide = jnp.dot(array, pick, precision=HIGHEST, preferred_element_type=f32)
        return jnp.sum(jnp.where(own_mode, wide, 0.0), axis=0, keepdims=True)

    decay_row = pair_row(decay)
    decay_column = jnp.transpose(jnp.broadcast_to(decay_row, (HALF, PAIRS)))
    weight_column = jnp.transpose(jnp.broadcast_to(pair_row(weight), (HALF, PAIRS)))
    to_end = (SEG - 1 - lax.broadcasted_iota(jnp.int32, (SEG, PAIRS), 0)).astype(f32)
    entering = high_low(jnp.exp(-decay_row * to_end))
    for part in range(2):
        for n in range(2):
            gather[part, :, n * FEWS : (n + 1) * FEWS] = entering[n][:, part * FEWS : (part + 1) * FEWS]
    for half in range(2):
        lanes = slice(half * HALF, (half + 1) * HALF)
        after = lax.broadcasted_iota(jnp.int32, (PAIRS, HALF), 1).astype(f32) + float(half * HALF + 1)
        high, low = high_low(weight_column * jnp.exp(-decay_column * after))
        for part in range(2):
            rows = slice(part * FEWS, (part + 1) * FEWS)
            for n, piece in enumerate((high, high, low)):
                top = FEW * SEG + n * FEWS
                reach[part, top : top + FEWS, lanes] = piece[rows]
    return decay_row


def short_filter_and_gate(table, tokens_ref, taps_ref, carried_ref, query_ref):
    f32, bf16 = jnp.float32, jnp.bfloat16
    rows = 3 * FEW
    entry = lax.broadcasted_iota(jnp.int32, (HALF, SEG), 0).astype(f32).astype(bf16)
    lane = lax.broadcasted_iota(jnp.int32, (rows, HALF), 1)
    one, zero = jnp.ones((), bf16), jnp.zeros((), bf16)

    def block(g, before):
        for part in range(PER):
            ids = tokens_ref[g, :, part * SEG : (part + 1) * SEG]
            chosen = (ids & (HALF - 1)).astype(f32).astype(bf16)
            each = dot(table, jnp.where(entry == chosen, one, zero)).reshape(4, rows, SEG)
            odd, upper = (ids & HALF) != 0, (ids & SEG) != 0
            projected = jnp.where(upper, jnp.where(odd, each[3], each[2]), jnp.where(odd, each[1], each[0]))
            at = pl.ds(pl.multiple_of((g * PER + part) * FEW, FEW), FEW)
            for half in range(2):
                lanes = slice(half * HALF, (half + 1) * HALF)
                here = projected[:, lanes]
                turned = (pltpu.roll(here, 1, axis=1), pltpu.roll(here, 2, axis=1))
                branches = (
                    taps_ref[0] * here
                    + taps_ref[1] * jnp.where(lane < 1, before[0], turned[0])
                    + taps_ref[2] * jnp.where(lane < 2, before[1], turned[1])
                )
                before = turned
                carried = branches[FEW : 2 * FEW] * branches[2 * FEW :]
                carried_ref[half, at, :] = carried.astype(bf16).astype(f32)
                query_ref[half, at, :] = branches[:FEW]
        return before

    nothing = jnp.zeros((rows, HALF), f32)
    lax.fori_loop(0, SEGS // PER, block, (nothing, nothing), unroll=UNROLL)


UNROLL = 16


def both_halves(ref, rows):
    return jnp.concatenate([ref[half, rows, :] for half in range(2)], axis=1)


def own_pairs():
    shape = (1, FEW, FEWS)
    return lax.broadcasted_iota(jnp.int32, shape, 2) // MODES == lax.broadcasted_iota(jnp.int32, shape, 1)


def segment_states(carried_ref, gather, decay_row, state_ref):
    f32, bf16 = jnp.float32, jnp.bfloat16
    enters = dot(both_halves(carried_ref, slice(None)).astype(bf16), gather[...])
    enters = (enters[:, :FEWS] + enters[:, FEWS:]).reshape(SEGS, FEW, FEWS)
    added = jnp.sum(jnp.where(own_pairs(), enters, 0.0), axis=1)

    def later(x, by):
        return jnp.concatenate([jnp.zeros((by, FEWS), f32), x[: SEGS - by]], axis=0)

    state = later(added, 1)
    by = 1
    while by < SEGS:
        state = state + jnp.exp(-decay_row * float(SEG * by)) * later(state, by)
        by *= 2
    state_ref[...] = state


def inside_segments(carried_ref, reach, conv_ref):
    for ch in range(FEW):
        rows = pl.ds(ch, SEGS, stride=FEW)
        conv = dot(both_halves(carried_ref, rows).astype(jnp.bfloat16), reach[ch * SEG : (ch + 1) * SEG, :])
        for half in range(2):
            conv_ref[half, rows, :] = conv[:, half * HALF : (half + 1) * HALF]


def outputs_of_part(q, carried_ref, query_ref, state_ref, conv_ref, reach, skip_ref, ready):
    first = pl.multiple_of(q * PART, PART)
    rows = pl.ds(pl.multiple_of(first * FEW, FEW), PART * FEW)
    state = jnp.where(own_pairs(), state_ref[pl.ds(first, PART), :][:, None, :], 0.0)
    high, low = high_low(state.reshape(PART * FEW, FEWS))
    reached = dot(jnp.concatenate([high, low, high], axis=1), reach[FEW * SEG :, :])
    halves = []
    for half in range(2):
        lanes = slice(half * HALF, (half + 1) * HALF)
        carried = carried_ref[half, rows, :].reshape(PART, FEW, HALF)
        direct = (skip_ref[:, lanes][None] * carried).reshape(PART * FEW, HALF)
        gated = query_ref[half, rows, :] * (conv_ref[half, rows, :] + reached[:, lanes] + direct)
        halves.append(gated.reshape(PART, 1, FEW, HALF))
    block = jnp.concatenate(halves, axis=1).reshape(PLANE, PER, 2 * FEW, HALF)
    ready[pl.ds(q * PLANE, PLANE)] = block.astype(jnp.bfloat16)


def main_kernel(
    tok_hbm, embed_hbm, gain_hbm, weight_hbm, taps_hbm, residue_hbm, decay_hbm, skip_hbm, got_ref,
    tok, own_tokens, embed, gain, weight, taps_all, residue, decay, skip_all,
    turned_weight, got_weight, got_square, scaled, part, part_send0, part_send1, part_got0, part_got1, tokens, table,
    gather, reach, taps, skip, carried, query, state, conv, ready,
    in_sem, w_send, w_recv, t_send, t_recv, u_send, u_recv, s_send, s_recv, p_send, p_recv, o_send, o_recv,
):
    f32, bf16 = jnp.float32, jnp.bfloat16
    i, c = lax.axis_index("ctx"), lax.axis_index("chan")
    plane, place = i // PLANE, i % PLANE

    loads = [
        pltpu.make_async_copy(src, dst, in_sem.at[n])
        for n, (src, dst) in enumerate(
            (
                (weight_hbm, weight), (tok_hbm, tok), (embed_hbm, embed), (gain_hbm, gain),
                (taps_hbm, taps_all), (residue_hbm, residue), (decay_hbm, decay), (skip_hbm, skip_all),
            )
        )
    ]
    for load in loads:
        load.start()

    barrier = pltpu.get_barrier_semaphore()

    @pl.loop(0, CTX)
    def _(j):
        row, col = c * PLANE + j % PLANE, j // PLANE

        @pl.when(jnp.logical_or(row != i, col != c))
        def _():
            pl.semaphore_signal(barrier, inc=1, device_id=(row, col), device_id_type=MESH)

    for d in range(1, CHAN):
        pl.semaphore_signal(barrier, inc=1, device_id=(i, (c + d) % CHAN), device_id_type=MESH)

    loads[0].wait()
    eights = [jnp.transpose(weight[b].astype(f32)).reshape(CTX, 2, FEW, HALF) for b in range(3)]
    order = ((0, 0), (1, 0), (2, 0), (1, 1), (0, 1), (2, 1))
    rows = jnp.concatenate([eights[b][:, part : part + 1] for b, part in order], axis=1)
    turned_weight[...] = rows.reshape(turned_weight.shape).astype(bf16)
    loads[1].wait()
    own_tokens[...] = tok[...].reshape(1, tok.shape[0])

    pl.semaphore_wait(barrier, CTX - jnp.where(plane == c, 1, 0) + CHAN - 1)

    def weight_slices(h, to, slot):
        rows = pl.ds(*WEIGHT_ROWS[h])
        lanes = pl.ds(pl.multiple_of(slot % PLANE * HALF, HALF), HALF)
        return turned_weight.at[to, rows, :], got_weight.at[slot // PLANE, rows, lanes], w_recv.at[h]

    def weight_copy(h, j):
        to = (i + CTX - j) % CTX
        src, dst, sem = weight_slices(h, to, c * PLANE + place)
        return send(src, dst, w_send.at[h], sem, to, plane)

    def start_weights(h):
        @pl.loop(1, CTX)
        def _(j):
            weight_copy(h, j).start()

        @pl.when(plane == c)
        def _():
            pltpu.make_async_copy(*weight_slices(h, i, c * PLANE + place)).start()

        @pl.when(plane != c)
        def _():
            weight_copy(h, 0).start()

    def wait_for(region, sem):
        pltpu.make_async_copy(region, region, sem).wait()

    def wait_weights(h):
        wait_for(got_weight.at[:, pl.ds(*WEIGHT_ROWS[h]), :], w_recv.at[h])

    def token_copy(n):
        to = c * PLANE + (place + n) % PLANE
        return send(own_tokens, tokens.at[i], t_send, t_recv, to, plane)

    own_token_copy = pltpu.make_async_copy(own_tokens, tokens.at[i], t_recv)

    @pl.when(plane == c)
    def _():
        own_token_copy.start()

    @pl.when(plane != c)
    def _():
        token_copy(0).start()

    @pl.loop(1, PLANE)
    def _(n):
        token_copy(n).start()

    start_weights(0)

    loads[2].wait()
    loads[3].wait()
    wide = embed[...].astype(f32)
    feats = embed.shape[1]
    square_high, square_low = high_low(wide * wide)
    ones = jnp.ones((8, feats), bf16)
    squares = lax.dot_general(ones, square_high, NT, preferred_element_type=f32)
    got_square[c] = squares + lax.dot_general(ones, square_low, NT, preferred_element_type=f32)

    wait_for(tokens.at[pl.ds(c * PLANE, PLANE)], t_recv)

    def plane_copy(source, to, d):
        block = tokens.at[pl.ds(source * PLANE, PLANE)]
        return send(block, block, u_send.at[d], u_recv.at[source], i, to)

    for d in range(1, CHAN):
        plane_copy(c, (c + d) % CHAN, d).start()

    def square_copy(d):
        return send(got_square.at[c], got_square.at[c], s_send.at[d], s_recv.at[c], i, (c + d) % CHAN)

    for d in range(1, CHAN):
        square_copy(d).start()
    scaled[...] = (wide * gain[pl.ds(c * feats, feats)].reshape(1, feats)).astype(bf16)

    start_weights(1)
    near, far = (c // 2) * 2, 2 - (c // 2) * 2
    other = c + 1 - 2 * (c % 2)
    part_send, part_got = (part_send0, part_send1), (part_got0, part_got1)

    def part_copy(h, to, d):
        return send(part_send[h].at[to], part_got[h].at[c], p_send.at[h, d], p_recv.at[h, c], i, to)

    def products(h, first):
        top, count = WEIGHT_ROWS[h]
        weights = got_weight[pl.ds(first, 2), pl.ds(top, count), :].reshape(2 * count, feats)
        product = lax.dot_general(weights, scaled[...], NT, preferred_element_type=f32)
        return product.reshape(2, count, product.shape[1])

    def start_parts(h):
        top, count = WEIGHT_ROWS[h]
        part_send[h][pl.ds(far, 2)] = products(h, far).astype(bf16)
        part_copy(h, far, 0).start()
        part_copy(h, far + 1, 1).start()
        product = products(h, near)
        part[:, top : top + count, :] = product
        part_send[h][pl.ds(near, 2)] = product.astype(bf16)
        part_copy(h, other, 2).start()

    def finish_parts(h, scale):
        top, count = WEIGHT_ROWS[h]
        total = part[c % 2, top : top + count, :]
        for d in range(1, CHAN):
            source = (c + d) % CHAN
            send(
                part_send[h].at[0], part_got[h].at[source], p_send.at[h, d], p_recv.at[h, source], i, source
            ).wait_recv()
            total = total + part_got[h][source].astype(f32)
        table[top : top + count, :] = (total * scale).astype(bf16).astype(f32)

    def branches_of(h):
        rows = jnp.concatenate([table[top : top + FEW, :] for top in TABLE_ROWS[h]], axis=0)
        quarters = jnp.concatenate([rows[:, n * HALF : (n + 1) * HALF] for n in range(4)], axis=0)
        short_filter_and_gate(quarters.astype(bf16), tokens, taps.at[h], carried.at[h], query.at[h])

    def out_slot(h, source):
        return got_ref.at[h, :, pl.ds(pl.multiple_of(source * OWN, OWN), OWN), :], o_recv.at[h]

    def out_copy(h, to):
        dst, sem = out_slot(h, i)
        return send(ready.at[h, to], dst, o_send.at[h], sem, to, c)

    def start_outputs(h, decay_row):
        segment_states(carried.at[h], gather.at[h], decay_row[:, h * FEWS : (h + 1) * FEWS], state.at[h])

        inside_segments(carried.at[h], reach.at[h], conv)

        @pl.loop(0, CTX // PLANE)
        def _(step):
            q = (plane + 1 + step) % (CTX // PLANE)
            outputs_of_part(
                q, carried.at[h], query.at[h], state.at[h], conv, reach.at[h], skip.at[h], ready.at[h]
            )

            @pl.loop(0, PLANE)
            def _(n):
                to = q * PLANE + (place + n) % PLANE

                @pl.when(to != i)
                def _():
                    out_copy(h, to).start()

                @pl.when(to == i)
                def _():
                    pltpu.make_async_copy(ready.at[h, to], *out_slot(h, i)).start()

    wait_weights(0)
    start_parts(0)

    for load in loads[4:]:
        load.wait()
    lanes_from = pl.multiple_of((i // PLANE) * HALF, HALF)
    shift = lax.rem(HALF - place * OWN, HALF)
    decay_own, residue_own = load_own([decay, residue], lanes_from, shift)
    weight_own = residue_own * jnp.sqrt(decay_own)
    decay_row = filter_tables(decay_own, weight_own, gather, reach)
    for j in range(3):
        (rows,) = load_own([taps_all.at[j]], lanes_from, shift)
        padded = jnp.concatenate([rows, jnp.zeros((5, HALF), f32)], axis=0)
        columns = jnp.transpose(padded)[:OWN]
        for b in range(3):
            wide_column = jnp.broadcast_to(columns[:, b : b + 1], (OWN, HALF))
            for h in range(2):
                taps[h, j, b * FEW : (b + 1) * FEW, :] = wide_column[h * FEW : (h + 1) * FEW]
    skip_row = pltpu.roll(
        jnp.broadcast_to(skip_all[pl.ds(lanes_from, HALF)].reshape(1, HALF), (8, HALF)), shift, axis=1
    )
    skip_column = jnp.transpose(skip_row)[:OWN, 0:1]
    skip[...] = jnp.broadcast_to(skip_column, (OWN, SEG)).reshape(2, FEW, SEG)

    wait_weights(1)
    start_parts(1)
    mean = got_square[c]
    for d in range(1, CHAN):
        source = (c + d) % CHAN
        send(got_square.at[c], got_square.at[source], s_send.at[d], s_recv.at[source], i, source).wait_recv()
        mean = mean + got_square[source]
    scale = lax.rsqrt(mean[0:1] * (1.0 / (CHAN * feats)) + EPS)
    for d in range(1, CHAN):
        plane_copy((c + d) % CHAN, c, d).wait_recv()
    finish_parts(0, scale)
    branches_of(0)
    start_outputs(0, decay_row)
    finish_parts(1, scale)
    branches_of(1)
    start_outputs(1, decay_row)

    for h in range(2):
        wait_for(ready.at[h, pl.ds(0, CTX - 1)], o_send.at[h])
        part_copy(h, far, 0).wait_send()
        part_copy(h, far + 1, 1).wait_send()
        part_copy(h, other, 2).wait_send()

    def wait_sends(skipped):
        for h in range(2):
            rows = pl.ds(*WEIGHT_ROWS[h])
            wait_for(turned_weight.at[pl.ds(0, CTX - skipped), rows, :], w_send.at[h])
        wait_for(tokens.at[pl.ds(0, PLANE - skipped)], t_send)

    @pl.when(plane != c)
    def _():
        wait_sends(0)

    @pl.when(plane == c)
    def _():
        wait_sends(1)

    for d in range(1, CHAN):
        square_copy(d).wait_send()
        plane_copy(c, (c + d) % CHAN, d).wait_send()
    for h in range(2):
        wait_for(got_ref.at[h], o_recv.at[h])


def gathered(
    token_ids, embed_table, norm_gain, in_weight, short_filter, residue, decay_rate, skip_bias
):
    f32, bf16 = jnp.float32, jnp.bfloat16
    rows = token_ids.shape[0]
    vocab, feats = embed_table.shape
    chans = decay_rate.shape[1]
    weight = jnp.transpose(in_weight, (1, 0, 2))
    operands = (token_ids, embed_table, norm_gain, weight, short_filter, residue, decay_rate, skip_bias)
    dma, vmem = pltpu.SemaphoreType.DMA, pltpu.VMEM
    return pl.pallas_call(
        main_kernel,
        name="hyena",
        out_shape=pltpu.VMEM((2, PER, CTX * OWN, HALF), bf16),
        in_specs=[pl.BlockSpec(memory_space=pl.ANY)] * len(operands),
        out_specs=pl.BlockSpec(memory_space=pl.ANY),
        scratch_shapes=[
            vmem(token_ids.shape, jnp.int32),
            vmem((1, rows), jnp.int32),
            vmem(embed_table.shape, bf16),
            vmem(norm_gain.shape, f32),
            vmem(weight.shape, bf16),
            vmem(short_filter.shape, f32),
            vmem(residue.shape, f32),
            vmem(decay_rate.shape, f32),
            vmem(skip_bias.shape, f32),
            vmem((CTX, 3 * OWN, in_weight.shape[0]), bf16),
            vmem((CHAN, 3 * OWN, feats), bf16),
            vmem((CHAN, 8, vocab), f32),
            vmem((vocab, feats), bf16),
            vmem((2, 3 * OWN, vocab), f32),
            vmem((CHAN, WEIGHT_ROWS[0][1], vocab), bf16),
            vmem((CHAN, WEIGHT_ROWS[1][1], vocab), bf16),
            vmem((CHAN, WEIGHT_ROWS[0][1], vocab), bf16),
            vmem((CHAN, WEIGHT_ROWS[1][1], vocab), bf16),
            vmem((CTX, 1, rows), jnp.int32),
            vmem((3 * OWN, vocab), f32),
            vmem((2, SEG, 2 * FEWS), bf16),
            vmem((2, FEW * SEG + 3 * FEWS, SEG), bf16),
            vmem((2, 3, 3 * FEW, HALF), f32),
            vmem((2, FEW, SEG), f32),
            vmem((2, 2, SEGS * FEW, HALF), f32),
            vmem((2, 2, SEGS * FEW, HALF), f32),
            vmem((2, SEGS, FEWS), f32),
            vmem((2, SEGS * FEW, HALF), f32),
            vmem((2, CTX, PER, 2 * FEW, HALF), bf16),
            dma((8,)),
            dma((2,)), dma((2,)), dma(()), dma(()),
            dma((CHAN,)), dma((CHAN,)), dma((CHAN,)), dma((CHAN,)), dma((2, CHAN)), dma((2, CHAN)),
            dma((2,)), dma((2,)),
        ],
        compiler_params=pltpu.CompilerParams(
            collective_id=0, has_side_effects=True, vmem_limit_bytes=VMEM_LIMIT
        ),
    )(*operands)


def turn_kernel(got, out_hbm, out, out_sem):
    f32, bf16 = jnp.float32, jnp.bfloat16
    unit = (
        lax.broadcasted_iota(jnp.int32, (HALF, HALF), 0) == lax.broadcasted_iota(jnp.int32, (HALF, HALF), 1)
    ).astype(bf16)
    stores = []
    for g in range(PER):
        eights = [got[h, g].astype(f32).reshape(CTX, 2, FEW, HALF) for h in range(2)]
        for half in range(2):
            rows = jnp.concatenate([eights[h][:, half : half + 1] for h in range(2)], axis=1)
            rows = rows.reshape(CTX * OWN, HALF).astype(bf16)
            top = g * SEG + half * HALF
            turned = lax.dot_general(unit, rows, NT, preferred_element_type=f32)
            out[top : top + HALF, :] = turned.astype(bf16)
        rows = pl.ds(g * SEG, SEG)
        stores.append(pltpu.make_async_copy(out.at[rows, :], out_hbm.at[rows, :], out_sem.at[g]))
        stores[g].start()
    for store in stores:
        store.wait()


def turned(got):
    bf16 = jnp.bfloat16
    shape = (PER * SEG, CTX * OWN)
    return pl.pallas_call(
        turn_kernel,
        name="turn",
        out_shape=jax.ShapeDtypeStruct(shape, bf16),
        in_specs=[pl.BlockSpec(memory_space=pltpu.VMEM)],
        out_specs=pl.BlockSpec(memory_space=pl.ANY),
        scratch_shapes=[pltpu.VMEM(shape, bf16), pltpu.SemaphoreType.DMA((PER,))],
        compiler_params=pltpu.CompilerParams(vmem_limit_bytes=TURN_LIMIT),
    )(got)


def per_device(*arrays):
    return turned(gathered(*arrays))


def solution(mesh):
    return jax.shard_map(
        per_device,
        mesh=mesh,
        in_specs=(
            P("ctx"),
            P(None, "chan"),
            P(),
            P("ctx", None, "chan"),
            P(None, None, "chan"),
            P(None, "chan"),
            P(None, "chan"),
            P("chan"),
        ),
        out_specs=P("ctx", "chan"),
        check_vma=False,
    )
```

```python
import functools

import jax
import jax.numpy as jnp
from jax import lax
from jax.experimental import pallas as pl
from jax.experimental.pallas import tpu as pltpu
from jax.sharding import PartitionSpec as P

MESH = pl.DeviceIdType.MESH
EPS = 1e-06
VMEM_LIMIT = 56 * 1024 * 1024
TURN_LIMIT = 16 * 1024 * 1024

CTX, CHAN, PLANE = 32, 4, 8
OWN = 16
SEG = 256
SEGS = 96
PER = 3
PART = 24
HALF = 128
MODES = 16
PAIRS = OWN * MODES
FEW = 8
FEWS = FEW * MODES
WEIGHT_ROWS = ((0, 32), (32, 16))
TABLE_ROWS = ((0, 8, 16), (32, 24, 40))
NT = (((1,), (1,)), ((), ()))
HIGHEST = lax.Precision.HIGHEST


def dot(a, b):
    return jnp.dot(a, b, preferred_element_type=jnp.float32)


def high_low(x):
    high = x.astype(jnp.bfloat16)
    return high, (x - high.astype(jnp.float32)).astype(jnp.bfloat16)


def send(src, dst, send_sem, recv_sem, i, c):
    return pltpu.make_async_remote_copy(
        src_ref=src, dst_ref=dst, send_sem=send_sem, recv_sem=recv_sem, device_id=(i, c), device_id_type=MESH
    )


def load_own(row_refs, lanes_from, shift):
    rows = [ref[:, pl.ds(lanes_from, HALF)] for ref in row_refs]
    return [pltpu.roll(array, shift, axis=1) for array in rows]


def filter_tables(decay, weight, gather, reach):
    f32, bf16 = jnp.float32, jnp.bfloat16
    decay_turned = jnp.transpose(decay)[:OWN]
    weight_turned = jnp.transpose(weight)[:OWN]
    lane = lax.broadcasted_iota(jnp.int32, (OWN, HALF), 1).astype(f32)
    near = jnp.zeros((OWN, HALF), f32)
    far = jnp.zeros((OWN, HALF), f32)
    for m in range(MODES):
        rate = jnp.broadcast_to(decay_turned[:, m : m + 1], (OWN, HALF))
        height = jnp.broadcast_to(weight_turned[:, m : m + 1], (OWN, HALF))
        near = near + height * jnp.exp(-rate * lane)
        far = far + height * jnp.exp(-rate * (lane + float(HALF)))
    causal = lax.broadcasted_iota(jnp.int32, (HALF, HALF), 1) >= lax.broadcasted_iota(jnp.int32, (HALF, HALF), 0)
    for ch in range(OWN):
        near_rolled = pltpu.roll(
            jnp.broadcast_to(near[ch : ch + 1], (HALF, HALF)), 0, axis=1, stride=1, stride_axis=0
        )
        far_rolled = pltpu.roll(
            jnp.broadcast_to(far[ch : ch + 1], (HALF, HALF)), 0, axis=1, stride=1, stride_axis=0
        )
        diagonal = jnp.where(causal, near_rolled, 0.0).astype(bf16)
        part, top = ch // FEW, ch % FEW * SEG
        middle, end = top + HALF, top + SEG
        reach[part, top:middle, :HALF] = diagonal
        reach[part, middle:end, HALF:] = diagonal
        reach[part, top:middle, HALF:] = jnp.where(causal, far_rolled, near_rolled).astype(bf16)
        reach[part, middle:end, :HALF] = jnp.zeros((HALF, HALF), bf16)

    pick = (
        lax.broadcasted_iota(jnp.int32, (HALF, PAIRS), 0)
        == lax.broadcasted_iota(jnp.int32, (HALF, PAIRS), 1) // MODES
    ).astype(f32)
    own_mode = (
        lax.broadcasted_iota(jnp.int32, (MODES, PAIRS), 0)
        == lax.broadcasted_iota(jnp.int32, (MODES, PAIRS), 1) % MODES
    )

    def pair_row(array):
        wide = jnp.dot(array, pick, precision=HIGHEST, preferred_element_type=f32)
        return jnp.sum(jnp.where(own_mode, wide, 0.0), axis=0, keepdims=True)

    decay_row = pair_row(decay)
    decay_column = jnp.transpose(jnp.broadcast_to(decay_row, (HALF, PAIRS)))
    weight_column = jnp.transpose(jnp.broadcast_to(pair_row(weight), (HALF, PAIRS)))
    to_end = (SEG - 1 - lax.broadcasted_iota(jnp.int32, (SEG, PAIRS), 0)).astype(f32)
    entering = high_low(jnp.exp(-decay_row * to_end))
    for part in range(2):
        for n in range(2):
            gather[part, :, n * FEWS : (n + 1) * FEWS] = entering[n][:, part * FEWS : (part + 1) * FEWS]
    for half in range(2):
        lanes = slice(half * HALF, (half + 1) * HALF)
        after = lax.broadcasted_iota(jnp.int32, (PAIRS, HALF), 1).astype(f32) + float(half * HALF + 1)
        high, low = high_low(weight_column * jnp.exp(-decay_column * after))
        for part in range(2):
            rows = slice(part * FEWS, (part + 1) * FEWS)
            for n, piece in enumerate((high, high, low)):
                top = FEW * SEG + n * FEWS
                reach[part, top : top + FEWS, lanes] = piece[rows]
    return decay_row


def short_filter_and_gate(table, tokens_ref, taps_ref, carried_ref, query_ref):
    f32, bf16 = jnp.float32, jnp.bfloat16
    rows = 3 * FEW
    entry = lax.broadcasted_iota(jnp.int32, (HALF, SEG), 0).astype(f32).astype(bf16)
    lane = lax.broadcasted_iota(jnp.int32, (rows, HALF), 1)
    one, zero = jnp.ones((), bf16), jnp.zeros((), bf16)

    def block(g, before):
        for part in range(PER):
            ids = tokens_ref[g, :, part * SEG : (part + 1) * SEG]
            chosen = (ids & (HALF - 1)).astype(f32).astype(bf16)
            each = dot(table, jnp.where(entry == chosen, one, zero)).reshape(4, rows, SEG)
            odd, upper = (ids & HALF) != 0, (ids & SEG) != 0
            projected = jnp.where(upper, jnp.where(odd, each[3], each[2]), jnp.where(odd, each[1], each[0]))
            at = pl.ds(pl.multiple_of((g * PER + part) * FEW, FEW), FEW)
            for half in range(2):
                lanes = slice(half * HALF, (half + 1) * HALF)
                here = projected[:, lanes]
                turned = (pltpu.roll(here, 1, axis=1), pltpu.roll(here, 2, axis=1))
                branches = (
                    taps_ref[0] * here
                    + taps_ref[1] * jnp.where(lane < 1, before[0], turned[0])
                    + taps_ref[2] * jnp.where(lane < 2, before[1], turned[1])
                )
                before = turned
                carried = branches[FEW : 2 * FEW] * branches[2 * FEW :]
                carried_ref[half, at, :] = carried.astype(bf16).astype(f32)
                query_ref[half, at, :] = branches[:FEW]
        return before

    nothing = jnp.zeros((rows, HALF), f32)
    lax.fori_loop(0, SEGS // PER, block, (nothing, nothing), unroll=UNROLL)


UNROLL = 16


def both_halves(ref, rows):
    return jnp.concatenate([ref[half, rows, :] for half in range(2)], axis=1)


def own_pairs():
    shape = (1, FEW, FEWS)
    return lax.broadcasted_iota(jnp.int32, shape, 2) // MODES == lax.broadcasted_iota(jnp.int32, shape, 1)


def segment_states(carried_ref, gather, decay_row, state_ref):
    f32, bf16 = jnp.float32, jnp.bfloat16
    enters = dot(both_halves(carried_ref, slice(None)).astype(bf16), gather[...])
    enters = (enters[:, :FEWS] + enters[:, FEWS:]).reshape(SEGS, FEW, FEWS)
    added = jnp.sum(jnp.where(own_pairs(), enters, 0.0), axis=1)

    def later(x, by):
        return jnp.concatenate([jnp.zeros((by, FEWS), f32), x[: SEGS - by]], axis=0)

    state = later(added, 1)
    by = 1
    while by < SEGS:
        state = state + jnp.exp(-decay_row * float(SEG * by)) * later(state, by)
        by *= 2
    state_ref[...] = state


def inside_segments(carried_ref, reach, conv_ref):
    for ch in range(FEW):
        rows = pl.ds(ch, SEGS, stride=FEW)
        conv = dot(both_halves(carried_ref, rows).astype(jnp.bfloat16), reach[ch * SEG : (ch + 1) * SEG, :])
        for half in range(2):
            conv_ref[half, rows, :] = conv[:, half * HALF : (half + 1) * HALF]


def outputs_of_part(q, carried_ref, query_ref, state_ref, conv_ref, reach, skip_ref, ready):
    first = pl.multiple_of(q * PART, PART)
    rows = pl.ds(pl.multiple_of(first * FEW, FEW), PART * FEW)
    state = jnp.where(own_pairs(), state_ref[pl.ds(first, PART), :][:, None, :], 0.0)
    high, low = high_low(state.reshape(PART * FEW, FEWS))
    reached = dot(jnp.concatenate([high, low, high], axis=1), reach[FEW * SEG :, :])
    halves = []
    for half in range(2):
        lanes = slice(half * HALF, (half + 1) * HALF)
        carried = carried_ref[half, rows, :].reshape(PART, FEW, HALF)
        direct = (skip_ref[:, lanes][None] * carried).reshape(PART * FEW, HALF)
        gated = query_ref[half, rows, :] * (conv_ref[half, rows, :] + reached[:, lanes] + direct)
        halves.append(gated.reshape(PART, 1, FEW, HALF))
    block = jnp.concatenate(halves, axis=1).reshape(PLANE, PER, 2 * FEW, HALF)
    ready[pl.ds(q * PLANE, PLANE)] = block.astype(jnp.bfloat16)


def main_kernel(
    tok_hbm, embed_hbm, gain_hbm, weight_hbm, taps_hbm, residue_hbm, decay_hbm, skip_hbm, got_ref,
    tok, own_tokens, embed, gain, weight, taps_all, residue, decay, skip_all,
    turned_weight, got_weight, got_square, scaled, part, part_send0, part_send1, part_got0, part_got1, tokens, table,
    gather, reach, taps, skip, carried, query, state, conv, ready,
    in_sem, w_send, w_recv, t_send, t_recv, u_send, u_recv, s_send, s_recv, p_send, p_recv, o_send, o_recv,
):
    f32, bf16 = jnp.float32, jnp.bfloat16
    i, c = lax.axis_index("ctx"), lax.axis_index("chan")
    plane, place = i // PLANE, i % PLANE

    loads = [
        pltpu.make_async_copy(src, dst, in_sem.at[n])
        for n, (src, dst) in enumerate(
            (
                (weight_hbm, weight), (tok_hbm, tok), (embed_hbm, embed), (gain_hbm, gain),
                (taps_hbm, taps_all), (residue_hbm, residue), (decay_hbm, decay), (skip_hbm, skip_all),
            )
        )
    ]
    for load in loads:
        load.start()

    barrier = pltpu.get_barrier_semaphore()

    @pl.loop(0, CTX)
    def _(j):
        row, col = c * PLANE + j % PLANE, j // PLANE

        @pl.when(jnp.logical_or(row != i, col != c))
        def _():
            pl.semaphore_signal(barrier, inc=1, device_id=(row, col), device_id_type=MESH)

    for d in range(1, CHAN):
        pl.semaphore_signal(barrier, inc=1, device_id=(i, (c + d) % CHAN), device_id_type=MESH)

    loads[0].wait()
    eights = [jnp.transpose(weight[b].astype(f32)).reshape(CTX, 2, FEW, HALF) for b in range(3)]
    order = ((0, 0), (1, 0), (2, 0), (1, 1), (0, 1), (2, 1))
    rows = jnp.concatenate([eights[b][:, part : part + 1] for b, part in order], axis=1)
    turned_weight[...] = rows.reshape(turned_weight.shape).astype(bf16)
    loads[1].wait()
    own_tokens[...] = tok[...].reshape(1, tok.shape[0])

    pl.semaphore_wait(barrier, CTX - jnp.where(plane == c, 1, 0) + CHAN - 1)

    def weight_slices(h, to, slot):
        rows = pl.ds(*WEIGHT_ROWS[h])
        lanes = pl.ds(pl.multiple_of(slot % PLANE * HALF, HALF), HALF)
        return turned_weight.at[to, rows, :], got_weight.at[slot // PLANE, rows, lanes], w_recv.at[h]

    def weight_copy(h, j):
        to = (i + CTX - j) % CTX
        src, dst, sem = weight_slices(h, to, c * PLANE + place)
        return send(src, dst, w_send.at[h], sem, to, plane)

    def start_weights(h):
        @pl.loop(1, CTX)
        def _(j):
            weight_copy(h, j).start()

        @pl.when(plane == c)
        def _():
            pltpu.make_async_copy(*weight_slices(h, i, c * PLANE + place)).start()

        @pl.when(plane != c)
        def _():
            weight_copy(h, 0).start()

    def wait_for(region, sem):
        pltpu.make_async_copy(region, region, sem).wait()

    def wait_weights(h):
        wait_for(got_weight.at[:, pl.ds(*WEIGHT_ROWS[h]), :], w_recv.at[h])

    def token_copy(n):
        to = c * PLANE + (place + n) % PLANE
        return send(own_tokens, tokens.at[i], t_send, t_recv, to, plane)

    own_token_copy = pltpu.make_async_copy(own_tokens, tokens.at[i], t_recv)

    @pl.when(plane == c)
    def _():
        own_token_copy.start()

    @pl.when(plane != c)
    def _():
        token_copy(0).start()

    @pl.loop(1, PLANE)
    def _(n):
        token_copy(n).start()

    start_weights(0)

    loads[2].wait()
    loads[3].wait()
    wide = embed[...].astype(f32)
    feats = embed.shape[1]
    square_high, square_low = high_low(wide * wide)
    ones = jnp.ones((8, feats), bf16)
    squares = lax.dot_general(ones, square_high, NT, preferred_element_type=f32)
    got_square[c] = squares + lax.dot_general(ones, square_low, NT, preferred_element_type=f32)

    wait_for(tokens.at[pl.ds(c * PLANE, PLANE)], t_recv)

    def plane_copy(source, to, d):
        block = tokens.at[pl.ds(source * PLANE, PLANE)]
        return send(block, block, u_send.at[d], u_recv.at[source], i, to)

    for d in range(1, CHAN):
        plane_copy(c, (c + d) % CHAN, d).start()

    def square_copy(d):
        return send(got_square.at[c], got_square.at[c], s_send.at[d], s_recv.at[c], i, (c + d) % CHAN)

    for d in range(1, CHAN):
        square_copy(d).start()
    scaled[...] = (wide * gain[pl.ds(c * feats, feats)].reshape(1, feats)).astype(bf16)

    start_weights(1)
    near, far = (c // 2) * 2, 2 - (c // 2) * 2
    other = c + 1 - 2 * (c % 2)
    part_send, part_got = (part_send0, part_send1), (part_got0, part_got1)

    def part_copy(h, to, d):
        return send(part_send[h].at[to], part_got[h].at[c], p_send.at[h, d], p_recv.at[h, c], i, to)

    def products(h, first):
        top, count = WEIGHT_ROWS[h]
        weights = got_weight[pl.ds(first, 2), pl.ds(top, count), :].reshape(2 * count, feats)
        product = lax.dot_general(weights, scaled[...], NT, preferred_element_type=f32)
        return product.reshape(2, count, product.shape[1])

    def start_parts(h):
        top, count = WEIGHT_ROWS[h]
        part_send[h][pl.ds(far, 2)] = products(h, far).astype(bf16)
        part_copy(h, far, 0).start()
        part_copy(h, far + 1, 1).start()
        product = products(h, near)
        part[:, top : top + count, :] = product
        part_send[h][pl.ds(near, 2)] = product.astype(bf16)
        part_copy(h, other, 2).start()

    def finish_parts(h, scale):
        top, count = WEIGHT_ROWS[h]
        total = part[c % 2, top : top + count, :]
        for d in range(1, CHAN):
            source = (c + d) % CHAN
            send(
                part_send[h].at[0], part_got[h].at[source], p_send.at[h, d], p_recv.at[h, source], i, source
            ).wait_recv()
            total = total + part_got[h][source].astype(f32)
        table[top : top + count, :] = (total * scale).astype(bf16).astype(f32)

    def branches_of(h):
        rows = jnp.concatenate([table[top : top + FEW, :] for top in TABLE_ROWS[h]], axis=0)
        quarters = jnp.concatenate([rows[:, n * HALF : (n + 1) * HALF] for n in range(4)], axis=0)
        short_filter_and_gate(quarters.astype(bf16), tokens, taps.at[h], carried.at[h], query.at[h])

    def out_slot(h, source):
        return got_ref.at[h, :, pl.ds(pl.multiple_of(source * OWN, OWN), OWN), :], o_recv.at[h]

    def out_copy(h, to):
        dst, sem = out_slot(h, i)
        return send(ready.at[h, to], dst, o_send.at[h], sem, to, c)

    def start_outputs(h, decay_row):
        segment_states(carried.at[h], gather.at[h], decay_row[:, h * FEWS : (h + 1) * FEWS], state.at[h])

        inside_segments(carried.at[h], reach.at[h], conv)

        @pl.loop(0, CTX // PLANE)
        def _(step):
            q = (plane + (1 + step if h == 0 else CTX // PLANE - 1 - step)) % (CTX // PLANE)
            outputs_of_part(
                q, carried.at[h], query.at[h], state.at[h], conv, reach.at[h], skip.at[h], ready.at[h]
            )

            @pl.loop(0, PLANE)
            def _(n):
                to = q * PLANE + (place + n) % PLANE

                @pl.when(to != i)
                def _():
                    out_copy(h, to).start()

                @pl.when(to == i)
                def _():
                    pltpu.make_async_copy(ready.at[h, to], *out_slot(h, i)).start()

    wait_weights(0)
    start_parts(0)

    for load in loads[4:]:
        load.wait()
    lanes_from = pl.multiple_of((i // PLANE) * HALF, HALF)
    shift = lax.rem(HALF - place * OWN, HALF)
    decay_own, residue_own = load_own([decay, residue], lanes_from, shift)
    weight_own = residue_own * jnp.sqrt(decay_own)
    decay_row = filter_tables(decay_own, weight_own, gather, reach)
    for j in range(3):
        (rows,) = load_own([taps_all.at[j]], lanes_from, shift)
        padded = jnp.concatenate([rows, jnp.zeros((5, HALF), f32)], axis=0)
        columns = jnp.transpose(padded)[:OWN]
        for b in range(3):
            wide_column = jnp.broadcast_to(columns[:, b : b + 1], (OWN, HALF))
            for h in range(2):
                taps[h, j, b * FEW : (b + 1) * FEW, :] = wide_column[h * FEW : (h + 1) * FEW]
    skip_row = pltpu.roll(
        jnp.broadcast_to(skip_all[pl.ds(lanes_from, HALF)].reshape(1, HALF), (8, HALF)), shift, axis=1
    )
    skip_column = jnp.transpose(skip_row)[:OWN, 0:1]
    skip[...] = jnp.broadcast_to(skip_column, (OWN, SEG)).reshape(2, FEW, SEG)

    wait_weights(1)
    start_parts(1)
    mean = got_square[c]
    for d in range(1, CHAN):
        source = (c + d) % CHAN
        send(got_square.at[c], got_square.at[source], s_send.at[d], s_recv.at[source], i, source).wait_recv()
        mean = mean + got_square[source]
    scale = lax.rsqrt(mean[0:1] * (1.0 / (CHAN * feats)) + EPS)
    for d in range(1, CHAN):
        plane_copy((c + d) % CHAN, c, d).wait_recv()
    finish_parts(0, scale)
    branches_of(0)
    start_outputs(0, decay_row)
    finish_parts(1, scale)
    branches_of(1)
    start_outputs(1, decay_row)

    for h in range(2):
        wait_for(ready.at[h, pl.ds(0, CTX - 1)], o_send.at[h])
        part_copy(h, far, 0).wait_send()
        part_copy(h, far + 1, 1).wait_send()
        part_copy(h, other, 2).wait_send()

    def wait_sends(skipped):
        for h in range(2):
            rows = pl.ds(*WEIGHT_ROWS[h])
            wait_for(turned_weight.at[pl.ds(0, CTX - skipped), rows, :], w_send.at[h])
        wait_for(tokens.at[pl.ds(0, PLANE - skipped)], t_send)

    @pl.when(plane != c)
    def _():
        wait_sends(0)

    @pl.when(plane == c)
    def _():
        wait_sends(1)

    for d in range(1, CHAN):
        square_copy(d).wait_send()
        plane_copy(c, (c + d) % CHAN, d).wait_send()
    for h in range(2):
        wait_for(got_ref.at[h], o_recv.at[h])


def gathered(
    token_ids, embed_table, norm_gain, in_weight, short_filter, residue, decay_rate, skip_bias
):
    f32, bf16 = jnp.float32, jnp.bfloat16
    rows = token_ids.shape[0]
    vocab, feats = embed_table.shape
    chans = decay_rate.shape[1]
    weight = jnp.transpose(in_weight, (1, 0, 2))
    operands = (token_ids, embed_table, norm_gain, weight, short_filter, residue, decay_rate, skip_bias)
    dma, vmem = pltpu.SemaphoreType.DMA, pltpu.VMEM
    return pl.pallas_call(
        main_kernel,
        name="hyena",
        out_shape=pltpu.VMEM((2, PER, CTX * OWN, HALF), bf16),
        in_specs=[pl.BlockSpec(memory_space=pl.ANY)] * len(operands),
        out_specs=pl.BlockSpec(memory_space=pl.ANY),
        scratch_shapes=[
            vmem(token_ids.shape, jnp.int32),
            vmem((1, rows), jnp.int32),
            vmem(embed_table.shape, bf16),
            vmem(norm_gain.shape, f32),
            vmem(weight.shape, bf16),
            vmem(short_filter.shape, f32),
            vmem(residue.shape, f32),
            vmem(decay_rate.shape, f32),
            vmem(skip_bias.shape, f32),
            vmem((CTX, 3 * OWN, in_weight.shape[0]), bf16),
            vmem((CHAN, 3 * OWN, feats), bf16),
            vmem((CHAN, 8, vocab), f32),
            vmem((vocab, feats), bf16),
            vmem((2, 3 * OWN, vocab), f32),
            vmem((CHAN, WEIGHT_ROWS[0][1], vocab), bf16),
            vmem((CHAN, WEIGHT_ROWS[1][1], vocab), bf16),
            vmem((CHAN, WEIGHT_ROWS[0][1], vocab), bf16),
            vmem((CHAN, WEIGHT_ROWS[1][1], vocab), bf16),
            vmem((CTX, 1, rows), jnp.int32),
            vmem((3 * OWN, vocab), f32),
            vmem((2, SEG, 2 * FEWS), bf16),
            vmem((2, FEW * SEG + 3 * FEWS, SEG), bf16),
            vmem((2, 3, 3 * FEW, HALF), f32),
            vmem((2, FEW, SEG), f32),
            vmem((2, 2, SEGS * FEW, HALF), f32),
            vmem((2, 2, SEGS * FEW, HALF), f32),
            vmem((2, SEGS, FEWS), f32),
            vmem((2, SEGS * FEW, HALF), f32),
            vmem((2, CTX, PER, 2 * FEW, HALF), bf16),
            dma((8,)),
            dma((2,)), dma((2,)), dma(()), dma(()),
            dma((CHAN,)), dma((CHAN,)), dma((CHAN,)), dma((CHAN,)), dma((2, CHAN)), dma((2, CHAN)),
            dma((2,)), dma((2,)),
        ],
        compiler_params=pltpu.CompilerParams(
            collective_id=0, has_side_effects=True, vmem_limit_bytes=VMEM_LIMIT
        ),
    )(*operands)


def turn_kernel(got, out_hbm, out, out_sem):
    f32, bf16 = jnp.float32, jnp.bfloat16
    unit = (
        lax.broadcasted_iota(jnp.int32, (HALF, HALF), 0) == lax.broadcasted_iota(jnp.int32, (HALF, HALF), 1)
    ).astype(bf16)
    stores = []
    for g in range(PER):
        eights = [got[h, g].astype(f32).reshape(CTX, 2, FEW, HALF) for h in range(2)]
        for half in range(2):
            rows = jnp.concatenate([eights[h][:, half : half + 1] for h in range(2)], axis=1)
            rows = rows.reshape(CTX * OWN, HALF).astype(bf16)
            top = g * SEG + half * HALF
            turned = lax.dot_general(unit, rows, NT, preferred_element_type=f32)
            out[top : top + HALF, :] = turned.astype(bf16)
        rows = pl.ds(g * SEG, SEG)
        stores.append(pltpu.make_async_copy(out.at[rows, :], out_hbm.at[rows, :], out_sem.at[g]))
        stores[g].start()
    for store in stores:
        store.wait()


def turned(got):
    bf16 = jnp.bfloat16
    shape = (PER * SEG, CTX * OWN)
    return pl.pallas_call(
        turn_kernel,
        name="turn",
        out_shape=jax.ShapeDtypeStruct(shape, bf16),
        in_specs=[pl.BlockSpec(memory_space=pltpu.VMEM)],
        out_specs=pl.BlockSpec(memory_space=pl.ANY),
        scratch_shapes=[pltpu.VMEM(shape, bf16), pltpu.SemaphoreType.DMA((PER,))],
        compiler_params=pltpu.CompilerParams(vmem_limit_bytes=TURN_LIMIT),
    )(got)


def per_device(*arrays):
    return turned(gathered(*arrays))


def solution(mesh):
    return jax.shard_map(
        per_device,
        mesh=mesh,
        in_specs=(
            P("ctx"),
            P(None, "chan"),
            P(),
            P("ctx", None, "chan"),
            P(None, None, "chan"),
            P(None, "chan"),
            P(None, "chan"),
            P("chan"),
        ),
        out_specs=P("ctx", "chan"),
        check_vma=False,
    )
```

```python
import functools

import jax
import jax.numpy as jnp
from jax import lax
from jax.experimental import pallas as pl
from jax.experimental.pallas import tpu as pltpu
from jax.sharding import PartitionSpec as P

MESH = pl.DeviceIdType.MESH
EPS = 1e-06
VMEM_LIMIT = 56 * 1024 * 1024
TURN_LIMIT = 16 * 1024 * 1024

CTX, CHAN, PLANE = 32, 4, 8
OWN = 16
SEG = 256
SEGS = 96
PER = 3
PART = 24
HALF = 128
MODES = 16
PAIRS = OWN * MODES
FEW = 8
FEWS = FEW * MODES
WEIGHT_ROWS = ((0, 32), (32, 16))
TABLE_ROWS = ((0, 8, 16), (32, 24, 40))
NT = (((1,), (1,)), ((), ()))
HIGHEST = lax.Precision.HIGHEST


def dot(a, b):
    return jnp.dot(a, b, preferred_element_type=jnp.float32)


def high_low(x):
    high = x.astype(jnp.bfloat16)
    return high, (x - high.astype(jnp.float32)).astype(jnp.bfloat16)


def send(src, dst, send_sem, recv_sem, i, c):
    return pltpu.make_async_remote_copy(
        src_ref=src, dst_ref=dst, send_sem=send_sem, recv_sem=recv_sem, device_id=(i, c), device_id_type=MESH
    )


def load_own(row_refs, lanes_from, shift):
    rows = [ref[:, pl.ds(lanes_from, HALF)] for ref in row_refs]
    return [pltpu.roll(array, shift, axis=1) for array in rows]


def filter_tables(decay, weight, gather, reach):
    f32, bf16 = jnp.float32, jnp.bfloat16
    decay_turned = jnp.transpose(decay)[:OWN]
    weight_turned = jnp.transpose(weight)[:OWN]
    lane = lax.broadcasted_iota(jnp.int32, (OWN, HALF), 1).astype(f32)
    near = jnp.zeros((OWN, HALF), f32)
    far = jnp.zeros((OWN, HALF), f32)
    for m in range(MODES):
        rate = jnp.broadcast_to(decay_turned[:, m : m + 1], (OWN, HALF))
        height = jnp.broadcast_to(weight_turned[:, m : m + 1], (OWN, HALF))
        near = near + height * jnp.exp(-rate * lane)
        far = far + height * jnp.exp(-rate * (lane + float(HALF)))
    causal = lax.broadcasted_iota(jnp.int32, (HALF, HALF), 1) >= lax.broadcasted_iota(jnp.int32, (HALF, HALF), 0)
    for ch in range(OWN):
        near_rolled = pltpu.roll(
            jnp.broadcast_to(near[ch : ch + 1], (HALF, HALF)), 0, axis=1, stride=1, stride_axis=0
        )
        far_rolled = pltpu.roll(
            jnp.broadcast_to(far[ch : ch + 1], (HALF, HALF)), 0, axis=1, stride=1, stride_axis=0
        )
        diagonal = jnp.where(causal, near_rolled, 0.0).astype(bf16)
        part, top = ch // FEW, ch % FEW * SEG
        middle, end = top + HALF, top + SEG
        reach[part, top:middle, :HALF] = diagonal
        reach[part, middle:end, HALF:] = diagonal
        reach[part, top:middle, HALF:] = jnp.where(causal, far_rolled, near_rolled).astype(bf16)
        reach[part, middle:end, :HALF] = jnp.zeros((HALF, HALF), bf16)

    pick = (
        lax.broadcasted_iota(jnp.int32, (HALF, PAIRS), 0)
        == lax.broadcasted_iota(jnp.int32, (HALF, PAIRS), 1) // MODES
    ).astype(f32)
    own_mode = (
        lax.broadcasted_iota(jnp.int32, (MODES, PAIRS), 0)
        == lax.broadcasted_iota(jnp.int32, (MODES, PAIRS), 1) % MODES
    )

    def pair_row(array):
        wide = jnp.dot(array, pick, precision=HIGHEST, preferred_element_type=f32)
        return jnp.sum(jnp.where(own_mode, wide, 0.0), axis=0, keepdims=True)

    decay_row = pair_row(decay)
    decay_column = jnp.transpose(jnp.broadcast_to(decay_row, (HALF, PAIRS)))
    weight_column = jnp.transpose(jnp.broadcast_to(pair_row(weight), (HALF, PAIRS)))
    to_end = (SEG - 1 - lax.broadcasted_iota(jnp.int32, (SEG, PAIRS), 0)).astype(f32)
    entering = high_low(jnp.exp(-decay_row * to_end))
    for part in range(2):
        for n in range(2):
            gather[part, :, n * FEWS : (n + 1) * FEWS] = entering[n][:, part * FEWS : (part + 1) * FEWS]
    for half in range(2):
        lanes = slice(half * HALF, (half + 1) * HALF)
        after = lax.broadcasted_iota(jnp.int32, (PAIRS, HALF), 1).astype(f32) + float(half * HALF + 1)
        high, low = high_low(weight_column * jnp.exp(-decay_column * after))
        for part in range(2):
            rows = slice(part * FEWS, (part + 1) * FEWS)
            for n, piece in enumerate((high, high, low)):
                top = FEW * SEG + n * FEWS
                reach[part, top : top + FEWS, lanes] = piece[rows]
    return decay_row


def short_filter_and_gate(table, tokens_ref, taps_ref, carried_ref, query_ref):
    f32, bf16 = jnp.float32, jnp.bfloat16
    rows = 3 * FEW
    entry = lax.broadcasted_iota(jnp.int32, (HALF, SEG), 0).astype(f32).astype(bf16)
    lane = lax.broadcasted_iota(jnp.int32, (rows, HALF), 1)
    one, zero = jnp.ones((), bf16), jnp.zeros((), bf16)

    def block(g, before):
        for part in range(PER):
            ids = tokens_ref[g, :, part * SEG : (part + 1) * SEG]
            chosen = (ids & (HALF - 1)).astype(f32).astype(bf16)
            each = dot(table, jnp.where(entry == chosen, one, zero)).reshape(4, rows, SEG)
            odd, upper = (ids & HALF) != 0, (ids & SEG) != 0
            projected = jnp.where(upper, jnp.where(odd, each[3], each[2]), jnp.where(odd, each[1], each[0]))
            at = pl.ds(pl.multiple_of((g * PER + part) * FEW, FEW), FEW)
            for half in range(2):
                lanes = slice(half * HALF, (half + 1) * HALF)
                here = projected[:, lanes]
                turned = (pltpu.roll(here, 1, axis=1), pltpu.roll(here, 2, axis=1))
                branches = (
                    taps_ref[0] * here
                    + taps_ref[1] * jnp.where(lane < 1, before[0], turned[0])
                    + taps_ref[2] * jnp.where(lane < 2, before[1], turned[1])
                )
                before = turned
                carried = branches[FEW : 2 * FEW] * branches[2 * FEW :]
                carried_ref[half, at, :] = carried.astype(bf16).astype(f32)
                query_ref[half, at, :] = branches[:FEW]
        return before

    nothing = jnp.zeros((rows, HALF), f32)
    lax.fori_loop(0, SEGS // PER, block, (nothing, nothing), unroll=UNROLL)


UNROLL = 32


def both_halves(ref, rows):
    return jnp.concatenate([ref[half, rows, :] for half in range(2)], axis=1)


def own_pairs():
    shape = (1, FEW, FEWS)
    return lax.broadcasted_iota(jnp.int32, shape, 2) // MODES == lax.broadcasted_iota(jnp.int32, shape, 1)


def segment_states(carried_ref, gather, decay_row, state_ref):
    f32, bf16 = jnp.float32, jnp.bfloat16
    enters = dot(both_halves(carried_ref, slice(None)).astype(bf16), gather[...])
    enters = (enters[:, :FEWS] + enters[:, FEWS:]).reshape(SEGS, FEW, FEWS)
    added = jnp.sum(jnp.where(own_pairs(), enters, 0.0), axis=1)

    def later(x, by):
        return jnp.concatenate([jnp.zeros((by, FEWS), f32), x[: SEGS - by]], axis=0)

    state = later(added, 1)
    by = 1
    while by < SEGS:
        state = state + jnp.exp(-decay_row * float(SEG * by)) * later(state, by)
        by *= 2
    state_ref[...] = state


def inside_segments(carried_ref, reach, conv_ref):
    for ch in range(FEW):
        rows = pl.ds(ch, SEGS, stride=FEW)
        conv = dot(both_halves(carried_ref, rows).astype(jnp.bfloat16), reach[ch * SEG : (ch + 1) * SEG, :])
        for half in range(2):
            conv_ref[half, rows, :] = conv[:, half * HALF : (half + 1) * HALF]


def outputs_of_part(q, carried_ref, query_ref, state_ref, conv_ref, reach, skip_ref, ready):
    first = pl.multiple_of(q * PART, PART)
    rows = pl.ds(pl.multiple_of(first * FEW, FEW), PART * FEW)
    state = jnp.where(own_pairs(), state_ref[pl.ds(first, PART), :][:, None, :], 0.0)
    high, low = high_low(state.reshape(PART * FEW, FEWS))
    reached = dot(jnp.concatenate([high, low, high], axis=1), reach[FEW * SEG :, :])
    halves = []
    for half in range(2):
        lanes = slice(half * HALF, (half + 1) * HALF)
        carried = carried_ref[half, rows, :].reshape(PART, FEW, HALF)
        direct = (skip_ref[:, lanes][None] * carried).reshape(PART * FEW, HALF)
        gated = query_ref[half, rows, :] * (conv_ref[half, rows, :] + reached[:, lanes] + direct)
        halves.append(gated.reshape(PART, 1, FEW, HALF))
    block = jnp.concatenate(halves, axis=1).reshape(PLANE, PER, 2 * FEW, HALF)
    ready[pl.ds(q * PLANE, PLANE)] = block.astype(jnp.bfloat16)


def main_kernel(
    tok_hbm, embed_hbm, gain_hbm, weight_hbm, taps_hbm, residue_hbm, decay_hbm, skip_hbm, got_ref,
    tok, own_tokens, embed, gain, weight, taps_all, residue, decay, skip_all,
    turned_weight, got_weight, got_square, scaled, part, part_send0, part_send1, part_got0, part_got1, tokens, table,
    gather, reach, taps, skip, carried, query, state, conv, ready,
    in_sem, w_send, w_recv, t_send, t_recv, u_send, u_recv, s_send, s_recv, p_send, p_recv, o_send, o_recv,
):
    f32, bf16 = jnp.float32, jnp.bfloat16
    i, c = lax.axis_index("ctx"), lax.axis_index("chan")
    plane, place = i // PLANE, i % PLANE

    loads = [
        pltpu.make_async_copy(src, dst, in_sem.at[n])
        for n, (src, dst) in enumerate(
            (
                (weight_hbm, weight), (tok_hbm, tok), (embed_hbm, embed), (gain_hbm, gain),
                (taps_hbm, taps_all), (residue_hbm, residue), (decay_hbm, decay), (skip_hbm, skip_all),
            )
        )
    ]
    for load in loads:
        load.start()

    barrier = pltpu.get_barrier_semaphore()

    @pl.loop(0, CTX)
    def _(j):
        row, col = c * PLANE + j % PLANE, j // PLANE

        @pl.when(jnp.logical_or(row != i, col != c))
        def _():
            pl.semaphore_signal(barrier, inc=1, device_id=(row, col), device_id_type=MESH)

    for d in range(1, CHAN):
        pl.semaphore_signal(barrier, inc=1, device_id=(i, (c + d) % CHAN), device_id_type=MESH)

    loads[0].wait()
    eights = [jnp.transpose(weight[b].astype(f32)).reshape(CTX, 2, FEW, HALF) for b in range(3)]
    order = ((0, 0), (1, 0), (2, 0), (1, 1), (0, 1), (2, 1))
    rows = jnp.concatenate([eights[b][:, part : part + 1] for b, part in order], axis=1)
    turned_weight[...] = rows.reshape(turned_weight.shape).astype(bf16)
    loads[1].wait()
    own_tokens[...] = tok[...].reshape(1, tok.shape[0])

    pl.semaphore_wait(barrier, CTX - jnp.where(plane == c, 1, 0) + CHAN - 1)

    def weight_slices(h, to, slot):
        rows = pl.ds(*WEIGHT_ROWS[h])
        lanes = pl.ds(pl.multiple_of(slot % PLANE * HALF, HALF), HALF)
        return turned_weight.at[to, rows, :], got_weight.at[slot // PLANE, rows, lanes], w_recv.at[h]

    def weight_copy(h, j):
        to = (i + CTX - j) % CTX
        src, dst, sem = weight_slices(h, to, c * PLANE + place)
        return send(src, dst, w_send.at[h], sem, to, plane)

    def start_weights(h):
        @pl.loop(1, CTX)
        def _(j):
            weight_copy(h, j).start()

        @pl.when(plane == c)
        def _():
            pltpu.make_async_copy(*weight_slices(h, i, c * PLANE + place)).start()

        @pl.when(plane != c)
        def _():
            weight_copy(h, 0).start()

    def wait_for(region, sem):
        pltpu.make_async_copy(region, region, sem).wait()

    def wait_weights(h):
        wait_for(got_weight.at[:, pl.ds(*WEIGHT_ROWS[h]), :], w_recv.at[h])

    def token_copy(n):
        to = c * PLANE + (place + n) % PLANE
        return send(own_tokens, tokens.at[i], t_send, t_recv, to, plane)

    own_token_copy = pltpu.make_async_copy(own_tokens, tokens.at[i], t_recv)

    @pl.when(plane == c)
    def _():
        own_token_copy.start()

    @pl.when(plane != c)
    def _():
        token_copy(0).start()

    @pl.loop(1, PLANE)
    def _(n):
        token_copy(n).start()

    start_weights(0)

    loads[2].wait()
    loads[3].wait()
    wide = embed[...].astype(f32)
    feats = embed.shape[1]
    square_high, square_low = high_low(wide * wide)
    ones = jnp.ones((8, feats), bf16)
    squares = lax.dot_general(ones, square_high, NT, preferred_element_type=f32)
    got_square[c] = squares + lax.dot_general(ones, square_low, NT, preferred_element_type=f32)

    wait_for(tokens.at[pl.ds(c * PLANE, PLANE)], t_recv)

    def plane_copy(source, to, d):
        block = tokens.at[pl.ds(source * PLANE, PLANE)]
        return send(block, block, u_send.at[d], u_recv.at[source], i, to)

    for d in range(1, CHAN):
        plane_copy(c, (c + d) % CHAN, d).start()

    def square_copy(d):
        return send(got_square.at[c], got_square.at[c], s_send.at[d], s_recv.at[c], i, (c + d) % CHAN)

    for d in range(1, CHAN):
        square_copy(d).start()
    scaled[...] = (wide * gain[pl.ds(c * feats, feats)].reshape(1, feats)).astype(bf16)

    start_weights(1)
    near, far = (c // 2) * 2, 2 - (c // 2) * 2
    other = c + 1 - 2 * (c % 2)
    part_send, part_got = (part_send0, part_send1), (part_got0, part_got1)

    def part_copy(h, to, d):
        return send(part_send[h].at[to], part_got[h].at[c], p_send.at[h, d], p_recv.at[h, c], i, to)

    def products(h, first):
        top, count = WEIGHT_ROWS[h]
        weights = got_weight[pl.ds(first, 2), pl.ds(top, count), :].reshape(2 * count, feats)
        product = lax.dot_general(weights, scaled[...], NT, preferred_element_type=f32)
        return product.reshape(2, count, product.shape[1])

    def start_parts(h):
        top, count = WEIGHT_ROWS[h]
        part_send[h][pl.ds(far, 2)] = products(h, far).astype(bf16)
        part_copy(h, far, 0).start()
        part_copy(h, far + 1, 1).start()
        product = products(h, near)
        part[:, top : top + count, :] = product
        part_send[h][pl.ds(near, 2)] = product.astype(bf16)
        part_copy(h, other, 2).start()

    def finish_parts(h, scale):
        top, count = WEIGHT_ROWS[h]
        total = part[c % 2, top : top + count, :]
        for d in range(1, CHAN):
            source = (c + d) % CHAN
            send(
                part_send[h].at[0], part_got[h].at[source], p_send.at[h, d], p_recv.at[h, source], i, source
            ).wait_recv()
            total = total + part_got[h][source].astype(f32)
        table[top : top + count, :] = (total * scale).astype(bf16).astype(f32)

    def branches_of(h):
        rows = jnp.concatenate([table[top : top + FEW, :] for top in TABLE_ROWS[h]], axis=0)
        quarters = jnp.concatenate([rows[:, n * HALF : (n + 1) * HALF] for n in range(4)], axis=0)
        short_filter_and_gate(quarters.astype(bf16), tokens, taps.at[h], carried.at[h], query.at[h])

    def out_slot(h, source):
        return got_ref.at[h, :, pl.ds(pl.multiple_of(source * OWN, OWN), OWN), :], o_recv.at[h]

    def out_copy(h, to):
        dst, sem = out_slot(h, i)
        return send(ready.at[h, to], dst, o_send.at[h], sem, to, c)

    def start_outputs(h, decay_row):
        segment_states(carried.at[h], gather.at[h], decay_row[:, h * FEWS : (h + 1) * FEWS], state.at[h])

        inside_segments(carried.at[h], reach.at[h], conv)

        @pl.loop(0, CTX // PLANE)
        def _(step):
            q = (plane + (1 + step if h == 0 else CTX // PLANE - 1 - step)) % (CTX // PLANE)
            outputs_of_part(
                q, carried.at[h], query.at[h], state.at[h], conv, reach.at[h], skip.at[h], ready.at[h]
            )

            @pl.loop(0, PLANE)
            def _(n):
                to = q * PLANE + (place + n) % PLANE

                @pl.when(to != i)
                def _():
                    out_copy(h, to).start()

                @pl.when(to == i)
                def _():
                    pltpu.make_async_copy(ready.at[h, to], *out_slot(h, i)).start()

    wait_weights(0)
    start_parts(0)

    for load in loads[4:]:
        load.wait()
    lanes_from = pl.multiple_of((i // PLANE) * HALF, HALF)
    shift = lax.rem(HALF - place * OWN, HALF)
    decay_own, residue_own = load_own([decay, residue], lanes_from, shift)
    weight_own = residue_own * jnp.sqrt(decay_own)
    decay_row = filter_tables(decay_own, weight_own, gather, reach)
    for j in range(3):
        (rows,) = load_own([taps_all.at[j]], lanes_from, shift)
        padded = jnp.concatenate([rows, jnp.zeros((5, HALF), f32)], axis=0)
        columns = jnp.transpose(padded)[:OWN]
        for b in range(3):
            wide_column = jnp.broadcast_to(columns[:, b : b + 1], (OWN, HALF))
            for h in range(2):
                taps[h, j, b * FEW : (b + 1) * FEW, :] = wide_column[h * FEW : (h + 1) * FEW]
    skip_row = pltpu.roll(
        jnp.broadcast_to(skip_all[pl.ds(lanes_from, HALF)].reshape(1, HALF), (8, HALF)), shift, axis=1
    )
    skip_column = jnp.transpose(skip_row)[:OWN, 0:1]
    skip[...] = jnp.broadcast_to(skip_column, (OWN, SEG)).reshape(2, FEW, SEG)

    wait_weights(1)
    start_parts(1)
    mean = got_square[c]
    for d in range(1, CHAN):
        source = (c + d) % CHAN
        send(got_square.at[c], got_square.at[source], s_send.at[d], s_recv.at[source], i, source).wait_recv()
        mean = mean + got_square[source]
    scale = lax.rsqrt(mean[0:1] * (1.0 / (CHAN * feats)) + EPS)
    for d in range(1, CHAN):
        plane_copy((c + d) % CHAN, c, d).wait_recv()
    finish_parts(0, scale)
    branches_of(0)
    start_outputs(0, decay_row)
    finish_parts(1, scale)
    branches_of(1)
    start_outputs(1, decay_row)

    for h in range(2):
        wait_for(ready.at[h, pl.ds(0, CTX - 1)], o_send.at[h])
        part_copy(h, far, 0).wait_send()
        part_copy(h, far + 1, 1).wait_send()
        part_copy(h, other, 2).wait_send()

    def wait_sends(skipped):
        for h in range(2):
            rows = pl.ds(*WEIGHT_ROWS[h])
            wait_for(turned_weight.at[pl.ds(0, CTX - skipped), rows, :], w_send.at[h])
        wait_for(tokens.at[pl.ds(0, PLANE - skipped)], t_send)

    @pl.when(plane != c)
    def _():
        wait_sends(0)

    @pl.when(plane == c)
    def _():
        wait_sends(1)

    for d in range(1, CHAN):
        square_copy(d).wait_send()
        plane_copy(c, (c + d) % CHAN, d).wait_send()
    for h in range(2):
        wait_for(got_ref.at[h], o_recv.at[h])


def gathered(
    token_ids, embed_table, norm_gain, in_weight, short_filter, residue, decay_rate, skip_bias
):
    f32, bf16 = jnp.float32, jnp.bfloat16
    rows = token_ids.shape[0]
    vocab, feats = embed_table.shape
    chans = decay_rate.shape[1]
    weight = jnp.transpose(in_weight, (1, 0, 2))
    operands = (token_ids, embed_table, norm_gain, weight, short_filter, residue, decay_rate, skip_bias)
    dma, vmem = pltpu.SemaphoreType.DMA, pltpu.VMEM
    return pl.pallas_call(
        main_kernel,
        name="hyena",
        out_shape=pltpu.VMEM((2, PER, CTX * OWN, HALF), bf16),
        in_specs=[pl.BlockSpec(memory_space=pl.ANY)] * len(operands),
        out_specs=pl.BlockSpec(memory_space=pl.ANY),
        scratch_shapes=[
            vmem(token_ids.shape, jnp.int32),
            vmem((1, rows), jnp.int32),
            vmem(embed_table.shape, bf16),
            vmem(norm_gain.shape, f32),
            vmem(weight.shape, bf16),
            vmem(short_filter.shape, f32),
            vmem(residue.shape, f32),
            vmem(decay_rate.shape, f32),
            vmem(skip_bias.shape, f32),
            vmem((CTX, 3 * OWN, in_weight.shape[0]), bf16),
            vmem((CHAN, 3 * OWN, feats), bf16),
            vmem((CHAN, 8, vocab), f32),
            vmem((vocab, feats), bf16),
            vmem((2, 3 * OWN, vocab), f32),
            vmem((CHAN, WEIGHT_ROWS[0][1], vocab), bf16),
            vmem((CHAN, WEIGHT_ROWS[1][1], vocab), bf16),
            vmem((CHAN, WEIGHT_ROWS[0][1], vocab), bf16),
            vmem((CHAN, WEIGHT_ROWS[1][1], vocab), bf16),
            vmem((CTX, 1, rows), jnp.int32),
            vmem((3 * OWN, vocab), f32),
            vmem((2, SEG, 2 * FEWS), bf16),
            vmem((2, FEW * SEG + 3 * FEWS, SEG), bf16),
            vmem((2, 3, 3 * FEW, HALF), f32),
            vmem((2, FEW, SEG), f32),
            vmem((2, 2, SEGS * FEW, HALF), f32),
            vmem((2, 2, SEGS * FEW, HALF), f32),
            vmem((2, SEGS, FEWS), f32),
            vmem((2, SEGS * FEW, HALF), f32),
            vmem((2, CTX, PER, 2 * FEW, HALF), bf16),
            dma((8,)),
            dma((2,)), dma((2,)), dma(()), dma(()),
            dma((CHAN,)), dma((CHAN,)), dma((CHAN,)), dma((CHAN,)), dma((2, CHAN)), dma((2, CHAN)),
            dma((2,)), dma((2,)),
        ],
        compiler_params=pltpu.CompilerParams(
            collective_id=0, has_side_effects=True, vmem_limit_bytes=VMEM_LIMIT
        ),
    )(*operands)


def turn_kernel(got, out_hbm, out, out_sem):
    f32, bf16 = jnp.float32, jnp.bfloat16
    unit = (
        lax.broadcasted_iota(jnp.int32, (HALF, HALF), 0) == lax.broadcasted_iota(jnp.int32, (HALF, HALF), 1)
    ).astype(bf16)
    stores = []
    for g in range(PER):
        eights = [got[h, g].astype(f32).reshape(CTX, 2, FEW, HALF) for h in range(2)]
        for half in range(2):
            rows = jnp.concatenate([eights[h][:, half : half + 1] for h in range(2)], axis=1)
            rows = rows.reshape(CTX * OWN, HALF).astype(bf16)
            top = g * SEG + half * HALF
            turned = lax.dot_general(unit, rows, NT, preferred_element_type=f32)
            out[top : top + HALF, :] = turned.astype(bf16)
        rows = pl.ds(g * SEG, SEG)
        stores.append(pltpu.make_async_copy(out.at[rows, :], out_hbm.at[rows, :], out_sem.at[g]))
        stores[g].start()
    for store in stores:
        store.wait()


def turned(got):
    bf16 = jnp.bfloat16
    shape = (PER * SEG, CTX * OWN)
    return pl.pallas_call(
        turn_kernel,
        name="turn",
        out_shape=jax.ShapeDtypeStruct(shape, bf16),
        in_specs=[pl.BlockSpec(memory_space=pltpu.VMEM)],
        out_specs=pl.BlockSpec(memory_space=pl.ANY),
        scratch_shapes=[pltpu.VMEM(shape, bf16), pltpu.SemaphoreType.DMA((PER,))],
        compiler_params=pltpu.CompilerParams(vmem_limit_bytes=TURN_LIMIT),
    )(got)


def per_device(*arrays):
    return turned(gathered(*arrays))


def solution(mesh):
    return jax.shard_map(
        per_device,
        mesh=mesh,
        in_specs=(
            P("ctx"),
            P(None, "chan"),
            P(),
            P("ctx", None, "chan"),
            P(None, None, "chan"),
            P(None, "chan"),
            P(None, "chan"),
            P("chan"),
        ),
        out_specs=P("ctx", "chan"),
        check_vma=False,
    )
```
